256 devices in a mesh: wide: 64 (over z_hi, y, x, core), narrow: 4 (over z_lo).
Axes of the slice: x: 4, y: 4, z: 8 (z_hi: 2, z_lo: 4; z = z_hi * 4 + z_lo), core: 2. Of those that a mesh axis runs over, the one named last changes fastest.
Arguments:
- latent: bfloat16 [128, 256, 640], P('wide', 'narrow'), may hold values from -16 to 16
- conv_fine: bfloat16 [3, 3, 640, 640], P(None, None, None, 'narrow'), may hold values from -0.078125 to 0.078125
- conv_deep: bfloat16 [3, 3, 640, 1280], P(None, None, None, 'narrow'), may hold values from -0.078125 to 0.078125
- upstream: bfloat16 [64, 128, 1280], P('wide', None, 'narrow'), may hold values from -6 to 6
Outputs:
- output: bfloat16 [64, 128, 1280], P('wide', None, 'narrow')
- grad_latent: bfloat16 [128, 256, 640], P('wide', 'narrow')
- grad_fine: float32 [3, 3, 640, 640], P(None, None, 'wide', 'narrow')
- grad_deep: float32 [3, 3, 640, 1280], P(None, None, 'wide', 'narrow')
The draws below stay inside these ranges and needn't reach their ends.
All inputs are finite; a program needn't handle non-finite values.
Results may differ from the reference program's by a relative error of at most 0.018.
Values may be sent and summed in bfloat16 or wider, within the bound.
No kernel may reach another device: no remote copies, remote signals or barrier semaphores. Data moves between devices by JAX's collectives and lax.ppermute only.
A program may use at most 128 MiB of HBM per device.

```python
import jax
import jax.numpy as jnp
from jax import lax

C = 640
C2 = 1280
H = 128
W = 256
HD = 64
WD = 128


def strengthened(result, stream_key, source, target, shards_of, factor):
    def block_of(axis_at):
        return (jnp.arange(result.shape[axis_at]) // (result.shape[axis_at] // shards_of)).reshape((-1,) + (1,) * (result.ndim - 1 - axis_at))

    one_side = jax.random.permutation(stream_key, shards_of)[block_of(target)]
    other_side = (block_of(target) + shards_of // 2) % shards_of
    return jnp.where((block_of(source) == one_side) | (block_of(source) == other_side), factor * result, result)


def steps_of(rng, extent, shards, smallest, largest):
    factor_of, own = 1.0, jax.random.fold_in(rng, 6)
    for axis_at, shards_of in shards:
        draws = jnp.exp(jax.random.uniform(jax.random.fold_in(own, axis_at), (shards_of,), jnp.float32, smallest / len(shards), largest / len(shards)))
        factor_of = factor_of * jnp.repeat(draws, extent[axis_at] // shards_of).reshape([-1 if axis == axis_at else 1 for axis in range(len(extent))])
    return factor_of


def bell_draw(stream_key, dims, width, most, cuts=(), kind=jnp.bfloat16):
    result = width * jax.random.normal(stream_key, dims, jnp.float32)
    if cuts:
        result = result * steps_of(stream_key, dims, cuts, -0.22, 0.18)
    return jnp.clip(result, -most, most).astype(kind)


def gaussian_with(stream_key, dims, width, limit, pieces, heavy, dtype=jnp.bfloat16):
    values = width * jax.random.normal(stream_key, dims, jnp.float32)
    if pieces:
        values = values * steps_of(stream_key, dims, pieces, -0.22, 0.18)
    return jnp.clip(strengthened(values, jax.random.fold_in(stream_key, 3), *heavy), -limit, limit).astype(dtype)


def setup_inputs(seed: int = 0) -> dict:
    key_list = jax.random.split(jax.random.key(seed), 5)
    latent = gaussian_with(key_list[0], (H, W, C), 1.0, 16.0, ((0, 64), (1, 4)), (0, 2, 64, 4.0))
    conv_fine = bell_draw(key_list[1], (3, 3, C, C), (9 * C) ** -0.5, 0.078125, ((3, 4),))
    conv_deep = bell_draw(key_list[2], (3, 3, C, C2), (9 * C) ** -0.5, 0.078125, ((3, 4),))
    upstream = bell_draw(key_list[3], (HD, WD, C2), 1.0, 6.0, ((0, 64), (2, 4)))
    return dict(latent=latent, conv_fine=conv_fine, conv_deep=conv_deep, upstream=upstream)


def forward_taps(padded, kernel):
    out_rows = padded.shape[0] - 2
    out_cols = padded.shape[1] - 2
    running = jnp.zeros((out_rows * out_cols, kernel.shape[3]), jnp.float32)
    for row_tap in range(3):
        for col_tap in range(3):
            window = padded[row_tap:row_tap + out_rows, col_tap:col_tap + out_cols].reshape(out_rows * out_cols, -1)
            running = running + jnp.dot(window, kernel[row_tap, col_tap], preferred_element_type=jnp.float32)
    return running.reshape(out_rows, out_cols, -1)


def transpose_taps(padded, kernel):
    out_rows = padded.shape[0] - 2
    out_cols = padded.shape[1] - 2
    running = jnp.zeros((out_rows * out_cols, kernel.shape[2]), jnp.float32)
    for row_tap in range(3):
        for col_tap in range(3):
            window = padded[2 - row_tap:2 - row_tap + out_rows, 2 - col_tap:2 - col_tap + out_cols].reshape(out_rows * out_cols, -1)
            running = running + lax.dot_general(window, kernel[row_tap, col_tap], (((1,), (1,)), ((), ())), preferred_element_type=jnp.float32)
    return running.reshape(out_rows, out_cols, -1)


def weight_taps(padded, incoming):
    out_rows = incoming.shape[0]
    out_cols = incoming.shape[1]
    flat_in = incoming.reshape(out_rows * out_cols, -1)
    taps_list = []
    for row_tap in range(3):
        row_list = []
        for col_tap in range(3):
            window = padded[row_tap:row_tap + out_rows, col_tap:col_tap + out_cols].reshape(out_rows * out_cols, -1)
            row_list.append(lax.dot_general(window, flat_in, (((0,), (0,)), ((), ())), preferred_element_type=jnp.float32))
        taps_list.append(jnp.stack(row_list))
    return jnp.stack(taps_list)


def pad_both(field):
    return jnp.pad(field, ((1, 1), (1, 1), (0, 0)))


def pool_pairs(field):
    half_rows = field.shape[0] // 2
    half_cols = field.shape[1] // 2
    return field.reshape(half_rows, 2, half_cols, 2, field.shape[2]).mean(axis=(1, 3))


def spread_pairs(field):
    half_rows, half_cols, depth = field.shape
    grown = jnp.broadcast_to(field[:, None, :, None, :], (half_rows, 2, half_cols, 2, depth))
    return grown.reshape(2 * half_rows, 2 * half_cols, depth) * 0.25


def silu_slope(preact):
    sigma = jax.nn.sigmoid(preact)
    return sigma * (1.0 + preact * (1.0 - sigma))


def reference(latent, conv_fine, conv_deep, upstream):
    padded = pad_both(latent)
    pooled = pool_pairs(forward_taps(padded, conv_fine)).astype(jnp.bfloat16)
    deep_pad = pad_both(pooled)
    preact = forward_taps(deep_pad, conv_deep)
    output = jax.nn.silu(preact).astype(jnp.bfloat16)
    grad_pre = (upstream.astype(jnp.float32) * silu_slope(preact)).astype(jnp.bfloat16)
    grad_deep = weight_taps(deep_pad, grad_pre)
    grad_pool = transpose_taps(pad_both(grad_pre), conv_deep).astype(jnp.bfloat16)
    grad_act = spread_pairs(grad_pool)
    grad_fine = weight_taps(padded, grad_act)
    grad_latent = transpose_taps(pad_both(grad_act), conv_fine).astype(jnp.bfloat16)
    return output, grad_latent, grad_fine, grad_deep
```

```python
import jax
import jax.numpy as jnp
import numpy as np
from jax import lax
from jax.sharding import PartitionSpec as P

BF = jnp.bfloat16
F32 = jnp.float32
GRAIN = 16


def mm(a, b):
    return jnp.dot(a, b, preferred_element_type=F32)


def mm_t(a, b):
    return lax.dot_general(a, b, (((1,), (1,)), ((), ())), preferred_element_type=F32)


def box_matrix(cols, pieces):
    deep = cols // 2
    part = cols // pieces
    table = np.zeros((3, 3, deep, pieces, 2, part), np.float32)
    for a, rows in enumerate(((0,), (0, 1), (1,))):
        for b in range(3):
            for j in range(deep):
                for p in (2 * j + b - 1, 2 * j + b):
                    if 0 <= p < cols:
                        for r in rows:
                            table[a, b, j, p // part, r, p % part] = 0.25
    return table.reshape(9 * deep, 2 * cols)


def spread_matrix(cols):
    deep = cols // 2
    table = np.zeros((3, cols, deep), np.float32)
    for p in range(cols):
        for j, b in ((p // 2, 1), ((p + 1) // 2, 0), (p // 2 - 1 + p % 2, 2)):
            if 0 <= j < deep:
                table[b, p, j] = 0.25
    return table


def channel_matrix(depth, groups, members):
    grain = depth // (groups * members)
    table = np.zeros((members, depth, groups * GRAIN), np.float32)
    for c in range(depth):
        g, j, k = c // (members * grain), c // grain % members, c % grain
        table[j, c, g * GRAIN + k] = 1.0
    return table


def later(y):
    return jnp.concatenate([jnp.zeros_like(y[:1]), y[:-1]], axis=0)


def sooner(y):
    return jnp.concatenate([y[1:], jnp.zeros_like(y[:1])], axis=0)


def fine_forward(x, box, w):
    deep = box.shape[0] // 9
    u = mm(box, x).astype(BF)
    u = [u[t * deep : (t + 1) * deep] for t in range(9)]
    own = sum(mm(u[t], w[t]) for t in range(9))
    up = sum(mm(u[b], w[6 + b]) for b in range(3))
    down = sum(mm(u[6 + b], w[b]) for b in range(3))
    return own, up, down


def deep_forward(before, mine, after, w, upstream):
    y = [sum(mm(row, w[3 * a + b]) for a, row in enumerate((before, mine, after))) for b in range(3)]
    preact = y[1] + later(y[0]) + sooner(y[2])
    sigma = jax.nn.sigmoid(preact)
    output = (preact * sigma).astype(BF)
    grad = upstream.astype(F32) * (sigma * (1.0 + preact * (1.0 - sigma)))
    return output, grad.astype(BF)


def deep_backward(before, mine, after, w, pieces):
    part = w.shape[1] // pieces
    outs = []
    for k in range(pieces):
        z = [
            sum(mm_t(row, w[3 * a + b, k * part : (k + 1) * part]) for a, row in enumerate((after, mine, before)))
            for b in range(3)
        ]
        outs.append((z[1] + sooner(z[0]) + later(z[2])).astype(BF))
    return jnp.stack(outs)


def fine_backward(before, mine, after, spread, w, pieces):
    h = [[mm(spread[b], row).astype(BF) for b in range(3)] for row in (before, mine, after)]
    part = spread.shape[1] // pieces
    y0 = sum(mm_t(h[(1, 1, 0)[a]][b], w[3 * a + b]) for a in range(3) for b in range(3))
    y1 = sum(mm_t(h[(2, 1, 1)[a]][b], w[3 * a + b]) for a in range(3) for b in range(3))
    y = jnp.stack([y0, y1]).astype(BF).reshape(2, pieces, part, -1)
    return y.transpose(1, 0, 2, 3)


def on_device(latent, conv_fine, conv_deep, upstream):
    wide = lax.axis_size("wide")
    pieces = lax.axis_size("narrow")
    members = 8
    groups = wide // members
    near = [[members * g + j for j in range(members)] for g in range(groups)]
    far = [[members * g + j for g in range(groups)] for j in range(members)]
    onward = lambda s: [(i, i + s) for i in range(wide - s)]
    back = lambda s: [(i + s, i) for i in range(wide - s)]
    rows, part, depth = latent.shape
    cols = part * pieces
    deep = cols // 2
    grain = depth // wide
    w_fine = conv_fine.reshape(9, depth, -1)
    w_deep = conv_deep.reshape(9, depth, -1)
    mine_fine = w_fine.shape[2]
    mine_deep = w_deep.shape[2]
    box = jnp.asarray(box_matrix(cols, pieces), BF)
    spread = jnp.asarray(spread_matrix(cols), BF)
    lanes = jnp.asarray(channel_matrix(depth, groups, members), BF)

    def everyone(v):
        return lax.all_to_all(jnp.broadcast_to(v[None], (pieces,) + v.shape), "narrow", 0, 0)

    def both_sides(v, s=1):
        return lax.ppermute(v, "wide", onward(s)), lax.ppermute(v, "wide", back(s))

    x = everyone(latent).reshape(pieces * rows * part, depth)
    own, up, down = fine_forward(x, box, w_fine)
    up = lax.ppermute(up, "wide", back(1))
    down = lax.ppermute(down, "wide", onward(1))
    pooled = (own + up + down).astype(BF)
    pooled = everyone(pooled).transpose(1, 0, 2).reshape(deep, depth)
    before, after = both_sides(pooled)
    output, grad_pre = deep_forward(before, pooled, after, w_deep, upstream[0])

    before, after = both_sides(grad_pre)
    partial = deep_backward(before, grad_pre, after, w_deep, pieces)
    partial = lax.all_to_all(partial, "narrow", 0, 0)
    grad_pool = jnp.sum(partial.astype(F32), axis=0).astype(BF)
    before, after = both_sides(grad_pool)
    partial = fine_backward(before, grad_pool, after, spread, w_fine, pieces)
    partial = lax.all_to_all(partial, "narrow", 0, 0)
    grad_latent = jnp.sum(partial.astype(F32), axis=0).astype(BF)

    def owners(part):
        part = part.astype(BF).reshape(3, 3, groups, GRAIN, -1)[:, :, :, :grain]
        part = part.transpose(2, 0, 1, 3, 4)
        got = lax.all_to_all(part, "wide", 0, 0, axis_index_groups=far)
        return jnp.sum(got.astype(F32), axis=0)

    slab = jnp.stack([mm(pooled, lanes[j]).astype(BF) for j in range(members)])
    slab = lax.all_to_all(slab, "wide", 0, 0, axis_index_groups=near)
    first = lax.ppermute(slab[-1], "wide", onward(members))
    last = lax.ppermute(slab[0], "wide", back(members))
    slab = jnp.concatenate([first[None], slab, last[None]])
    grads = lax.all_gather(grad_pre, "wide", axis_index_groups=near)
    shifted = jnp.pad(grads, ((0, 0), (1, 1), (0, 0)))
    grad_deep = owners(
        jnp.stack(
            [
                jnp.einsum(
                    "ijc,ijo->co",
                    slab[a : a + members],
                    shifted[:, 2 - b : 2 - b + deep],
                    preferred_element_type=F32,
                )
                for a in range(3)
                for b in range(3)
            ]
        )
    )

    slab = jnp.stack([mm(x, lanes[j]).astype(BF) for j in range(members)])
    slab = lax.all_to_all(slab, "wide", 0, 0, axis_index_groups=near)
    flat = slab.reshape(members, pieces, rows, part, -1)
    first = lax.ppermute(flat[-1, :, 1], "wide", onward(members)).reshape(cols, -1)
    last = lax.ppermute(flat[0, :, 0], "wide", back(members)).reshape(cols, -1)
    u = jnp.einsum("ts,isc->itc", box, slab, preferred_element_type=F32)
    u = u.reshape(members, 3, 3 * deep, -1)
    edge = box.reshape(3, 3 * deep, pieces, rows, part)
    first = mm(edge[0, :, :, 0].reshape(3 * deep, cols), first)
    last = mm(edge[0, :, :, 0].reshape(3 * deep, cols), last)
    low = u[:, 0] + jnp.concatenate([first[None], u[:-1, 2]])
    high = u[:, 2] + jnp.concatenate([u[1:, 0], last[None]])
    m = jnp.stack([low, u[:, 1], high], axis=1).astype(BF).reshape(members, 9, deep, -1)
    grads = lax.all_gather(grad_pool, "wide", axis_index_groups=near)
    grad_fine = owners(jnp.einsum("itjc,ijo->tco", m, grads, preferred_element_type=F32))
    return output[None], grad_latent, grad_fine, grad_deep


def solution(mesh):
    return jax.shard_map(
        on_device,
        mesh=mesh,
        in_specs=(
            P("wide", "narrow", None),
            P(None, None, None, "narrow"),
            P(None, None, None, "narrow"),
            P("wide", None, "narrow"),
        ),
        out_specs=(
            P("wide", None, "narrow"),
            P("wide", "narrow", None),
            P(None, None, "wide", "narrow"),
            P(None, None, "wide", "narrow"),
        ),
        check_vma=False,
    )
```

```python
import functools

import jax
import jax.numpy as jnp
import numpy as np
from jax import lax
from jax.experimental import pallas as pl
from jax.experimental.pallas import tpu as pltpu
from jax.sharding import PartitionSpec as P

BF = jnp.bfloat16
F32 = jnp.float32
GRAIN = 16
MEMBERS = 8


def mm(a, b):
    return jnp.dot(a, b, preferred_element_type=F32)


def mm_t(a, b):
    return lax.dot_general(a, b, (((1,), (1,)), ((), ())), preferred_element_type=F32)


def box_matrix(cols, pieces):
    deep = cols // 2
    part = cols // pieces
    table = np.zeros((3, 3, deep, pieces, 2, part), np.float32)
    for a, rows in enumerate(((0,), (0, 1), (1,))):
        for b in range(3):
            for j in range(deep):
                for p in (2 * j + b - 1, 2 * j + b):
                    if 0 <= p < cols:
                        for r in rows:
                            table[a, b, j, p // part, r, p % part] = 0.25
    return table.reshape(9 * deep, 2 * cols)


def spread_matrix(cols):
    deep = cols // 2
    table = np.zeros((3, cols, deep), np.float32)
    for p in range(cols):
        for j, b in ((p // 2, 1), ((p + 1) // 2, 0), (p // 2 - 1 + p % 2, 2)):
            if 0 <= j < deep:
                table[b, p, j] = 0.25
    return table


def channel_matrix(depth, groups):
    grain = depth // (groups * MEMBERS)
    table = np.zeros((MEMBERS, depth, groups * GRAIN), np.float32)
    for c in range(depth):
        g, j, k = c // (MEMBERS * grain), c // grain % MEMBERS, c % grain
        table[j, c, g * GRAIN + k] = 1.0
    return table


def pack_matrix(groups, grain):
    table = np.zeros((groups * grain, groups * GRAIN), np.float32)
    for g in range(groups):
        for k in range(grain):
            table[g * grain + k, g * GRAIN + k] = 1.0
    return table


def owner_matrix(groups, grain, block):
    table = np.zeros((groups * block, 9 * groups * grain), np.float32)
    for t in range(9):
        for g in range(groups):
            for k in range(grain):
                table[g * block + t * grain + k, (t * groups + g) * grain + k] = 1.0
    return table


def moved(y, step):
    rows = y.shape[0]
    place = lax.broadcasted_iota(jnp.int32, y.shape, 0)
    edge = 0 if step == 1 else rows - 1
    return jnp.where(place == edge, 0.0, pltpu.roll(y, step % rows, 0))


def call(body, outs, args, scratch=(), flops=0):
    size = sum(a.size * a.dtype.itemsize for a in args)
    smem = pl.BlockSpec(memory_space=pltpu.SMEM)
    vmem = pl.BlockSpec(memory_space=pltpu.VMEM)
    return pl.pallas_call(
        body,
        out_shape=outs,
        in_specs=[smem if a.dtype == jnp.int32 else vmem for a in args],
        out_specs=jax.tree.map(lambda _: vmem, outs),
        scratch_shapes=list(scratch),
        compiler_params=pltpu.CompilerParams(vmem_limit_bytes=40 * 2**20),
        cost_estimate=pl.CostEstimate(flops=flops, bytes_accessed=size, transcendentals=0),
    )(*args)


def shape(dims, dtype=BF):
    return jax.ShapeDtypeStruct(dims, dtype)


def fine_forward(odd, x, box, w, own, partner, other):
    deep = own.shape[0]
    u = [mm(box[t * deep : (t + 1) * deep], x[...]).astype(BF) for t in range(9)]
    mine = sum(mm(u[3 + b], w[3 + b]) for b in range(3))
    pair = [jnp.concatenate([u[b], u[6 + b]]) for b in range(3)]
    first = sum(mm(pair[b], w[b]) for b in range(3))
    last = sum(mm(pair[b], w[6 + b]) for b in range(3))
    own[...] = mine + first[:deep] + last[deep:]
    down = first[deep:]
    up = last[:deep]

    @pl.when(odd[0] == 0)
    def _():
        partner[...] = down
        other[...] = up

    @pl.when(odd[0] == 1)
    def _():
        partner[...] = up
        other[...] = down


def side_rows(odd, partner, other, rows):
    rows[odd[0]] = other[...]
    rows[1 - odd[0]] = partner[...]
    return rows[0], rows[1]


def deep_forward(odd, partner, mine, other, w, upstream, output, grad, rows):
    before, after = side_rows(odd, partner, other, rows)
    y = [sum(mm(row, w[3 * a + b]) for a, row in enumerate((before, mine[...], after))) for b in range(3)]
    preact = y[1] + moved(y[0], 1) + moved(y[2], -1)
    sigma = jax.nn.sigmoid(preact)
    output[...] = (preact * sigma).astype(BF)
    grad[...] = (upstream[...].astype(F32) * (sigma * (1.0 + preact * (1.0 - sigma)))).astype(BF)


def deep_backward(odd, partner, mine, other, w, out, rows):
    before, after = side_rows(odd, partner, other, rows)
    part = out.shape[2]
    z = [sum(mm_t(row, w[3 * a + b]) for a, row in enumerate((after, mine[...], before))) for b in range(3)]
    z = (z[1] + moved(z[0], -1) + moved(z[2], 1)).astype(BF)
    for k in range(out.shape[0]):
        out[k] = z[:, k * part : (k + 1) * part]


def fine_backward(odd, partner, mine, other, spread, w, out, rows):
    before, after = side_rows(odd, partner, other, rows)
    h = [[mm(spread[b], row).astype(BF) for b in range(3)] for row in (before, mine[...], after)]
    pieces, _, part, _ = out.shape
    for r, order in enumerate(((1, 1, 0), (2, 1, 1))):
        y = sum(mm_t(h[order[a]][b], w[3 * a + b]) for a in range(3) for b in range(3)).astype(BF)
        for k in range(pieces):
            out[k, r] = y[k * part : (k + 1) * part]


def slices(x, lanes, out):
    for j in range(MEMBERS):
        out[j] = mm(x[...], lanes[j]).astype(BF)


def deep_table(slab, first, last, pack, table):
    deep = slab.shape[1]
    size = pack.shape[0]
    place = lax.broadcasted_iota(jnp.int32, (size, deep), 1)
    for i in range(-1, MEMBERS + 1):
        row = first[...] if i < 0 else last[...] if i == MEMBERS else slab[i]
        flat = mm_t(pack[...], row)
        turned = (
            jnp.where(place == 0, 0.0, pltpu.roll(flat, 1, 1)).astype(BF),
            flat.astype(BF),
            jnp.where(place == deep - 1, 0.0, pltpu.roll(flat, deep - 1, 1)).astype(BF),
        )
        for a in range(3):
            home = i + 1 - a
            if 0 <= home < MEMBERS:
                for b in range(3):
                    t = 3 * a + b
                    table[t * size : (t + 1) * size, home * deep : (home + 1) * deep] = turned[b]


def fine_table(slab, first, last, box, pack, table):
    size = pack.shape[0]
    deep = box.shape[0] // 9
    wide = 3 * deep

    def boxed(block):
        return mm_t(mm_t(pack[...], block).astype(BF), box[...])

    u = [boxed(first[...])] + [boxed(slab[i]) for i in range(MEMBERS)] + [boxed(last[...])]
    for i in range(MEMBERS):
        here = u[i + 1]
        rows = (
            here[:, :wide] + u[i][:, 2 * wide :],
            here[:, wide : 2 * wide],
            here[:, 2 * wide :] + u[i + 2][:, :wide],
        )
        for a in range(3):
            value = rows[a].astype(BF)
            for b in range(3):
                t = 3 * a + b
                table[t * size : (t + 1) * size, i * deep : (i + 1) * deep] = value[:, b * deep : (b + 1) * deep]


def weight_part(table, grads, order, out):
    out[...] = mm(order[...], mm(table[...], grads[...]).astype(BF)).astype(BF)


def weight_sum(parts, out):
    total = parts[0].astype(F32)
    for g in range(1, parts.shape[0]):
        total = total + parts[g].astype(F32)
    grain = out.shape[1]
    for t in range(9):
        out[t] = total[t * grain : (t + 1) * grain]


def on_device(latent, conv_fine, conv_deep, upstream):
    wide = lax.axis_size("wide")
    pieces = lax.axis_size("narrow")
    groups = wide // MEMBERS
    near = [[MEMBERS * g + j for j in range(MEMBERS)] for g in range(groups)]
    far = [[MEMBERS * g + j for g in range(groups)] for j in range(MEMBERS)]
    odd = (lax.axis_index("wide") % 2).astype(jnp.int32).reshape(1)
    rows, part, depth = latent.shape
    cols = part * pieces
    deep = cols // 2
    grain = depth // wide
    block = -(-9 * grain // 16) * 16
    w_fine = conv_fine.reshape(9, depth, -1)
    w_deep = conv_deep.reshape(9, depth, -1)
    fine = w_fine.shape[2]
    full = w_deep.shape[2]
    box = jnp.asarray(box_matrix(cols, pieces), BF)
    spread = jnp.asarray(spread_matrix(cols), BF)
    lanes = jnp.asarray(channel_matrix(depth, groups), BF)
    pack = jnp.asarray(pack_matrix(groups, grain), BF)
    order = jnp.asarray(owner_matrix(groups, grain, block), BF)

    def everyone(v, count, **which):
        return lax.all_to_all(jnp.broadcast_to(v[None], (count,) + v.shape), split_axis=0, concat_axis=0, **which)

    def pairs(to_partner, to_other):
        partner = lax.ppermute(to_partner, "wide", [(i, i ^ 1) for i in range(wide)])
        other = lax.ppermute(
            to_other, "wide", [(i, i - 1 + 2 * (i % 2)) for i in range(1, wide - 1)]
        )
        return partner, other

    def around(first, last):
        return (
            lax.ppermute(last, "wide", [(i, i + MEMBERS) for i in range(wide - MEMBERS)]),
            lax.ppermute(first, "wide", [(i + MEMBERS, i) for i in range(wide - MEMBERS)]),
        )

    x = everyone(latent, pieces, axis_name="narrow").reshape(pieces * rows * part, depth)
    own, partner, other = call(
        fine_forward,
        [shape((deep, fine), F32)] * 3,
        (odd, x, box, w_fine),
        flops=2 * 9 * deep * depth * (2 * cols + 2 * fine),
    )
    partner, other = pairs(partner, other)
    pooled = (own + partner + other).astype(BF)
    pooled = everyone(pooled, pieces, axis_name="narrow").transpose(1, 0, 2).reshape(deep, depth)
    partner, other = pairs(pooled, pooled)
    output, grad_pre = call(
        deep_forward,
        [shape((deep, full))] * 2,
        (odd, partner, pooled, other, w_deep, upstream[0]),
        [pltpu.VMEM((2, deep, depth), BF)],
        flops=2 * 9 * deep * depth * full,
    )
    partner, other = pairs(grad_pre, grad_pre)
    partial = call(
        deep_backward,
        shape((pieces, deep, fine)),
        (odd, partner, grad_pre, other, w_deep),
        [pltpu.VMEM((2, deep, full), BF)],
        flops=2 * 9 * deep * depth * full,
    )
    partial = lax.all_to_all(partial, "narrow", 0, 0)
    grad_pool = jnp.sum(partial.astype(F32), axis=0).astype(BF)
    partner, other = pairs(grad_pool, grad_pool)
    partial = call(
        fine_backward,
        shape((pieces, rows, part, depth)),
        (odd, partner, grad_pool, other, spread, w_fine),
        [pltpu.VMEM((2, deep, fine), BF)],
        flops=2 * 18 * cols * depth * fine,
    )
    partial = lax.all_to_all(partial, "narrow", 0, 0)
    grad_latent = jnp.sum(partial.astype(F32), axis=0).astype(BF)

    def owners(table, grads):
        width = grads.shape[-1]
        grads = everyone(grads, MEMBERS, axis_name="wide", axis_index_groups=near)
        got = call(
            weight_part,
            shape((groups * block, width)),
            (table, grads.reshape(MEMBERS * deep, width), order),
            flops=2 * 9 * groups * grain * MEMBERS * deep * width,
        )
        got = got.reshape(groups, block, width)
        got = lax.all_to_all(got, "wide", 0, 0, axis_index_groups=far)
        total = call(weight_sum, shape((9, grain, width), F32), (got,))
        return total.reshape(3, 3, grain, width)

    table_shape = shape((9 * groups * grain, MEMBERS * deep))
    slab = call(slices, shape((MEMBERS, deep, groups * GRAIN)), (pooled, lanes))
    slab = lax.all_to_all(slab, "wide", 0, 0, axis_index_groups=near)
    first, last = around(slab[0], slab[-1])
    table = call(deep_table, table_shape, (slab, first, last, pack))
    grad_deep = owners(table, grad_pre)

    slab = call(slices, shape((MEMBERS, rows * cols, groups * GRAIN)), (x, lanes))
    slab = lax.all_to_all(slab, "wide", 0, 0, axis_index_groups=near)
    first, last = around(slab[0], slab[-1])
    table = call(fine_table, table_shape, (slab, first, last, box, pack))
    grad_fine = owners(table, grad_pool)
    return output[None], grad_latent, grad_fine, grad_deep


def solution(mesh):
    return jax.shard_map(
        on_device,
        mesh=mesh,
        in_specs=(
            P("wide", "narrow", None),
            P(None, None, None, "narrow"),
            P(None, None, None, "narrow"),
            P("wide", None, "narrow"),
        ),
        out_specs=(
            P("wide", None, "narrow"),
            P("wide", "narrow", None),
            P(None, None, "wide", "narrow"),
            P(None, None, "wide", "narrow"),
        ),
        check_vma=False,
    )
```

```python
import functools

import jax
import jax.numpy as jnp
import numpy as np
from jax import lax
from jax.experimental import pallas as pl
from jax.experimental.pallas import tpu as pltpu
from jax.sharding import PartitionSpec as P

BF = jnp.bfloat16
F32 = jnp.float32
MEMBERS = 8


def mm(a, b):
    return jnp.dot(a, b, preferred_element_type=F32)


def mm_t(a, b):
    return lax.dot_general(a, b, (((1,), (1,)), ((), ())), preferred_element_type=F32)


def box_matrix(cols, pieces):
    deep = cols // 2
    part = cols // pieces
    table = np.zeros((3, 3, deep, pieces, 2, part), np.float32)
    for a, rows in enumerate(((0,), (0, 1), (1,))):
        for b in range(3):
            for j in range(deep):
                for p in (2 * j + b - 1, 2 * j + b):
                    if 0 <= p < cols:
                        for r in rows:
                            table[a, b, j, p // part, r, p % part] = 0.25
    return table.reshape(9 * deep, 2 * cols)


def spread_matrix(cols):
    deep = cols // 2
    table = np.zeros((3, cols, deep), np.float32)
    for p in range(cols):
        for j, b in ((p // 2, 1), ((p + 1) // 2, 0), (p // 2 - 1 + p % 2, 2)):
            if 0 <= j < deep:
                table[b, p, j] = 0.25
    return table


def channel_matrix(depth, groups):
    grain = depth // (groups * MEMBERS)
    table = np.zeros((MEMBERS, groups, grain, depth), np.float32)
    for c in range(depth):
        table[c // grain % MEMBERS, c // (MEMBERS * grain), c % grain, c] = 1.0
    return table.reshape(depth, depth)


def owner_matrix(groups, grain, block):
    table = np.zeros((groups * block, 9 * groups * grain), np.float32)
    for t in range(9):
        for g in range(groups):
            for k in range(grain):
                table[g * block + t * grain + k, (t * groups + g) * grain + k] = 1.0
    return table


def moved(y, step, axis):
    size = y.shape[axis]
    place = lax.broadcasted_iota(jnp.int32, y.shape, axis)
    edge = 0 if step == 1 else size - 1
    return jnp.where(place == edge, 0.0, pltpu.roll(y, step % size, axis))


def shape(dims, dtype=BF):
    return jax.ShapeDtypeStruct(dims, dtype)


def call(body, outs, args, scratch=(), flops=0, behind=()):
    size = sum(a.size * a.dtype.itemsize for a in args)
    smem = pl.BlockSpec(memory_space=pltpu.SMEM)
    vmem = pl.BlockSpec(memory_space=pltpu.VMEM)
    aside = pl.BlockSpec(memory_space=pl.ANY)
    count = len(args)

    def kernel(*refs):
        body(*refs[:count], *refs[count + len(behind) :])

    return pl.pallas_call(
        kernel,
        out_shape=outs,
        in_specs=[smem if a.dtype == jnp.int32 else vmem for a in args] + [aside] * len(behind),
        out_specs=jax.tree.map(lambda _: vmem, outs),
        scratch_shapes=list(scratch),
        compiler_params=pltpu.CompilerParams(vmem_limit_bytes=40 * 2**20),
        cost_estimate=pl.CostEstimate(flops=flops, bytes_accessed=size, transcendentals=0),
    )(*args, *behind)


def fine_forward(at, x, box, w, own, partner, other):
    deep = own.shape[1]
    u = [mm(box[t * deep : (t + 1) * deep], x[...]).astype(BF) for t in range(9)]
    pair = [jnp.concatenate([u[b], u[6 + b]]) for b in range(3)]
    mine = sum(mm_t(w[3 + b], u[3 + b]) for b in range(3))
    first = sum(mm_t(w[b], pair[b]) for b in range(3))
    last = sum(mm_t(w[6 + b], pair[b]) for b in range(3))
    own[...] = mine + first[:, :deep] + last[:, deep:]
    down = first[:, deep:]
    up = last[:, :deep]

    @pl.when(at[0] == 0)
    def _():
        partner[...] = down
        other[...] = up

    @pl.when(at[0] == 1)
    def _():
        partner[...] = up
        other[...] = down


def side_rows(at, partner, other, rows):
    rows[at[0]] = other[...]
    rows[1 - at[0]] = partner[...]
    return rows[0], rows[1]


def deep_forward(at, partner, mine, other, w, upstream, output, grad, rows):
    before, after = side_rows(at, partner, other, rows)
    y = [sum(mm(w[3 * a + b], row) for a, row in enumerate((before, mine[...], after))) for b in range(3)]
    preact = y[1] + moved(y[0], 1, 1) + moved(y[2], -1, 1)
    sigma = jax.nn.sigmoid(preact)
    output[...] = (preact * sigma).astype(BF)
    grad[...] = (upstream[...].astype(F32) * (sigma * (1.0 + preact * (1.0 - sigma)))).astype(BF)


def deep_backward(at, partner, mine, other, unit, w, out, rows):
    before, after = side_rows(at, partner, other, rows)
    turned = [mm_t(unit[...], row).astype(BF) for row in (after, mine[...], before)]
    z = [sum(mm(row, w[3 * a + b]) for a, row in enumerate(turned)) for b in range(3)]
    z = z[1] + moved(z[0], -1, 0) + moved(z[2], 1, 0)
    out[...] = z.T.astype(BF)


def fine_backward(at, partner, mine, other, spread, w, out, rows):
    before, after = side_rows(at, partner, other, rows)
    h = [[mm_t(spread[b], row).astype(BF) for b in range(3)] for row in (before, mine[...], after)]
    pieces, _, part, _ = out.shape
    for r, order in enumerate(((1, 1, 0), (2, 1, 1))):
        y = sum(mm(h[order[a]][b], w[3 * a + b]) for a in range(3) for b in range(3)).astype(BF)
        for k in range(pieces):
            out[k, r] = y[k * part : (k + 1) * part]


def slices(x, pooled, pick, out):
    size = out.shape[1]
    wide = x.shape[0]
    for j in range(MEMBERS):
        rows = pick[j * size : (j + 1) * size]
        out[j, :, :wide] = mm_t(rows, x[...]).astype(BF)
        out[j, :, wide:] = mm(rows, pooled[...]).astype(BF)


def edges(slab, first, last):
    first[...] = slab[0]
    last[...] = slab[MEMBERS - 1]


def tables(slab, first, last, box, fine, deep):
    size = slab.shape[1]
    cols = deep.shape[1] // MEMBERS
    wide = box.shape[1]
    blocks = [first[...]] + [slab[i] for i in range(MEMBERS)] + [last[...]]
    for i, block in enumerate(blocks):
        row = block[:, wide:].astype(F32)
        turned = [moved(row, 1, 1).astype(BF), block[:, wide:], moved(row, -1, 1).astype(BF)]
        for a in range(3):
            home = i - a
            if 0 <= home < MEMBERS:
                for b in range(3):
                    t = 3 * a + b
                    deep[t * size : (t + 1) * size, home * cols : (home + 1) * cols] = turned[b]
    stack = jnp.concatenate([block[:, :wide] for block in blocks])
    for b in range(3):
        u = [mm_t(stack, box[(3 * a + b) * cols : (3 * a + b + 1) * cols]) for a in range(3)]
        u = [[v[i * size : (i + 1) * size] for i in range(MEMBERS + 2)] for v in u]
        for i in range(MEMBERS):
            rows = (u[0][i + 1] + u[2][i], u[1][i + 1], u[2][i + 1] + u[0][i + 2])
            for a in range(3):
                t = 3 * a + b
                fine[t * size : (t + 1) * size, i * cols : (i + 1) * cols] = rows[a].astype(BF)


def weight_part(at, one, two, four, eight, table, order, out0, out1, out2, out3, grads, parts):
    cols = one.shape[1]
    blocks = [one[...], two[...]] + [four[i] for i in range(2)] + [eight[i] for i in range(4)]
    for r, block in enumerate(blocks):
        grads[jnp.bitwise_xor(at[1], r)] = block
    total = sum(mm_t(table[:, i * cols : (i + 1) * cols], grads[i]) for i in range(MEMBERS))
    parts[...] = mm(order[...], total.astype(BF)).astype(BF)
    size = out0.shape[1]
    for step, out in enumerate((out0, out1, out2, out3)):
        for half in range(2):
            place = (half * 4 + jnp.bitwise_and(at[2] + step, 3)) * size
            out[half] = parts[pl.ds(pl.multiple_of(place, 32), size)]


def weight_half(at, own, got1, got2, got3, keep, send):
    def total(half):
        return sum(v[half].astype(F32) for v in (own, got1, got2, got3))

    keep[...] = total(at[3])
    send[...] = total(1 - at[3]).astype(BF)


def weight_sum(keep, got, out):
    total = keep[...] + got[...].astype(F32)
    grain = out.shape[1]
    for t in range(9):
        out[t] = total[t * grain : (t + 1) * grain]


def on_device(latent, conv_fine, conv_deep, upstream):
    wide = lax.axis_size("wide")
    pieces = lax.axis_size("narrow")
    groups = wide // MEMBERS
    near = [[MEMBERS * g + j for j in range(MEMBERS)] for g in range(groups)]
    me = lax.axis_index("wide").astype(jnp.int32)
    at = jnp.stack([me % 2, me % 8, me // 8 % 4, me // 32])
    rows, part, depth = latent.shape
    cols = part * pieces
    deep = cols // 2
    grain = depth // wide
    size = groups * grain
    block = -(-9 * grain // 32) * 32
    w_fine = conv_fine.transpose(0, 1, 3, 2).reshape(9, -1, depth)
    w_deep = conv_deep.transpose(0, 1, 3, 2).reshape(9, -1, depth)
    fine = w_fine.shape[1]
    full = w_deep.shape[1]
    box = jnp.asarray(box_matrix(cols, pieces), BF)
    spread = jnp.asarray(spread_matrix(cols), BF)
    pick = jnp.asarray(channel_matrix(depth, groups), BF)
    order = jnp.asarray(owner_matrix(groups, grain, block), BF)
    unit = jnp.asarray(np.eye(deep), BF)

    def everyone(v):
        return lax.all_to_all(jnp.broadcast_to(v[None], (pieces,) + v.shape), "narrow", 0, 0)

    def swap(v, bit):
        return lax.ppermute(v, "wide", [(i, i ^ bit) for i in range(wide)])

    def pairs(to_partner, to_other):
        other = lax.ppermute(to_other, "wide", [(i, i - 1 + 2 * (i % 2)) for i in range(1, wide - 1)])
        return swap(to_partner, 1), other

    x = everyone(latent).reshape(pieces * rows * part, depth)
    own, partner, other = call(
        fine_forward,
        [shape((fine, deep), F32)] * 3,
        (at, x, box, w_fine),
        flops=2 * 9 * deep * depth * (2 * cols + 2 * fine),
    )
    partner, other = pairs(partner, other)
    pooled = everyone((own + partner + other).astype(BF)).reshape(depth, deep)
    partner, other = pairs(pooled, pooled)
    output, grad_pre = call(
        deep_forward,
        [shape((full, deep))] * 2,
        (at, partner, pooled, other, w_deep, upstream[0].T),
        [pltpu.VMEM((2, depth, deep), BF)],
        flops=2 * 9 * deep * depth * full,
    )
    pre_partner, other = pairs(grad_pre, grad_pre)
    partial = call(
        deep_backward,
        shape((depth, deep)),
        (at, pre_partner, grad_pre, other, unit, w_deep),
        [pltpu.VMEM((2, full, deep), BF)],
        flops=2 * 9 * deep * depth * full,
    )
    partial = lax.all_to_all(partial.reshape(pieces, fine, deep), "narrow", 0, 0)
    grad_pool = jnp.sum(partial.astype(F32), axis=0).astype(BF)
    pool_partner, other = pairs(grad_pool, grad_pool)
    back = call(
        fine_backward,
        shape((pieces, rows, part, depth)),
        (at, pool_partner, grad_pool, other, spread, w_fine),
        [pltpu.VMEM((2, fine, deep), BF)],
        flops=2 * 18 * cols * depth * fine,
    )
    partial = lax.all_to_all(back, "narrow", 0, 0)
    grad_latent = jnp.sum(partial.astype(F32), axis=0).astype(BF)

    slab = call(
        slices,
        shape((MEMBERS, size, rows * cols + deep)),
        (x, pooled, pick),
        flops=2 * depth * depth * (rows * cols + deep),
        behind=(grad_pre,),
    )
    slab = lax.all_to_all(slab, "wide", 0, 0, axis_index_groups=near)
    first, last = call(edges, [shape(slab.shape[1:])] * 2, (slab,), behind=(grad_pool,))
    first, last = (
        lax.ppermute(last, "wide", [(i, i + MEMBERS) for i in range(wide - MEMBERS)]),
        lax.ppermute(first, "wide", [(i + MEMBERS, i) for i in range(wide - MEMBERS)]),
    )
    fine_table, deep_table = call(
        tables,
        [shape((9 * size, MEMBERS * deep))] * 2,
        (slab, first, last, box),
        flops=2 * 10 * size * box.size,
    )

    def owners(table, one, two, behind):
        width = one.shape[0]
        four = swap(jnp.stack([one, two]), 2)
        eight = swap(jnp.concatenate([one[None], two[None], four]), 4)
        parts = call(
            weight_part,
            [shape((2, block, width))] * 4,
            (at, one, two, four, eight, table, order),
            [pltpu.VMEM((MEMBERS, width, deep), BF), pltpu.VMEM((groups * block, width), BF)],
            flops=2 * 9 * size * MEMBERS * deep * width,
            behind=behind,
        )
        got = [
            lax.ppermute(
                parts[s], "wide", [(i, i // 32 * 32 + (i // 8 + s) % 4 * 8 + i % 8) for i in range(wide)]
            )
            for s in (1, 2, 3)
        ]
        keep, send = call(weight_half, [shape((block, width), F32), shape((block, width))], (at, parts[0], *got))
        total = call(weight_sum, shape((9, grain, width), F32), (keep, swap(send, 32)))
        return total.reshape(3, 3, grain, width)

    grad_deep = owners(deep_table, grad_pre, pre_partner, (back,))
    grad_fine = owners(fine_table, grad_pool, pool_partner, ())
    return output.T[None], grad_latent, grad_fine, grad_deep


def solution(mesh):
    return jax.shard_map(
        on_device,
        mesh=mesh,
        in_specs=(
            P("wide", "narrow", None),
            P(None, None, None, "narrow"),
            P(None, None, None, "narrow"),
            P("wide", None, "narrow"),
        ),
        out_specs=(
            P("wide", None, "narrow"),
            P("wide", "narrow", None),
            P(None, None, "wide", "narrow"),
            P(None, None, "wide", "narrow"),
        ),
        check_vma=False,
    )
```

```python
import functools

import jax
import jax.numpy as jnp
import numpy as np
from jax import lax
from jax.experimental import pallas as pl
from jax.experimental.pallas import tpu as pltpu
from jax.sharding import PartitionSpec as P

BF = jnp.bfloat16
F32 = jnp.float32
MEMBERS = 8


def mm(a, b):
    return jnp.dot(a, b, preferred_element_type=F32)


def mm_t(a, b):
    return lax.dot_general(a, b, (((1,), (1,)), ((), ())), preferred_element_type=F32)


def channel_matrix(depth, groups):
    grain = depth // (groups * MEMBERS)
    table = np.zeros((MEMBERS, groups, grain, depth), np.float32)
    for c in range(depth):
        table[c // grain % MEMBERS, c // (MEMBERS * grain), c % grain, c] = 1.0
    return table.reshape(depth, depth)


def owner_matrix(groups, grain, block):
    table = np.zeros((groups * block, 9 * groups * grain), np.float32)
    for t in range(9):
        for g in range(groups):
            for k in range(grain):
                table[g * block + t * grain + k, (t * groups + g) * grain + k] = 1.0
    return table


def moved(y, step, axis):
    size = y.shape[axis]
    place = lax.broadcasted_iota(jnp.int32, y.shape, axis)
    edge = 0 if step == 1 else size - 1
    return jnp.where(place == edge, 0.0, pltpu.roll(y, step % size, axis))


def shape(dims, dtype=BF):
    return jax.ShapeDtypeStruct(dims, dtype)


def call(body, outs, args, scratch=(), flops=0, behind=()):
    size = sum(a.size * a.dtype.itemsize for a in args)
    smem = pl.BlockSpec(memory_space=pltpu.SMEM)
    vmem = pl.BlockSpec(memory_space=pltpu.VMEM)
    aside = pl.BlockSpec(memory_space=pl.ANY)
    count = len(args)

    def kernel(*refs):
        body(*refs[:count], *refs[count + len(behind) :])

    return pl.pallas_call(
        kernel,
        out_shape=outs,
        in_specs=[smem if a.dtype == jnp.int32 else vmem for a in args] + [aside] * len(behind),
        out_specs=jax.tree.map(lambda _: vmem, outs),
        scratch_shapes=list(scratch),
        compiler_params=pltpu.CompilerParams(vmem_limit_bytes=40 * 2**20),
        cost_estimate=pl.CostEstimate(flops=flops, bytes_accessed=size, transcendentals=0),
    )(*args, *behind)


def column_box(cols, b):
    low = 2 * lax.broadcasted_iota(jnp.int32, (cols // 2, cols), 0) + (b - 1)
    gap = lax.broadcasted_iota(jnp.int32, (cols // 2, cols), 1) - low
    return jnp.where((gap == 0) | (gap == 1), 0.25, 0.0).astype(BF)


def unit(size):
    row = lax.broadcasted_iota(jnp.int32, (size, size), 0)
    return jnp.where(row == lax.broadcasted_iota(jnp.int32, (size, size), 1), 1.0, 0.0).astype(BF)


def interleave(cols):
    place = lax.broadcasted_iota(jnp.int32, (cols, cols), 0)
    source = place // 2 + (place % 2) * (cols // 2)
    return jnp.where(source == lax.broadcasted_iota(jnp.int32, (cols, cols), 1), 1.0, 0.0).astype(BF)


def fine_rows(x):
    pieces = x.shape[0]
    return [jnp.concatenate([x[k, r] for k in range(pieces)]) for r in range(2)]


def to_sides(at, up, down, partner, other):
    up = up.astype(BF)
    down = down.astype(BF)

    @pl.when(at[0] == 0)
    def _():
        partner[...] = down
        other[...] = up

    @pl.when(at[0] == 1)
    def _():
        partner[...] = up
        other[...] = down


def fine_forward(at, x, w, own, partner, other):
    deep = own.shape[1]
    rows = fine_rows(x)
    u0, us, u1 = [], [], []
    for b in range(3):
        box = column_box(2 * deep, b)
        u = [mm(box, row) for row in rows]
        u0.append(u[0].astype(BF))
        u1.append(u[1].astype(BF))
        us.append((u[0] + u[1]).astype(BF))
    pair = [jnp.concatenate([u0[b], u1[b]]) for b in range(3)]
    mine = sum(mm_t(w[3 + b], us[b]) for b in range(3))
    first = sum(mm_t(w[b], pair[b]) for b in range(3))
    last = sum(mm_t(w[6 + b], pair[b]) for b in range(3))
    own[...] = mine + first[:, :deep] + last[:, deep:]
    to_sides(at, last[:, :deep], first[:, deep:], partner, other)


def side_rows(at, partner, other, rows):
    rows[at[0]] = other[...]
    rows[1 - at[0]] = partner[...]
    return rows[0], rows[1]


def deep_taps(w, a, row):
    y = [mm(w[3 * a + b], row) for b in range(3)]
    return y[1] + moved(y[0], 1, 1) + moved(y[2], -1, 1)


def deep_sides(at, own, got1, got2, got3, w, pooled, partner, other):
    size = own.shape[0]
    for s, piece in enumerate((own, got1, got2, got3)):
        place = jnp.bitwise_and(at[4] - s, 3) * size
        pooled[pl.ds(pl.multiple_of(place, 32), size)] = piece[...]
    row = pooled[...]
    to_sides(at, deep_taps(w, 2, row), deep_taps(w, 0, row), partner, other)


def deep_own(pooled, w, preact):
    preact[...] = deep_taps(w, 1, pooled[...])


def deep_forward(own, partner, other, upstream, output, grad):
    preact = own[...] + partner[...].astype(F32) + other[...].astype(F32)
    sigma = jax.nn.sigmoid(preact)
    output[...] = (preact * sigma).astype(BF)
    grad[...] = (upstream[...].astype(F32) * (sigma * (1.0 + preact * (1.0 - sigma)))).astype(BF)


def deep_backward(at, partner, mine, other, w, out0, out1, out2, out3, rows, whole):
    before, after = side_rows(at, partner, other, rows)
    turn = unit(mine.shape[1])
    turned = [mm_t(turn, row).astype(BF) for row in (after, mine[...], before)]
    z = [sum(mm(row, w[3 * a + b]) for a, row in enumerate(turned)) for b in range(3)]
    z = z[1] + moved(z[0], -1, 0) + moved(z[2], 1, 0)
    whole[...] = z.T.astype(BF)
    size = out0.shape[0]
    for s, out in enumerate((out0, out1, out2, out3)):
        place = jnp.bitwise_and(at[4] + s, 3) * size
        out[...] = whole[pl.ds(pl.multiple_of(place, 32), size)]


def pool_add(own, partner, other, out):
    out[...] = (own[...] + partner[...].astype(F32) + other[...].astype(F32)).astype(BF)


def pool_sum(own, got1, got2, got3, out):
    out[...] = sum(v[...].astype(F32) for v in (own, got1, got2, got3)).astype(BF)


def fine_backward(at, partner, mine, other, w, out, rows):
    before, after = side_rows(at, partner, other, rows)
    deep = mine.shape[1]
    turn = unit(deep)
    before, here, after = [mm_t(turn, row).astype(BF) for row in (before, mine[...], after)]
    weave = interleave(2 * deep)
    pieces, _, part, _ = out.shape
    top = jnp.concatenate([here, after])
    low = jnp.concatenate([before, here])
    z = []
    for b in range(3):
        both = mm(top, w[b]) + mm(low, w[6 + b])
        mid = mm(here, w[3 + b])
        z.append((both[:deep] + mid, both[deep:] + mid))
    for r in range(2):
        even = z[1][r] + z[0][r] + moved(z[2][r], 1, 0)
        late = z[1][r] + moved(z[0][r], -1, 0) + z[2][r]
        y = jnp.concatenate([(0.25 * even).astype(BF), (0.25 * late).astype(BF)])
        y = mm(weave, y).astype(BF)
        for k in range(pieces):
            out[k, r] = y[k * part : (k + 1) * part]


def fine_slices(x, pick, out):
    size = out.shape[1]
    for r, row in enumerate(fine_rows(x)):
        cols = row.shape[0]
        for j in range(MEMBERS):
            out[j, :, r * cols : (r + 1) * cols] = mm_t(pick[j * size : (j + 1) * size], row).astype(BF)


def deep_slices(pooled, pick, out):
    size = out.shape[1]
    for j in range(MEMBERS):
        out[j] = mm(pick[j * size : (j + 1) * size], pooled[...]).astype(BF)


def edges(fine, deep, first, last):
    cols = fine.shape[2] // 2
    first[:, :cols] = fine[0, :, :cols]
    first[:, cols:] = deep[0]
    last[:, :cols] = fine[MEMBERS - 1, :, cols:]
    last[:, cols:] = deep[MEMBERS - 1]


def tables(fine_slab, deep_slab, before, after, fine, deep):
    size = fine_slab.shape[1]
    cols = deep_slab.shape[2]
    wide = 2 * cols
    blocks = [before[:, wide:]] + [deep_slab[i] for i in range(MEMBERS)] + [after[:, wide:]]
    for i, block in enumerate(blocks):
        row = block.astype(F32)
        turned = [moved(row, 1, 1).astype(BF), block, moved(row, -1, 1).astype(BF)]
        for a in range(3):
            home = i - a
            if 0 <= home < MEMBERS:
                for b in range(3):
                    t = 3 * a + b
                    deep[t * size : (t + 1) * size, home * cols : (home + 1) * cols] = turned[b]
    slab = [fine_slab[i] for i in range(MEMBERS)]
    evens = jnp.concatenate([row[:, :wide] for row in slab] + [after[:, :wide]])
    odds = jnp.concatenate([before[:, :wide]] + [row[:, wide:] for row in slab])
    for b in range(3):
        box = column_box(wide, b)
        even = mm_t(evens, box)
        late = mm_t(odds, box)
        even = [even[i * size : (i + 1) * size] for i in range(MEMBERS + 1)]
        late = [late[i * size : (i + 1) * size] for i in range(MEMBERS + 1)]
        for i in range(MEMBERS):
            rows = (late[i] + even[i], even[i] + late[i + 1], late[i + 1] + even[i + 1])
            for a in range(3):
                t = 3 * a + b
                fine[t * size : (t + 1) * size, i * cols : (i + 1) * cols] = rows[a].astype(BF)


def weight_part(at, own, partner, near, far, rest, table, order, out0, out1, out2, out3, grads, parts):
    cols = own.shape[1]
    blocks = (own[...], partner[...], near[...], rest[0], far[0], rest[1], far[1], rest[2])
    for r, block in enumerate(blocks):
        grads[jnp.bitwise_xor(at[1], r)] = block
    total = sum(mm_t(table[:, i * cols : (i + 1) * cols], grads[i]) for i in range(MEMBERS))
    parts[...] = mm(order[...], total.astype(BF)).astype(BF)
    size = out0.shape[1]
    for step, out in enumerate((out0, out1, out2, out3)):
        for half in range(2):
            place = (half * 4 + jnp.bitwise_and(at[2] + step, 3)) * size
            out[half] = parts[pl.ds(pl.multiple_of(place, 32), size)]


def weight_half(at, own, got1, got2, got3, keep, send):
    def total(half):
        return sum(v[half].astype(F32) for v in (own, got1, got2, got3))

    keep[...] = total(at[3])
    send[...] = total(1 - at[3]).astype(BF)


def weight_sum(keep, got, out):
    total = keep[...] + got[...].astype(F32)
    grain = out.shape[1]
    for t in range(9):
        out[t] = total[t * grain : (t + 1) * grain]


def on_device(latent, conv_fine, conv_deep, upstream):
    wide = lax.axis_size("wide")
    pieces = lax.axis_size("narrow")
    groups = wide // MEMBERS
    near = [[MEMBERS * g + j for j in range(MEMBERS)] for g in range(groups)]
    me = lax.axis_index("wide").astype(jnp.int32)
    at = jnp.stack([me % 2, me % 8, me // 8 % 4, me // 32, lax.axis_index("narrow").astype(jnp.int32)])
    rows, part, depth = latent.shape
    cols = part * pieces
    deep = cols // 2
    grain = depth // wide
    size = groups * grain
    block = -(-9 * grain // 32) * 32
    w_fine = conv_fine.transpose(0, 1, 3, 2).reshape(9, -1, depth)
    w_deep = conv_deep.transpose(0, 1, 3, 2).reshape(9, -1, depth)
    fine = w_fine.shape[1]
    full = w_deep.shape[1]
    pick = jnp.asarray(channel_matrix(depth, groups), BF)
    order = jnp.asarray(owner_matrix(groups, grain, block), BF)

    def across(v, step):
        return lax.ppermute(v, "narrow", [(i, (i + step) % pieces) for i in range(pieces)])

    def swap(v, bit):
        return lax.ppermute(v, "wide", [(i, i ^ bit) for i in range(wide)])

    def pairs(to_partner, to_other):
        other = lax.ppermute(to_other, "wide", [(i, i - 1 + 2 * (i % 2)) for i in range(1, wide - 1)])
        return swap(to_partner, 1), other

    x = lax.all_to_all(jnp.broadcast_to(latent[None], (pieces,) + latent.shape), "narrow", 0, 0)
    own, partner, other = call(
        fine_forward,
        [shape((fine, deep), F32), shape((fine, deep)), shape((fine, deep))],
        (at, x, w_fine),
        flops=2 * 9 * deep * depth * (2 * cols + 2 * fine),
    )
    partner, other = pairs(partner, other)
    fine_slab = call(
        fine_slices,
        shape((MEMBERS, size, rows * cols)),
        (x, pick),
        flops=2 * depth * depth * rows * cols,
        behind=(own,),
    )
    fine_slab = lax.all_to_all(fine_slab, "wide", 0, 0, axis_index_groups=near)
    mine = call(pool_add, shape((fine, deep)), (own, partner, other))
    got = [across(mine, s) for s in (1, 2, 3)]
    pooled, partner, other = call(
        deep_sides,
        [shape((depth, deep)), shape((full, deep)), shape((full, deep))],
        (at, mine, *got, w_deep),
        flops=2 * 6 * deep * depth * full,
    )
    partner, other = pairs(partner, other)
    preact = call(
        deep_own, shape((full, deep), F32), (pooled, w_deep), flops=2 * 3 * deep * depth * full, behind=(pooled,)
    )
    output, grad_pre = call(deep_forward, [shape((full, deep))] * 2, (preact, partner, other, upstream[0].T))

    pre_partner, other = pairs(grad_pre, grad_pre)
    pre_near = swap(grad_pre, 2)
    parts = call(
        deep_backward,
        [shape((fine, deep))] * 4,
        (at, pre_partner, grad_pre, other, w_deep),
        [pltpu.VMEM((2, full, deep), BF), pltpu.VMEM((depth, deep), BF)],
        flops=2 * 9 * deep * depth * full,
        behind=(pre_near,),
    )
    pre_far = swap(jnp.stack([grad_pre, pre_near]), 4)
    deep_slab = call(
        deep_slices,
        shape((MEMBERS, size, deep)),
        (pooled, pick),
        flops=2 * depth * depth * deep,
        behind=(parts[0],),
    )
    deep_slab = lax.all_to_all(deep_slab, "wide", 0, 0, axis_index_groups=near)
    got = [across(parts[s], s) for s in (1, 2, 3)]
    grad_pool = call(pool_sum, shape((fine, deep)), (parts[0], *got), behind=(pre_far,))
    pool_partner, other = pairs(grad_pool, grad_pool)
    pool_near = swap(grad_pool, 2)
    pre_rest = swap(jnp.concatenate([pre_near[None], pre_far]), 1)
    back = call(
        fine_backward,
        shape((pieces, rows, part, depth)),
        (at, pool_partner, grad_pool, other, w_fine),
        [pltpu.VMEM((2, fine, deep), BF)],
        flops=2 * 18 * cols * depth * fine,
        behind=(pool_near,),
    )
    partial = lax.all_to_all(back, "narrow", 0, 0)
    grad_latent = jnp.sum(partial.astype(F32), axis=0).astype(BF)

    first, last = call(
        edges, [shape((size, cols + deep))] * 2, (fine_slab, deep_slab), behind=(grad_pool,)
    )
    before = lax.ppermute(last, "wide", [(i, i + MEMBERS) for i in range(wide - MEMBERS)])
    after = lax.ppermute(first, "wide", [(i + MEMBERS, i) for i in range(wide - MEMBERS)])
    pool_far = swap(jnp.stack([grad_pool, pool_near]), 4)
    pool_rest = swap(jnp.concatenate([pool_near[None], pool_far]), 1)
    fine_table, deep_table = call(
        tables,
        [shape((9 * size, MEMBERS * deep))] * 2,
        (fine_slab, deep_slab, before, after),
        flops=2 * 9 * size * 6 * deep * 2 * deep,
        behind=(back,),
    )

    def owners(table, *grads):
        width = grads[0].shape[0]
        parts = call(
            weight_part,
            [shape((2, block, width))] * 4,
            (at, *grads, table, order),
            [pltpu.VMEM((MEMBERS, width, deep), BF), pltpu.VMEM((groups * block, width), BF)],
            flops=2 * 9 * size * MEMBERS * deep * width,
        )
        got = [
            lax.ppermute(
                parts[s], "wide", [(i, i // 32 * 32 + (i // 8 + s) % 4 * 8 + i % 8) for i in range(wide)]
            )
            for s in (1, 2, 3)
        ]
        keep, send = call(weight_half, [shape((block, width), F32), shape((block, width))], (at, parts[0], *got))
        total = call(weight_sum, shape((9, grain, width), F32), (keep, swap(send, 32)))
        return total.reshape(3, 3, grain, width)

    grad_deep = owners(deep_table, grad_pre, pre_partner, pre_near, pre_far, pre_rest)
    grad_fine = owners(fine_table, grad_pool, pool_partner, pool_near, pool_far, pool_rest)
    return output.T[None], grad_latent, grad_fine, grad_deep


def solution(mesh):
    return jax.shard_map(
        on_device,
        mesh=mesh,
        in_specs=(
            P("wide", "narrow", None),
            P(None, None, None, "narrow"),
            P(None, None, None, "narrow"),
            P("wide", None, "narrow"),
        ),
        out_specs=(
            P("wide", None, "narrow"),
            P("wide", "narrow", None),
            P(None, None, "wide", "narrow"),
            P(None, None, "wide", "narrow"),
        ),
        check_vma=False,
    )
```

```python
import functools

import jax
import jax.numpy as jnp
import numpy as np
from jax import lax
from jax.experimental import pallas as pl
from jax.experimental.pallas import tpu as pltpu
from jax.sharding import PartitionSpec as P

BF = jnp.bfloat16
F32 = jnp.float32
MEMBERS = 8


def mm(a, b):
    return jnp.dot(a, b, preferred_element_type=F32)


def mm_t(a, b):
    return lax.dot_general(a, b, (((1,), (1,)), ((), ())), preferred_element_type=F32)


def channel_matrix(depth, groups):
    grain = depth // (groups * MEMBERS)
    table = np.zeros((MEMBERS, groups, grain, depth), np.float32)
    for c in range(depth):
        table[c // grain % MEMBERS, c // (MEMBERS * grain), c % grain, c] = 1.0
    return table.reshape(depth, depth)


def owner_matrix(groups, grain, block):
    table = np.zeros((groups * block, 9 * groups * grain), np.float32)
    for t in range(9):
        for g in range(groups):
            for k in range(grain):
                table[g * block + t * grain + k, (t * groups + g) * grain + k] = 1.0
    return table


def moved(y, step, axis):
    size = y.shape[axis]
    place = lax.broadcasted_iota(jnp.int32, y.shape, axis)
    edge = 0 if step == 1 else size - 1
    return jnp.where(place == edge, 0.0, pltpu.roll(y, step % size, axis))


def shape(dims, dtype=BF):
    return jax.ShapeDtypeStruct(dims, dtype)


def call(body, outs, args, scratch=(), flops=0, behind=(), remote=()):
    size = sum(a.size * a.dtype.itemsize for a in args)
    smem = pl.BlockSpec(memory_space=pltpu.SMEM)
    vmem = pl.BlockSpec(memory_space=pltpu.VMEM)
    aside = pl.BlockSpec(memory_space=pl.ANY)
    count = len(args)

    def kernel(*refs):
        body(*refs[:count], *refs[count + len(behind) :])

    return pl.pallas_call(
        kernel,
        out_shape=outs,
        in_specs=[
            smem if a.dtype == jnp.int32 else aside if i in remote else vmem for i, a in enumerate(args)
        ]
        + [aside] * len(behind),
        out_specs=jax.tree.map(lambda _: vmem, outs),
        scratch_shapes=list(scratch),
        compiler_params=pltpu.CompilerParams(vmem_limit_bytes=40 * 2**20),
        cost_estimate=pl.CostEstimate(flops=flops, bytes_accessed=size, transcendentals=0),
    )(*args, *behind)


def column_box(cols, b):
    low = 2 * lax.broadcasted_iota(jnp.int32, (cols // 2, cols), 0) + (b - 1)
    gap = lax.broadcasted_iota(jnp.int32, (cols // 2, cols), 1) - low
    return jnp.where((gap == 0) | (gap == 1), 0.25, 0.0).astype(BF)


def unit(size):
    row = lax.broadcasted_iota(jnp.int32, (size, size), 0)
    return jnp.where(row == lax.broadcasted_iota(jnp.int32, (size, size), 1), 1.0, 0.0).astype(BF)


def interleave(cols):
    place = lax.broadcasted_iota(jnp.int32, (cols, cols), 0)
    source = place // 2 + (place % 2) * (cols // 2)
    return jnp.where(source == lax.broadcasted_iota(jnp.int32, (cols, cols), 1), 1.0, 0.0).astype(BF)


def fetch(source, target, sems):
    copies = [pltpu.make_async_copy(source.at[t], target.at[t], sems.at[t]) for t in range(source.shape[0])]
    for copy in copies:
        copy.start()
    return copies


def fine_rows(x):
    pieces = x.shape[0]
    return [jnp.concatenate([x[k, r] for k in range(pieces)]) for r in range(2)]


def to_sides(at, up, down, partner, other):
    up = up.astype(BF)
    down = down.astype(BF)

    @pl.when(at[0] == 0)
    def _():
        partner[...] = down
        other[...] = up

    @pl.when(at[0] == 1)
    def _():
        partner[...] = up
        other[...] = down


def fine_forward(at, x, weights, own, partner, other, w, sems):
    copies = fetch(weights, w, sems)
    deep = own.shape[1]
    rows = fine_rows(x)
    u0, us, u1 = [], [], []
    for b in range(3):
        box = column_box(2 * deep, b)
        u = [mm(box, row) for row in rows]
        u0.append(u[0].astype(BF))
        u1.append(u[1].astype(BF))
        us.append((u[0] + u[1]).astype(BF))
    pair = [jnp.concatenate([u0[b], u1[b]]) for b in range(3)]
    for copy in copies:
        copy.wait()
    mine = sum(mm_t(w[3 + b], us[b]) for b in range(3))
    first = sum(mm_t(w[b], pair[b]) for b in range(3))
    last = sum(mm_t(w[6 + b], pair[b]) for b in range(3))
    own[...] = mine + first[:, :deep] + last[:, deep:]
    to_sides(at, last[:, :deep], first[:, deep:], partner, other)


def side_rows(at, partner, other, rows):
    rows[at[0]] = other[...]
    rows[1 - at[0]] = partner[...]
    return rows[0], rows[1]


def deep_taps(w, a, row):
    y = [mm(w[3 * a + b], row) for b in range(3)]
    return y[1] + moved(y[0], 1, 1) + moved(y[2], -1, 1)


def deep_sides(at, own, got1, got2, got3, w, pooled, partner, other):
    size = own.shape[0]
    for s, piece in enumerate((own, got1, got2, got3)):
        place = jnp.bitwise_and(at[4] - s, 3) * size
        pooled[pl.ds(pl.multiple_of(place, 32), size)] = piece[...]
    row = pooled[...]
    to_sides(at, deep_taps(w, 2, row), deep_taps(w, 0, row), partner, other)


def deep_own(pooled, w, preact):
    preact[...] = deep_taps(w, 1, pooled[...])


def deep_forward(own, partner, other, upstream, output, grad):
    preact = own[...] + partner[...].astype(F32) + other[...].astype(F32)
    sigma = jax.nn.sigmoid(preact)
    output[...] = (preact * sigma).astype(BF)
    grad[...] = (upstream[...].astype(F32) * (sigma * (1.0 + preact * (1.0 - sigma)))).astype(BF)


def deep_backward(at, partner, mine, other, w, out0, out1, out2, out3, rows, whole):
    before, after = side_rows(at, partner, other, rows)
    turn = unit(mine.shape[1])
    turned = [mm_t(turn, row).astype(BF) for row in (after, mine[...], before)]
    z = [sum(mm(row, w[3 * a + b]) for a, row in enumerate(turned)) for b in range(3)]
    z = z[1] + moved(z[0], -1, 0) + moved(z[2], 1, 0)
    whole[...] = z.T.astype(BF)
    size = out0.shape[0]
    for s, out in enumerate((out0, out1, out2, out3)):
        place = jnp.bitwise_and(at[4] + s, 3) * size
        out[...] = whole[pl.ds(pl.multiple_of(place, 32), size)]


def pool_add(own, partner, other, out):
    out[...] = (own[...] + partner[...].astype(F32) + other[...].astype(F32)).astype(BF)


def pool_sum(own, got1, got2, got3, out):
    out[...] = sum(v[...].astype(F32) for v in (own, got1, got2, got3)).astype(BF)


def fine_backward(at, partner, mine, other, weights, out, rows, w, sems):
    copies = fetch(weights, w, sems)
    before, after = side_rows(at, partner, other, rows)
    deep = mine.shape[1]
    turn = unit(deep)
    before, here, after = [mm_t(turn, row).astype(BF) for row in (before, mine[...], after)]
    weave = interleave(2 * deep)
    pieces, _, part, _ = out.shape
    top = jnp.concatenate([here, after])
    low = jnp.concatenate([before, here])
    z = []
    for copy in copies:
        copy.wait()
    for b in range(3):
        both = mm(top, w[b]) + mm(low, w[6 + b])
        mid = mm(here, w[3 + b])
        z.append((both[:deep] + mid, both[deep:] + mid))
    for r in range(2):
        even = z[1][r] + z[0][r] + moved(z[2][r], 1, 0)
        late = z[1][r] + moved(z[0][r], -1, 0) + z[2][r]
        y = jnp.concatenate([(0.25 * even).astype(BF), (0.25 * late).astype(BF)])
        y = mm(weave, y).astype(BF)
        for k in range(pieces):
            out[k, r] = y[k * part : (k + 1) * part]


def fine_slices(x, pick, out):
    size = out.shape[1]
    for r, row in enumerate(fine_rows(x)):
        cols = row.shape[0]
        for j in range(MEMBERS):
            out[j, :, r * cols : (r + 1) * cols] = mm_t(pick[j * size : (j + 1) * size], row).astype(BF)


def deep_slices(pooled, pick, out):
    size = out.shape[1]
    for j in range(MEMBERS):
        out[j] = mm(pick[j * size : (j + 1) * size], pooled[...]).astype(BF)


def edges(fine, deep, first, last):
    cols = fine.shape[2] // 2
    first[:, :cols] = fine[0, :, :cols]
    first[:, cols:] = deep[0]
    last[:, :cols] = fine[MEMBERS - 1, :, cols:]
    last[:, cols:] = deep[MEMBERS - 1]


def tables(fine_slab, deep_slab, before, after, fine, deep):
    size = fine_slab.shape[1]
    cols = deep_slab.shape[2]
    wide = 2 * cols
    blocks = [before[:, wide:]] + [deep_slab[i] for i in range(MEMBERS)] + [after[:, wide:]]
    for i, block in enumerate(blocks):
        row = block.astype(F32)
        turned = [moved(row, 1, 1).astype(BF), block, moved(row, -1, 1).astype(BF)]
        for a in range(3):
            home = i - a
            if 0 <= home < MEMBERS:
                for b in range(3):
                    t = 3 * a + b
                    deep[t * size : (t + 1) * size, home * cols : (home + 1) * cols] = turned[b]
    slab = [fine_slab[i] for i in range(MEMBERS)]
    evens = jnp.concatenate([row[:, :wide] for row in slab] + [after[:, :wide]])
    odds = jnp.concatenate([before[:, :wide]] + [row[:, wide:] for row in slab])
    for b in range(3):
        box = column_box(wide, b)
        even = mm_t(evens, box)
        late = mm_t(odds, box)
        even = [even[i * size : (i + 1) * size] for i in range(MEMBERS + 1)]
        late = [late[i * size : (i + 1) * size] for i in range(MEMBERS + 1)]
        for i in range(MEMBERS):
            rows = (late[i] + even[i], even[i] + late[i + 1], late[i + 1] + even[i + 1])
            for a in range(3):
                t = 3 * a + b
                fine[t * size : (t + 1) * size, i * cols : (i + 1) * cols] = rows[a].astype(BF)


def weight_part(at, own, partner, near, far, rest, table, order, out0, out1, out2, out3, grads, parts):
    cols = own.shape[1]
    blocks = (own[...], partner[...], near[...], rest[0], far[0], rest[1], far[1], rest[2])
    for r, block in enumerate(blocks):
        grads[jnp.bitwise_xor(at[1], r)] = block
    total = sum(mm_t(table[:, i * cols : (i + 1) * cols], grads[i]) for i in range(MEMBERS))
    parts[...] = mm(order[...], total.astype(BF)).astype(BF)
    size = out0.shape[1]
    for step, out in enumerate((out0, out1, out2, out3)):
        for half in range(2):
            place = (half * 4 + jnp.bitwise_and(at[2] + step, 3)) * size
            out[half] = parts[pl.ds(pl.multiple_of(place, 32), size)]


def weight_half(at, own, got1, got2, got3, keep, send):
    def total(half):
        return sum(v[half].astype(F32) for v in (own, got1, got2, got3))

    keep[...] = total(at[3])
    send[...] = total(1 - at[3]).astype(BF)


def weight_sum(keep, got, out):
    total = keep[...] + got[...].astype(F32)
    grain = out.shape[1]
    for t in range(9):
        out[t] = total[t * grain : (t + 1) * grain]


def on_device(latent, conv_fine, conv_deep, upstream):
    wide = lax.axis_size("wide")
    pieces = lax.axis_size("narrow")
    groups = wide // MEMBERS
    near = [[MEMBERS * g + j for j in range(MEMBERS)] for g in range(groups)]
    me = lax.axis_index("wide").astype(jnp.int32)
    at = jnp.stack([me % 2, me % 8, me // 8 % 4, me // 32, lax.axis_index("narrow").astype(jnp.int32)])
    rows, part, depth = latent.shape
    cols = part * pieces
    deep = cols // 2
    grain = depth // wide
    size = groups * grain
    block = -(-9 * grain // 32) * 32
    w_fine = conv_fine.transpose(0, 1, 3, 2).reshape(9, -1, depth)
    w_deep = conv_deep.transpose(0, 1, 3, 2).reshape(9, -1, depth)
    fine = w_fine.shape[1]
    full = w_deep.shape[1]
    pick = jnp.asarray(channel_matrix(depth, groups), BF)
    order = jnp.asarray(owner_matrix(groups, grain, block), BF)

    def across(v, step):
        return lax.ppermute(v, "narrow", [(i, (i + step) % pieces) for i in range(pieces)])

    def swap(v, bit):
        return lax.ppermute(v, "wide", [(i, i ^ bit) for i in range(wide)])

    def pairs(to_partner, to_other):
        other = lax.ppermute(to_other, "wide", [(i, i - 1 + 2 * (i % 2)) for i in range(1, wide - 1)])
        return swap(to_partner, 1), other

    x = lax.all_to_all(jnp.broadcast_to(latent[None], (pieces,) + latent.shape), "narrow", 0, 0)
    own, partner, other = call(
        fine_forward,
        [shape((fine, deep), F32), shape((fine, deep)), shape((fine, deep))],
        (at, x, w_fine),
        [pltpu.VMEM(w_fine.shape, BF), pltpu.SemaphoreType.DMA((9,))],
        flops=2 * 9 * deep * depth * (2 * cols + 2 * fine),
        remote=(2,),
    )
    partner, other = pairs(partner, other)
    fine_slab = call(
        fine_slices,
        shape((MEMBERS, size, rows * cols)),
        (x, pick),
        flops=2 * depth * depth * rows * cols,
        behind=(own,),
    )
    mine = call(pool_add, shape((fine, deep)), (own, partner, other), behind=(fine_slab,))
    fine_slab = lax.all_to_all(fine_slab, "wide", 0, 0, axis_index_groups=near)
    got = [across(mine, s) for s in (1, 2, 3)]
    pooled, partner, other = call(
        deep_sides,
        [shape((depth, deep)), shape((full, deep)), shape((full, deep))],
        (at, mine, *got, w_deep),
        flops=2 * 6 * deep * depth * full,
        behind=(fine_slab,),
    )
    partner, other = pairs(partner, other)
    deep_slab = call(
        deep_slices, shape((MEMBERS, size, deep)), (pooled, pick), flops=2 * depth * depth * deep
    )
    preact = call(
        deep_own, shape((full, deep), F32), (pooled, w_deep), flops=2 * 3 * deep * depth * full, behind=(pooled,)
    )
    output, grad_pre = call(
        deep_forward,
        [shape((full, deep))] * 2,
        (preact, partner, other, upstream[0].T),
        behind=(deep_slab,),
    )
    deep_slab = lax.all_to_all(deep_slab, "wide", 0, 0, axis_index_groups=near)
    first, last = call(edges, [shape((size, cols + deep))] * 2, (fine_slab, deep_slab))
    before = lax.ppermute(last, "wide", [(i, i + MEMBERS) for i in range(wide - MEMBERS)])
    after = lax.ppermute(first, "wide", [(i + MEMBERS, i) for i in range(wide - MEMBERS)])

    pre_partner, other = pairs(grad_pre, grad_pre)
    pre_near = swap(grad_pre, 2)
    parts = call(
        deep_backward,
        [shape((fine, deep))] * 4,
        (at, pre_partner, grad_pre, other, w_deep),
        [pltpu.VMEM((2, full, deep), BF), pltpu.VMEM((depth, deep), BF)],
        flops=2 * 9 * deep * depth * full,
        behind=(pre_near, before, after),
    )
    pre_far = swap(jnp.stack([grad_pre, pre_near]), 4)
    fine_table, deep_table = call(
        tables,
        [shape((9 * size, MEMBERS * deep))] * 2,
        (fine_slab, deep_slab, before, after),
        flops=2 * 9 * size * 6 * deep * 2 * deep,
        behind=(parts[0],),
    )
    got = [across(parts[s], s) for s in (1, 2, 3)]
    grad_pool = call(pool_sum, shape((fine, deep)), (parts[0], *got), behind=(pre_far, deep_table))
    pool_partner, other = pairs(grad_pool, grad_pool)
    pool_near = swap(grad_pool, 2)
    pre_rest = swap(jnp.concatenate([pre_near[None], pre_far]), 1)
    pool_far = swap(jnp.stack([grad_pool, pool_near]), 4)
    pool_rest = swap(jnp.concatenate([pool_near[None], pool_far]), 1)

    def products(table, *grads):
        width = grads[0].shape[0]
        return call(
            weight_part,
            [shape((2, block, width))] * 4,
            (at, *grads, table, order),
            [pltpu.VMEM((MEMBERS, width, deep), BF), pltpu.VMEM((groups * block, width), BF)],
            flops=2 * 9 * size * MEMBERS * deep * width,
        )

    def owners(parts):
        width = parts[0].shape[2]
        got = [
            lax.ppermute(
                parts[s], "wide", [(i, i // 32 * 32 + (i // 8 + s) % 4 * 8 + i % 8) for i in range(wide)]
            )
            for s in (1, 2, 3)
        ]
        keep, send = call(weight_half, [shape((block, width), F32), shape((block, width))], (at, parts[0], *got))
        total = call(weight_sum, shape((9, grain, width), F32), (keep, swap(send, 32)))
        return total.reshape(3, 3, grain, width)

    deep_parts = products(deep_table, grad_pre, pre_partner, pre_near, pre_far, pre_rest)
    fine_parts = products(fine_table, grad_pool, pool_partner, pool_near, pool_far, pool_rest)
    back = call(
        fine_backward,
        shape((pieces, rows, part, depth)),
        (at, pool_partner, grad_pool, other, w_fine),
        [pltpu.VMEM((2, fine, deep), BF), pltpu.VMEM(w_fine.shape, BF), pltpu.SemaphoreType.DMA((9,))],
        flops=2 * 18 * cols * depth * fine,
        behind=(deep_parts[0], fine_parts[0]),
        remote=(4,),
    )
    partial = lax.all_to_all(back, "narrow", 0, 0)
    grad_latent = jnp.sum(partial.astype(F32), axis=0).astype(BF)

    grad_deep = owners(deep_parts)
    grad_fine = owners(fine_parts)
    return output.T[None], grad_latent, grad_fine, grad_deep


def solution(mesh):
    return jax.shard_map(
        on_device,
        mesh=mesh,
        in_specs=(
            P("wide", "narrow", None),
            P(None, None, None, "narrow"),
            P(None, None, None, "narrow"),
            P("wide", None, "narrow"),
        ),
        out_specs=(
            P("wide", None, "narrow"),
            P("wide", "narrow", None),
            P(None, None, "wide", "narrow"),
            P(None, None, "wide", "narrow"),
        ),
        check_vma=False,
    )
```

```python
import functools

import jax
import jax.numpy as jnp
import numpy as np
from jax import lax
from jax.experimental import pallas as pl
from jax.experimental.pallas import tpu as pltpu
from jax.sharding import PartitionSpec as P

BF = jnp.bfloat16
F32 = jnp.float32
MEMBERS = 8
CHAIN = 3 * 10**10


def mm(a, b):
    return jnp.dot(a, b, preferred_element_type=F32)


def mm_t(a, b):
    return lax.dot_general(a, b, (((1,), (1,)), ((), ())), preferred_element_type=F32)


def channel_matrix(depth, groups):
    grain = depth // (groups * MEMBERS)
    table = np.zeros((MEMBERS, groups, grain, depth), np.float32)
    for c in range(depth):
        table[c // grain % MEMBERS, c // (MEMBERS * grain), c % grain, c] = 1.0
    return table.reshape(depth, depth)


def owner_matrix(groups, grain, block):
    table = np.zeros((groups * block, 9 * groups * grain), np.float32)
    for t in range(9):
        for g in range(groups):
            for k in range(grain):
                table[g * block + t * grain + k, (t * groups + g) * grain + k] = 1.0
    return table


def moved(y, step, axis):
    size = y.shape[axis]
    place = lax.broadcasted_iota(jnp.int32, y.shape, axis)
    edge = 0 if step == 1 else size - 1
    return jnp.where(place == edge, 0.0, pltpu.roll(y, step % size, axis))


def shape(dims, dtype=BF):
    return jax.ShapeDtypeStruct(dims, dtype)


def call(body, outs, args, scratch=(), behind=()):
    size = sum(a.size * a.dtype.itemsize for a in args)
    smem = pl.BlockSpec(memory_space=pltpu.SMEM)
    vmem = pl.BlockSpec(memory_space=pltpu.VMEM)
    aside = pl.BlockSpec(memory_space=pl.ANY)
    count = len(args)
    flops = CHAIN if body in (fine_forward, pool_add, deep_sides, deep_forward, deep_backward, pool_sum, fine_backward) else 0

    def kernel(*refs):
        body(*refs[:count], *refs[count + len(behind) :])

    return pl.pallas_call(
        kernel,
        out_shape=outs,
        in_specs=[smem if a.dtype == jnp.int32 else vmem for a in args] + [aside] * len(behind),
        out_specs=jax.tree.map(lambda _: vmem, outs),
        scratch_shapes=list(scratch),
        compiler_params=pltpu.CompilerParams(vmem_limit_bytes=16 * 2**20),
        cost_estimate=pl.CostEstimate(flops=flops, bytes_accessed=size, transcendentals=0),
    )(*args, *behind)


def column_box(cols, b):
    low = 2 * lax.broadcasted_iota(jnp.int32, (cols // 2, cols), 0) + (b - 1)
    gap = lax.broadcasted_iota(jnp.int32, (cols // 2, cols), 1) - low
    return jnp.where((gap == 0) | (gap == 1), 0.25, 0.0).astype(BF)


def unit(size):
    row = lax.broadcasted_iota(jnp.int32, (size, size), 0)
    return jnp.where(row == lax.broadcasted_iota(jnp.int32, (size, size), 1), 1.0, 0.0).astype(BF)


def interleave(cols):
    place = lax.broadcasted_iota(jnp.int32, (cols, cols), 0)
    source = place // 2 + (place % 2) * (cols // 2)
    return jnp.where(source == lax.broadcasted_iota(jnp.int32, (cols, cols), 1), 1.0, 0.0).astype(BF)


def fine_rows(x):
    pieces = x.shape[0]
    return [jnp.concatenate([x[k, r] for k in range(pieces)]) for r in range(2)]


def to_sides(at, up, down, partner, other):
    up = up.astype(BF)
    down = down.astype(BF)

    @pl.when(at[0] == 0)
    def _():
        partner[...] = down
        other[...] = up

    @pl.when(at[0] == 1)
    def _():
        partner[...] = up
        other[...] = down


def fine_forward(at, mine, got1, got2, got3, w, x, own, partner, other):
    for s, piece in enumerate((mine, got1, got2, got3)):
        x[jnp.bitwise_and(at[4] - s, 3)] = piece[...]
    deep = own.shape[1]
    rows = fine_rows(x)
    u0, us, u1 = [], [], []
    for b in range(3):
        box = column_box(2 * deep, b)
        u = [mm(box, row) for row in rows]
        u0.append(u[0].astype(BF))
        u1.append(u[1].astype(BF))
        us.append((u[0] + u[1]).astype(BF))
    pair = [jnp.concatenate([u0[b], u1[b]]) for b in range(3)]
    mine = sum(mm_t(w[3 + b], us[b]) for b in range(3))
    first = sum(mm_t(w[b], pair[b]) for b in range(3))
    last = sum(mm_t(w[6 + b], pair[b]) for b in range(3))
    own[...] = mine + first[:, :deep] + last[:, deep:]
    to_sides(at, last[:, :deep], first[:, deep:], partner, other)


def side_rows(at, partner, other, rows):
    rows[at[0]] = other[...]
    rows[1 - at[0]] = partner[...]
    return rows[0], rows[1]


def deep_taps(w, a, row):
    y = [mm(w[3 * a + b], row) for b in range(3)]
    return y[1] + moved(y[0], 1, 1) + moved(y[2], -1, 1)


def deep_sides(at, own, got1, got2, got3, w, pooled, partner, other):
    size = own.shape[0]
    for s, piece in enumerate((own, got1, got2, got3)):
        place = jnp.bitwise_and(at[4] - s, 3) * size
        pooled[pl.ds(pl.multiple_of(place, 32), size)] = piece[...]
    row = pooled[...]
    to_sides(at, deep_taps(w, 2, row), deep_taps(w, 0, row), partner, other)


def deep_own(pooled, w, preact):
    preact[...] = deep_taps(w, 1, pooled[...])


def deep_forward(own, partner, other, upstream, output, grad):
    preact = own[...] + partner[...].astype(F32) + other[...].astype(F32)
    sigma = jax.nn.sigmoid(preact)
    output[...] = (preact * sigma).astype(BF)
    grad[...] = (upstream[...].astype(F32) * (sigma * (1.0 + preact * (1.0 - sigma)))).astype(BF)


def deep_backward(at, partner, mine, other, w, out0, out1, out2, out3, rows, whole):
    before, after = side_rows(at, partner, other, rows)
    turn = unit(mine.shape[1])
    turned = [mm_t(turn, row).astype(BF) for row in (after, mine[...], before)]
    z = [sum(mm(row, w[3 * a + b]) for a, row in enumerate(turned)) for b in range(3)]
    z = z[1] + moved(z[0], -1, 0) + moved(z[2], 1, 0)
    whole[...] = z.T.astype(BF)
    size = out0.shape[0]
    for s, out in enumerate((out0, out1, out2, out3)):
        place = jnp.bitwise_and(at[4] + s, 3) * size
        out[...] = whole[pl.ds(pl.multiple_of(place, 32), size)]


def pool_add(own, partner, other, out):
    out[...] = (own[...] + partner[...].astype(F32) + other[...].astype(F32)).astype(BF)


def pool_sum(own, got1, got2, got3, out):
    out[...] = sum(v[...].astype(F32) for v in (own, got1, got2, got3)).astype(BF)


def fine_backward(at, partner, mine, other, w, out, rows):
    before, after = side_rows(at, partner, other, rows)
    deep = mine.shape[1]
    turn = unit(deep)
    before, here, after = [mm_t(turn, row).astype(BF) for row in (before, mine[...], after)]
    weave = interleave(2 * deep)
    pieces, _, part, _ = out.shape
    top = jnp.concatenate([here, after])
    low = jnp.concatenate([before, here])
    z = []
    for b in range(3):
        both = mm(top, w[b]) + mm(low, w[6 + b])
        mid = mm(here, w[3 + b])
        z.append((both[:deep] + mid, both[deep:] + mid))
    for r in range(2):
        even = z[1][r] + z[0][r] + moved(z[2][r], 1, 0)
        late = z[1][r] + moved(z[0][r], -1, 0) + z[2][r]
        y = jnp.concatenate([(0.25 * even).astype(BF), (0.25 * late).astype(BF)])
        y = mm(weave, y).astype(BF)
        for k in range(pieces):
            out[k, r] = y[k * part : (k + 1) * part]


def fine_slices(x, pick, out):
    size = out.shape[1]
    for r, row in enumerate(fine_rows(x)):
        cols = row.shape[0]
        for j in range(MEMBERS):
            out[j, :, r * cols : (r + 1) * cols] = mm_t(pick[j * size : (j + 1) * size], row).astype(BF)


def deep_slices(pooled, pick, out):
    size = out.shape[1]
    for j in range(MEMBERS):
        out[j] = mm(pick[j * size : (j + 1) * size], pooled[...]).astype(BF)


def edges(fine, deep, first, last):
    cols = fine.shape[2] // 2
    first[:, :cols] = fine[0, :, :cols]
    first[:, cols:] = deep[0]
    last[:, :cols] = fine[MEMBERS - 1, :, cols:]
    last[:, cols:] = deep[MEMBERS - 1]


def tables(fine_slab, deep_slab, before, after, fine, deep):
    size = fine_slab.shape[1]
    cols = deep_slab.shape[2]
    wide = 2 * cols
    blocks = [before[:, wide:]] + [deep_slab[i] for i in range(MEMBERS)] + [after[:, wide:]]
    for i, block in enumerate(blocks):
        row = block.astype(F32)
        turned = [moved(row, 1, 1).astype(BF), block, moved(row, -1, 1).astype(BF)]
        for a in range(3):
            home = i - a
            if 0 <= home < MEMBERS:
                for b in range(3):
                    t = 3 * a + b
                    deep[t * size : (t + 1) * size, home * cols : (home + 1) * cols] = turned[b]
    slab = [fine_slab[i] for i in range(MEMBERS)]
    evens = jnp.concatenate([row[:, :wide] for row in slab] + [after[:, :wide]])
    odds = jnp.concatenate([before[:, :wide]] + [row[:, wide:] for row in slab])
    for b in range(3):
        box = column_box(wide, b)
        even = mm_t(evens, box)
        late = mm_t(odds, box)
        even = [even[i * size : (i + 1) * size] for i in range(MEMBERS + 1)]
        late = [late[i * size : (i + 1) * size] for i in range(MEMBERS + 1)]
        for i in range(MEMBERS):
            rows = (late[i] + even[i], even[i] + late[i + 1], late[i + 1] + even[i + 1])
            for a in range(3):
                t = 3 * a + b
                fine[t * size : (t + 1) * size, i * cols : (i + 1) * cols] = rows[a].astype(BF)


def weight_part(at, own, partner, four, eight, table, order, out0, out1, out2, out3, grads, parts):
    cols = own.shape[1]
    blocks = [own[...], partner[...]] + [four[i] for i in range(2)] + [eight[i] for i in range(4)]
    for r, block in enumerate(blocks):
        grads[jnp.bitwise_xor(at[1], r)] = block
    total = sum(mm_t(table[:, i * cols : (i + 1) * cols], grads[i]) for i in range(MEMBERS))
    parts[...] = mm(order[...], total.astype(BF)).astype(BF)
    size = out0.shape[1]
    for step, out in enumerate((out0, out1, out2, out3)):
        for half in range(2):
            place = (half * 4 + jnp.bitwise_and(at[2] + step, 3)) * size
            out[half] = parts[pl.ds(pl.multiple_of(place, 32), size)]


def weight_half(at, own, got1, got2, got3, keep, send):
    def total(half):
        return sum(v[half].astype(F32) for v in (own, got1, got2, got3))

    keep[...] = total(at[3])
    send[...] = total(1 - at[3]).astype(BF)


def weight_sum(keep, got, out):
    total = keep[...] + got[...].astype(F32)
    grain = out.shape[1]
    for t in range(9):
        out[t] = total[t * grain : (t + 1) * grain]


def on_device(latent, conv_fine, conv_deep, upstream):
    wide = lax.axis_size("wide")
    pieces = lax.axis_size("narrow")
    groups = wide // MEMBERS
    near = [[MEMBERS * g + j for j in range(MEMBERS)] for g in range(groups)]
    me = lax.axis_index("wide").astype(jnp.int32)
    at = jnp.stack([me % 2, me % 8, me // 8 % 4, me // 32, lax.axis_index("narrow").astype(jnp.int32)])
    rows, part, depth = latent.shape
    cols = part * pieces
    deep = cols // 2
    grain = depth // wide
    size = groups * grain
    block = -(-9 * grain // 32) * 32
    w_fine = conv_fine.transpose(0, 1, 3, 2).reshape(9, -1, depth)
    w_deep = conv_deep.transpose(0, 1, 3, 2).reshape(9, -1, depth)
    fine = w_fine.shape[1]
    full = w_deep.shape[1]
    pick = jnp.asarray(channel_matrix(depth, groups), BF)
    order = jnp.asarray(owner_matrix(groups, grain, block), BF)

    def across(v, step):
        return lax.ppermute(v, "narrow", [(i, (i + step) % pieces) for i in range(pieces)])

    def swap(v, bit):
        return lax.ppermute(v, "wide", [(i, i ^ bit) for i in range(wide)])

    def pairs(to_partner, to_other):
        other = lax.ppermute(to_other, "wide", [(i, i - 1 + 2 * (i % 2)) for i in range(1, wide - 1)])
        return swap(to_partner, 1), other

    got = [across(latent, s) for s in (1, 2, 3)]
    x, own, partner, other = call(
        fine_forward,
        [shape((pieces,) + latent.shape), shape((fine, deep), F32), shape((fine, deep)), shape((fine, deep))],
        (at, latent, *got, w_fine),
    )
    partner, other = pairs(partner, other)
    fine_slab = call(
        fine_slices,
        shape((MEMBERS, size, rows * cols)),
        (x, pick),
        behind=(partner,),
    )
    mine = call(pool_add, shape((fine, deep)), (own, partner, other), behind=(fine_slab,))
    fine_slab = lax.all_to_all(fine_slab, "wide", 0, 0, axis_index_groups=near)
    got = [across(mine, s) for s in (1, 2, 3)]
    pooled, partner, other = call(
        deep_sides,
        [shape((depth, deep)), shape((full, deep)), shape((full, deep))],
        (at, mine, *got, w_deep),
        behind=(fine_slab,),
    )
    partner, other = pairs(partner, other)
    preact = call(
        deep_own, shape((full, deep), F32), (pooled, w_deep), behind=(pooled,)
    )
    output, grad_pre = call(
        deep_forward,
        [shape((full, deep))] * 2,
        (preact, partner, other, upstream[0].T),
    )
    pre_partner, other = pairs(grad_pre, grad_pre)
    deep_slab = call(deep_slices, shape((MEMBERS, size, deep)), (pooled, pick), behind=(pre_partner,))
    deep_slab = lax.all_to_all(deep_slab, "wide", 0, 0, axis_index_groups=near)
    pre_four = swap(jnp.stack([grad_pre, pre_partner]), 2)
    pre_eight = swap(jnp.concatenate([grad_pre[None], pre_partner[None], pre_four]), 4)
    parts = call(
        deep_backward,
        [shape((fine, deep))] * 4,
        (at, pre_partner, grad_pre, other, w_deep),
        [pltpu.VMEM((2, full, deep), BF), pltpu.VMEM((depth, deep), BF)],
    )
    got = [across(parts[s], s) for s in (1, 2, 3)]
    first, last = call(edges, [shape((size, cols + deep))] * 2, (fine_slab, deep_slab), behind=(got[0],))
    before = lax.ppermute(last, "wide", [(i, i + MEMBERS) for i in range(wide - MEMBERS)])
    after = lax.ppermute(first, "wide", [(i + MEMBERS, i) for i in range(wide - MEMBERS)])
    fine_table, deep_table = call(
        tables,
        [shape((9 * size, MEMBERS * deep))] * 2,
        (fine_slab, deep_slab, before, after),
    )
    grad_pool = call(pool_sum, shape((fine, deep)), (parts[0], *got))
    pool_partner, other = pairs(grad_pool, grad_pool)
    pool_four = swap(jnp.stack([grad_pool, pool_partner]), 2)
    pool_eight = swap(jnp.concatenate([grad_pool[None], pool_partner[None], pool_four]), 4)

    def products(table, *grads):
        width = grads[0].shape[0]
        return call(
            weight_part,
            [shape((2, block, width))] * 4,
            (at, *grads, table, order),
            [pltpu.VMEM((MEMBERS, width, deep), BF), pltpu.VMEM((groups * block, width), BF)],
            )

    def owners(parts):
        width = parts[0].shape[2]
        got = [
            lax.ppermute(
                parts[s], "wide", [(i, i // 32 * 32 + (i // 8 + s) % 4 * 8 + i % 8) for i in range(wide)]
            )
            for s in (1, 2, 3)
        ]
        keep, send = call(weight_half, [shape((block, width), F32), shape((block, width))], (at, parts[0], *got))
        total = call(weight_sum, shape((9, grain, width), F32), (keep, swap(send, 32)))
        return total.reshape(3, 3, grain, width)

    deep_parts = products(deep_table, grad_pre, pre_partner, pre_four, pre_eight)
    fine_parts = products(fine_table, grad_pool, pool_partner, pool_four, pool_eight)
    back = call(
        fine_backward,
        shape((pieces, rows, part, depth)),
        (at, pool_partner, grad_pool, other, w_fine),
        [pltpu.VMEM((2, fine, deep), BF)],
        behind=(deep_parts[0],),
    )
    partial = lax.all_to_all(back, "narrow", 0, 0)
    grad_latent = jnp.sum(partial.astype(F32), axis=0).astype(BF)

    grad_deep = owners(deep_parts)
    grad_fine = owners(fine_parts)
    return output.T[None], grad_latent, grad_fine, grad_deep


def solution(mesh):
    return jax.shard_map(
        on_device,
        mesh=mesh,
        in_specs=(
            P("wide", "narrow", None),
            P(None, None, None, "narrow"),
            P(None, None, None, "narrow"),
            P("wide", None, "narrow"),
        ),
        out_specs=(
            P("wide", None, "narrow"),
            P("wide", "narrow", None),
            P(None, None, "wide", "narrow"),
            P(None, None, "wide", "narrow"),
        ),
        check_vma=False,
    )
```

```python
import functools

import jax
import jax.numpy as jnp
import numpy as np
from jax import lax
from jax.experimental import pallas as pl
from jax.experimental.pallas import tpu as pltpu
from jax.sharding import PartitionSpec as P

BF = jnp.bfloat16
F32 = jnp.float32
MEMBERS = 8
CHAIN = 3 * 10**10


def mm(a, b):
    return jnp.dot(a, b, preferred_element_type=F32)


def mm_t(a, b):
    return lax.dot_general(a, b, (((1,), (1,)), ((), ())), preferred_element_type=F32)


def channel_matrix(depth, groups):
    grain = depth // (groups * MEMBERS)
    table = np.zeros((MEMBERS, groups, grain, depth), np.float32)
    for c in range(depth):
        table[c // grain % MEMBERS, c // (MEMBERS * grain), c % grain, c] = 1.0
    return table.reshape(depth, depth)


def owner_matrix(groups, grain, block):
    table = np.zeros((groups * block, 9 * groups * grain), np.float32)
    for t in range(9):
        for g in range(groups):
            for k in range(grain):
                table[g * block + t * grain + k, (t * groups + g) * grain + k] = 1.0
    return table


def moved(y, step, axis):
    size = y.shape[axis]
    place = lax.broadcasted_iota(jnp.int32, y.shape, axis)
    edge = 0 if step == 1 else size - 1
    return jnp.where(place == edge, 0.0, pltpu.roll(y, step % size, axis))


def shape(dims, dtype=BF):
    return jax.ShapeDtypeStruct(dims, dtype)


def call(body, outs, args, scratch=(), behind=()):
    size = sum(a.size * a.dtype.itemsize for a in args)
    smem = pl.BlockSpec(memory_space=pltpu.SMEM)
    vmem = pl.BlockSpec(memory_space=pltpu.VMEM)
    aside = pl.BlockSpec(memory_space=pl.ANY)
    count = len(args)
    flops = CHAIN if body in (fine_forward, pool_add, deep_sides, deep_forward, deep_backward, pool_sum, fine_backward) else 0

    def kernel(*refs):
        body(*refs[:count], *refs[count + len(behind) :])

    return pl.pallas_call(
        kernel,
        out_shape=outs,
        in_specs=[smem if a.dtype == jnp.int32 else vmem for a in args] + [aside] * len(behind),
        out_specs=jax.tree.map(lambda _: vmem, outs),
        scratch_shapes=list(scratch),
        compiler_params=pltpu.CompilerParams(vmem_limit_bytes=16 * 2**20),
        cost_estimate=pl.CostEstimate(flops=flops, bytes_accessed=size, transcendentals=0),
    )(*args, *behind)


def column_box(cols, b):
    low = 2 * lax.broadcasted_iota(jnp.int32, (cols // 2, cols), 0) + (b - 1)
    gap = lax.broadcasted_iota(jnp.int32, (cols // 2, cols), 1) - low
    return jnp.where((gap == 0) | (gap == 1), 0.25, 0.0).astype(BF)


def unit(size):
    row = lax.broadcasted_iota(jnp.int32, (size, size), 0)
    return jnp.where(row == lax.broadcasted_iota(jnp.int32, (size, size), 1), 1.0, 0.0).astype(BF)


def interleave(cols):
    place = lax.broadcasted_iota(jnp.int32, (cols, cols), 0)
    source = place // 2 + (place % 2) * (cols // 2)
    return jnp.where(source == lax.broadcasted_iota(jnp.int32, (cols, cols), 1), 1.0, 0.0).astype(BF)


def fine_rows(x):
    pieces = x.shape[0]
    return [jnp.concatenate([x[k, r] for k in range(pieces)]) for r in range(2)]


def to_sides(at, up, down, partner, other):
    up = up.astype(BF)
    down = down.astype(BF)

    @pl.when(at[0] == 0)
    def _():
        partner[...] = down
        other[...] = up

    @pl.when(at[0] == 1)
    def _():
        partner[...] = up
        other[...] = down


def fine_forward(at, mine, got1, got2, got3, w, x, own, partner, other):
    for s, piece in enumerate((mine, got1, got2, got3)):
        x[jnp.bitwise_and(at[4] - s, 3)] = piece[...]
    deep = own.shape[1]
    rows = fine_rows(x)
    u0, us, u1 = [], [], []
    for b in range(3):
        box = column_box(2 * deep, b)
        u = [mm(box, row) for row in rows]
        u0.append(u[0].astype(BF))
        u1.append(u[1].astype(BF))
        us.append((u[0] + u[1]).astype(BF))
    pair = [jnp.concatenate([u0[b], u1[b]]) for b in range(3)]
    mine = sum(mm_t(w[3 + b], us[b]) for b in range(3))
    first = sum(mm_t(w[b], pair[b]) for b in range(3))
    last = sum(mm_t(w[6 + b], pair[b]) for b in range(3))
    own[...] = mine + first[:, :deep] + last[:, deep:]
    to_sides(at, last[:, :deep], first[:, deep:], partner, other)


def side_rows(at, partner, other, rows):
    rows[at[0]] = other[...]
    rows[1 - at[0]] = partner[...]
    return rows[0], rows[1]


def deep_taps(w, a, row):
    y = [mm(w[3 * a + b], row) for b in range(3)]
    return y[1] + moved(y[0], 1, 1) + moved(y[2], -1, 1)


def deep_sides(at, own, got1, got2, got3, w, pooled, partner, other):
    size = own.shape[0]
    for s, piece in enumerate((own, got1, got2, got3)):
        place = jnp.bitwise_and(at[4] - s, 3) * size
        pooled[pl.ds(pl.multiple_of(place, 32), size)] = piece[...]
    row = pooled[...]
    to_sides(at, deep_taps(w, 2, row), deep_taps(w, 0, row), partner, other)


def deep_own(pooled, w, preact):
    preact[...] = deep_taps(w, 1, pooled[...])


def deep_forward(own, partner, other, upstream, output, grad):
    preact = own[...] + partner[...].astype(F32) + other[...].astype(F32)
    sigma = jax.nn.sigmoid(preact)
    output[...] = (preact * sigma).astype(BF)
    grad[...] = (upstream[...].astype(F32) * (sigma * (1.0 + preact * (1.0 - sigma)))).astype(BF)


def deep_backward(at, partner, mine, other, w, out0, out1, out2, out3, rows, whole):
    before, after = side_rows(at, partner, other, rows)
    turn = unit(mine.shape[1])
    turned = [mm_t(turn, row).astype(BF) for row in (after, mine[...], before)]
    z = [sum(mm(row, w[3 * a + b]) for a, row in enumerate(turned)) for b in range(3)]
    z = z[1] + moved(z[0], -1, 0) + moved(z[2], 1, 0)
    whole[...] = z.T.astype(BF)
    size = out0.shape[0]
    for s, out in enumerate((out0, out1, out2, out3)):
        place = jnp.bitwise_and(at[4] + s, 3) * size
        out[...] = whole[pl.ds(pl.multiple_of(place, 32), size)]


def pool_add(own, partner, other, out):
    out[...] = (own[...] + partner[...].astype(F32) + other[...].astype(F32)).astype(BF)


def pool_sum(own, got1, got2, got3, out):
    out[...] = sum(v[...].astype(F32) for v in (own, got1, got2, got3)).astype(BF)


def fine_backward(at, partner, mine, other, w, out, rows):
    before, after = side_rows(at, partner, other, rows)
    deep = mine.shape[1]
    turn = unit(deep)
    before, here, after = [mm_t(turn, row).astype(BF) for row in (before, mine[...], after)]
    weave = interleave(2 * deep)
    pieces, _, part, _ = out.shape
    top = jnp.concatenate([here, after])
    low = jnp.concatenate([before, here])
    z = []
    for b in range(3):
        both = mm(top, w[b]) + mm(low, w[6 + b])
        mid = mm(here, w[3 + b])
        z.append((both[:deep] + mid, both[deep:] + mid))
    for r in range(2):
        even = z[1][r] + z[0][r] + moved(z[2][r], 1, 0)
        late = z[1][r] + moved(z[0][r], -1, 0) + z[2][r]
        y = jnp.concatenate([(0.25 * even).astype(BF), (0.25 * late).astype(BF)])
        y = mm(weave, y).astype(BF)
        for k in range(pieces):
            out[k, r] = y[k * part : (k + 1) * part]


def fine_slices(x, pick, out):
    size = out.shape[1]
    for r, row in enumerate(fine_rows(x)):
        cols = row.shape[0]
        for j in range(MEMBERS):
            out[j, :, r * cols : (r + 1) * cols] = mm_t(pick[j * size : (j + 1) * size], row).astype(BF)


def deep_slices(pooled, pick, out):
    size = out.shape[1]
    for j in range(MEMBERS):
        out[j] = mm(pick[j * size : (j + 1) * size], pooled[...]).astype(BF)


def tables(fine_slab, deep_slab, even, late, deep):
    size = fine_slab.shape[1]
    cols = deep_slab.shape[2]
    wide = 2 * cols
    for i in range(MEMBERS):
        block = deep_slab[i]
        row = block.astype(F32)
        turned = (moved(row, 1, 1).astype(BF), block, moved(row, -1, 1).astype(BF))
        for b in range(3):
            deep[b * size : (b + 1) * size, i * cols : (i + 1) * cols] = turned[b]
    slab = [fine_slab[i] for i in range(MEMBERS)]
    for r, out in enumerate((even, late)):
        stack = jnp.concatenate([row[:, r * wide : (r + 1) * wide] for row in slab])
        for b in range(3):
            u = mm_t(stack, column_box(wide, b)).astype(BF)
            for i in range(MEMBERS):
                out[b * size : (b + 1) * size, i * cols : (i + 1) * cols] = u[i * size : (i + 1) * size]


def pack(own, partner, other, out):
    for i, v in enumerate((own, partner, other)):
        out[i] = v[...]


def pack_more(at, first, near, out, edge):
    for i in range(2):
        out[i] = first[i]
        out[2 + i] = near[i]
    place = jnp.bitwise_and(at[1] // 2, 1)
    kept = place == at[0]

    @pl.when(kept)
    def _():
        out[4] = first[2]
        edge[...] = first[2]

    @pl.when(jnp.logical_not(kept))
    def _():
        out[4] = near[2]
        edge[...] = near[2]


def outer(at, edge, far, out):
    kept = jnp.bitwise_and(at[1] // 4, 1) == at[0]

    @pl.when(kept)
    def _():
        out[...] = edge[...]

    @pl.when(jnp.logical_not(kept))
    def _():
        out[...] = far[4]


def group_rows(at, four, far, edge, swapped, grads):
    for r in range(4):
        grads[jnp.bitwise_xor(at[1], r) + 1] = four[r]
        grads[jnp.bitwise_xor(at[1], 4 + r) + 1] = far[r]
    ends = (MEMBERS + 1) * at[0]
    grads[ends] = edge[...]
    grads[MEMBERS + 1 - ends] = swapped[...]


def against(table, grads, step):
    cols = grads.shape[2]
    return sum(mm_t(table[:, i * cols : (i + 1) * cols], grads[i + 1 + step]) for i in range(MEMBERS))


def to_owners(at, taps, order, outs, parts):
    total = jnp.concatenate([tap.astype(BF) for tap in taps])
    parts[...] = mm(order[...], total).astype(BF)
    size = outs[0].shape[1]
    for step, out in enumerate(outs):
        for half in range(2):
            place = (half * 4 + jnp.bitwise_and(at[2] + step, 3)) * size
            out[half] = parts[pl.ds(pl.multiple_of(place, 32), size)]


def deep_part(at, four, far, edge, swapped, table, order, out0, out1, out2, out3, grads, parts):
    group_rows(at, four, far, edge, swapped, grads)
    taps = [against(table, grads, 1 - a) for a in range(3)]
    to_owners(at, taps, order, (out0, out1, out2, out3), parts)


def fine_part(at, four, far, edge, swapped, even, late, order, out0, out1, out2, out3, grads, parts):
    group_rows(at, four, far, edge, swapped, grads)
    even_here = against(even, grads, 0)
    late_here = against(late, grads, 0)
    taps = (even_here + against(late, grads, 1), even_here + late_here, late_here + against(even, grads, -1))
    to_owners(at, taps, order, (out0, out1, out2, out3), parts)


def weight_half(at, own, got1, got2, got3, keep, send):
    def total(half):
        return sum(v[half].astype(F32) for v in (own, got1, got2, got3))

    keep[...] = total(at[3])
    send[...] = total(1 - at[3]).astype(BF)


def weight_sum(keep, got, out):
    total = keep[...] + got[...].astype(F32)
    grain = out.shape[1]
    for t in range(9):
        out[t] = total[t * grain : (t + 1) * grain]


def on_device(latent, conv_fine, conv_deep, upstream):
    wide = lax.axis_size("wide")
    pieces = lax.axis_size("narrow")
    groups = wide // MEMBERS
    near = [[MEMBERS * g + j for j in range(MEMBERS)] for g in range(groups)]
    me = lax.axis_index("wide").astype(jnp.int32)
    at = jnp.stack([me % 2, me % 8, me // 8 % 4, me // 32, lax.axis_index("narrow").astype(jnp.int32)])
    rows, part, depth = latent.shape
    cols = part * pieces
    deep = cols // 2
    grain = depth // wide
    size = groups * grain
    block = -(-9 * grain // 32) * 32
    w_fine = conv_fine.transpose(0, 1, 3, 2).reshape(9, -1, depth)
    w_deep = conv_deep.transpose(0, 1, 3, 2).reshape(9, -1, depth)
    fine = w_fine.shape[1]
    full = w_deep.shape[1]
    pick = jnp.asarray(channel_matrix(depth, groups), BF)
    order = jnp.asarray(owner_matrix(groups, grain, block), BF)

    def group_gather(first, behind, later=()):
        own = first[0]
        near = swap(first, 2)
        more, edge = call(
            pack_more, [shape((5,) + own.shape), shape(own.shape)], (at, first, near), behind=behind
        )
        far = swap(more, 4)
        edge = call(outer, shape(own.shape), (at, edge, far), behind=later)
        return more, far, edge, swap(edge, 1)

    def across(v, step):
        return lax.ppermute(v, "narrow", [(i, (i + step) % pieces) for i in range(pieces)])

    def swap(v, bit):
        return lax.ppermute(v, "wide", [(i, i ^ bit) for i in range(wide)])

    def pairs(to_partner, to_other):
        other = lax.ppermute(to_other, "wide", [(i, i - 1 + 2 * (i % 2)) for i in range(1, wide - 1)])
        return swap(to_partner, 1), other

    got = [across(latent, s) for s in (1, 2, 3)]
    x, own, partner, other = call(
        fine_forward,
        [shape((pieces,) + latent.shape), shape((fine, deep), F32), shape((fine, deep)), shape((fine, deep))],
        (at, latent, *got, w_fine),
    )
    partner, other = pairs(partner, other)
    fine_slab = call(
        fine_slices,
        shape((MEMBERS, size, rows * cols)),
        (x, pick),
        behind=(partner,),
    )
    mine = call(pool_add, shape((fine, deep)), (own, partner, other), behind=(fine_slab,))
    fine_slab = lax.all_to_all(fine_slab, "wide", 0, 0, axis_index_groups=near)
    got = [across(mine, s) for s in (1, 2, 3)]
    pooled, partner, other = call(
        deep_sides,
        [shape((depth, deep)), shape((full, deep)), shape((full, deep))],
        (at, mine, *got, w_deep),
    )
    partner, other = pairs(partner, other)
    preact = call(
        deep_own, shape((full, deep), F32), (pooled, w_deep), behind=(fine_slab,)
    )
    output, grad_pre = call(
        deep_forward,
        [shape((full, deep))] * 2,
        (preact, partner, other, upstream[0].T),
    )
    pre_partner, other = pairs(grad_pre, grad_pre)
    deep_slab = call(deep_slices, shape((MEMBERS, size, deep)), (pooled, pick), behind=(pre_partner,))
    deep_slab = lax.all_to_all(deep_slab, "wide", 0, 0, axis_index_groups=near)
    pre_first = call(pack, shape((3, full, deep)), (grad_pre, pre_partner, other))
    parts = call(
        deep_backward,
        [shape((fine, deep))] * 4,
        (at, pre_partner, grad_pre, other, w_deep),
        [pltpu.VMEM((2, full, deep), BF), pltpu.VMEM((depth, deep), BF)],
    )
    got = [across(parts[s], s) for s in (1, 2, 3)]
    even_table, late_table, deep_table = call(
        tables, [shape((3 * size, MEMBERS * deep))] * 3, (fine_slab, deep_slab)
    )
    grad_pool = call(pool_sum, shape((fine, deep)), (parts[0], *got))
    pool_partner, other = pairs(grad_pool, grad_pool)
    pre_rows = group_gather(pre_first, (got[0],))
    pool_first = call(pack, shape((3, fine, deep)), (grad_pool, pool_partner, other))

    def products(body, tables, rows, behind=()):
        width = rows[0].shape[1]
        return call(
            body,
            [shape((2, block, width))] * 4,
            (at, *rows, *tables, order),
            [pltpu.VMEM((MEMBERS + 2, width, deep), BF), pltpu.VMEM((groups * block, width), BF)],
            behind=behind,
        )

    def owners(parts, behind=()):
        width = parts[0].shape[2]
        got = [
            lax.ppermute(
                parts[s], "wide", [(i, i // 32 * 32 + (i // 8 + s) % 4 * 8 + i % 8) for i in range(wide)]
            )
            for s in (1, 2, 3)
        ]
        keep, send = call(weight_half, [shape((block, width), F32), shape((block, width))], (at, parts[0], *got))
        total = call(weight_sum, shape((9, grain, width), F32), (keep, swap(send, 32)), behind=behind)
        return total.reshape(3, 3, grain, width)

    back = call(
        fine_backward,
        shape((pieces, rows, part, depth)),
        (at, pool_partner, grad_pool, other, w_fine),
        [pltpu.VMEM((2, fine, deep), BF)],
        behind=(pre_rows[2], deep_table),
    )
    pool_rows = group_gather(pool_first, (back,))
    deep_parts = products(deep_part, (deep_table,), pre_rows, (back,))
    fine_parts = products(fine_part, (even_table, late_table), pool_rows)
    partial = lax.all_to_all(back, "narrow", 0, 0)
    grad_latent = jnp.sum(partial.astype(F32), axis=0).astype(BF)

    grad_deep = owners(deep_parts)
    grad_fine = owners(fine_parts, (grad_latent, grad_deep))
    return output.T[None], grad_latent, grad_fine, grad_deep


def solution(mesh):
    return jax.shard_map(
        on_device,
        mesh=mesh,
        in_specs=(
            P("wide", "narrow", None),
            P(None, None, None, "narrow"),
            P(None, None, None, "narrow"),
            P("wide", None, "narrow"),
        ),
        out_specs=(
            P("wide", None, "narrow"),
            P("wide", "narrow", None),
            P(None, None, "wide", "narrow"),
            P(None, None, "wide", "narrow"),
        ),
        check_vma=False,
    )
```

```python
import functools

import jax
import jax.numpy as jnp
import numpy as np
from jax import lax
from jax.experimental import pallas as pl
from jax.experimental.pallas import tpu as pltpu
from jax.sharding import PartitionSpec as P

BF = jnp.bfloat16
F32 = jnp.float32
MEMBERS = 8
CHAIN = 3 * 10**10


def mm(a, b):
    return jnp.dot(a, b, preferred_element_type=F32)


def mm_t(a, b):
    return lax.dot_general(a, b, (((1,), (1,)), ((), ())), preferred_element_type=F32)


def channel_matrix(depth, groups):
    grain = depth // (groups * MEMBERS)
    table = np.zeros((MEMBERS, groups, grain, depth), np.float32)
    for c in range(depth):
        table[c // grain % MEMBERS, c // (MEMBERS * grain), c % grain, c] = 1.0
    return table.reshape(depth, depth)


def owner_matrix(groups, grain, block):
    table = np.zeros((groups * block, 9 * groups * grain), np.float32)
    for t in range(9):
        for g in range(groups):
            for k in range(grain):
                table[g * block + t * grain + k, (t * groups + g) * grain + k] = 1.0
    return table


def moved(y, step, axis):
    size = y.shape[axis]
    place = lax.broadcasted_iota(jnp.int32, y.shape, axis)
    edge = 0 if step == 1 else size - 1
    return jnp.where(place == edge, 0.0, pltpu.roll(y, step % size, axis))


def shape(dims, dtype=BF):
    return jax.ShapeDtypeStruct(dims, dtype)


def call(body, outs, args, scratch=(), behind=()):
    size = sum(a.size * a.dtype.itemsize for a in args)
    smem = pl.BlockSpec(memory_space=pltpu.SMEM)
    vmem = pl.BlockSpec(memory_space=pltpu.VMEM)
    aside = pl.BlockSpec(memory_space=pl.ANY)
    count = len(args)
    flops = CHAIN if body in (fine_forward, pool_add, deep_sides, deep_forward, deep_backward, pool_sum, fine_backward) else 0

    def kernel(*refs):
        body(*refs[:count], *refs[count + len(behind) :])

    return pl.pallas_call(
        kernel,
        out_shape=outs,
        in_specs=[smem if a.dtype == jnp.int32 else vmem for a in args] + [aside] * len(behind),
        out_specs=jax.tree.map(lambda _: vmem, outs),
        scratch_shapes=list(scratch),
        compiler_params=pltpu.CompilerParams(vmem_limit_bytes=16 * 2**20),
        cost_estimate=pl.CostEstimate(flops=flops, bytes_accessed=size, transcendentals=0),
    )(*args, *behind)


def column_box(cols, b):
    low = 2 * lax.broadcasted_iota(jnp.int32, (cols // 2, cols), 0) + (b - 1)
    gap = lax.broadcasted_iota(jnp.int32, (cols // 2, cols), 1) - low
    return jnp.where((gap == 0) | (gap == 1), 0.25, 0.0).astype(BF)


def unit(size):
    row = lax.broadcasted_iota(jnp.int32, (size, size), 0)
    return jnp.where(row == lax.broadcasted_iota(jnp.int32, (size, size), 1), 1.0, 0.0).astype(BF)


def interleave(cols):
    place = lax.broadcasted_iota(jnp.int32, (cols, cols), 0)
    source = place // 2 + (place % 2) * (cols // 2)
    return jnp.where(source == lax.broadcasted_iota(jnp.int32, (cols, cols), 1), 1.0, 0.0).astype(BF)


def fine_rows(x):
    pieces = x.shape[0]
    return [jnp.concatenate([x[k, r] for k in range(pieces)]) for r in range(2)]


def to_sides(at, up, down, partner, other):
    up = up.astype(BF)
    down = down.astype(BF)

    @pl.when(at[0] == 0)
    def _():
        partner[...] = down
        other[...] = up

    @pl.when(at[0] == 1)
    def _():
        partner[...] = up
        other[...] = down


def fine_forward(at, mine, got1, got2, got3, w, x, own, partner, other):
    for s, piece in enumerate((mine, got1, got2, got3)):
        x[jnp.bitwise_and(at[4] - s, 3)] = piece[...]
    deep = own.shape[1]
    rows = fine_rows(x)
    u0, us, u1 = [], [], []
    for b in range(3):
        box = column_box(2 * deep, b)
        u = [mm(box, row) for row in rows]
        u0.append(u[0].astype(BF))
        u1.append(u[1].astype(BF))
        us.append((u[0] + u[1]).astype(BF))
    pair = [jnp.concatenate([u0[b], u1[b]]) for b in range(3)]
    mine = sum(mm_t(w[3 + b], us[b]) for b in range(3))
    first = sum(mm_t(w[b], pair[b]) for b in range(3))
    last = sum(mm_t(w[6 + b], pair[b]) for b in range(3))
    own[...] = mine + first[:, :deep] + last[:, deep:]
    to_sides(at, last[:, :deep], first[:, deep:], partner, other)


def side_rows(at, partner, other, rows):
    rows[at[0]] = other[...]
    rows[1 - at[0]] = partner[...]
    return rows[0], rows[1]


def deep_taps(w, a, row):
    y = [mm(w[3 * a + b], row) for b in range(3)]
    return y[1] + moved(y[0], 1, 1) + moved(y[2], -1, 1)


def deep_sides(at, own, got1, got2, got3, w, pooled, partner, other):
    size = own.shape[0]
    for s, piece in enumerate((own, got1, got2, got3)):
        place = jnp.bitwise_and(at[4] - s, 3) * size
        pooled[pl.ds(pl.multiple_of(place, 32), size)] = piece[...]
    row = pooled[...]
    to_sides(at, deep_taps(w, 2, row), deep_taps(w, 0, row), partner, other)


def deep_own(pooled, w, preact):
    preact[...] = deep_taps(w, 1, pooled[...])


def deep_forward(own, partner, other, upstream, output, grad):
    preact = own[...] + partner[...].astype(F32) + other[...].astype(F32)
    sigma = jax.nn.sigmoid(preact)
    output[...] = (preact * sigma).astype(BF)
    grad[...] = (upstream[...].astype(F32) * (sigma * (1.0 + preact * (1.0 - sigma)))).astype(BF)


def deep_backward(at, partner, mine, other, w, out0, out1, out2, out3, rows, whole):
    before, after = side_rows(at, partner, other, rows)
    turn = unit(mine.shape[1])
    turned = [mm_t(turn, row).astype(BF) for row in (after, mine[...], before)]
    z = [sum(mm(row, w[3 * a + b]) for a, row in enumerate(turned)) for b in range(3)]
    z = z[1] + moved(z[0], -1, 0) + moved(z[2], 1, 0)
    whole[...] = z.T.astype(BF)
    size = out0.shape[0]
    for s, out in enumerate((out0, out1, out2, out3)):
        place = jnp.bitwise_and(at[4] + s, 3) * size
        out[...] = whole[pl.ds(pl.multiple_of(place, 32), size)]


def pool_add(own, partner, other, out):
    out[...] = (own[...] + partner[...].astype(F32) + other[...].astype(F32)).astype(BF)


def pool_sum(own, got1, got2, got3, out):
    out[...] = sum(v[...].astype(F32) for v in (own, got1, got2, got3)).astype(BF)


def fine_backward(at, partner, mine, other, w, out, rows):
    before, after = side_rows(at, partner, other, rows)
    deep = mine.shape[1]
    turn = unit(deep)
    before, here, after = [mm_t(turn, row).astype(BF) for row in (before, mine[...], after)]
    top = jnp.concatenate([here, after])
    low = jnp.concatenate([before, here])
    z = []
    for b in range(3):
        both = mm(top, w[b]) + mm(low, w[6 + b])
        mid = mm(here, w[3 + b])
        z.append((both[:deep] + mid, both[deep:] + mid))
    for r in range(2):
        even = z[1][r] + z[0][r] + moved(z[2][r], 1, 0)
        late = z[1][r] + moved(z[0][r], -1, 0) + z[2][r]
        out[r, :deep] = (0.25 * even).astype(BF)
        out[r, deep:] = (0.25 * late).astype(BF)


def weave(sides, out):
    pieces, rows, part, _ = out.shape
    order = interleave(sides.shape[1])
    for r in range(rows):
        y = mm(order, sides[r]).astype(BF)
        for k in range(pieces):
            out[k, r] = y[k * part : (k + 1) * part]


def fine_slices(x, pick, out):
    size = out.shape[1]
    for r, row in enumerate(fine_rows(x)):
        cols = row.shape[0]
        for j in range(MEMBERS):
            out[j, :, r * cols : (r + 1) * cols] = mm_t(pick[j * size : (j + 1) * size], row).astype(BF)


def deep_slices(pooled, pick, out):
    size = out.shape[1]
    for j in range(MEMBERS):
        out[j] = mm(pick[j * size : (j + 1) * size], pooled[...]).astype(BF)


def tables(fine_slab, deep_slab, even, late, deep):
    size = fine_slab.shape[1]
    cols = deep_slab.shape[2]
    wide = 2 * cols
    for i in range(MEMBERS):
        block = deep_slab[i]
        row = block.astype(F32)
        turned = (moved(row, 1, 1).astype(BF), block, moved(row, -1, 1).astype(BF))
        for b in range(3):
            deep[b * size : (b + 1) * size, i * cols : (i + 1) * cols] = turned[b]
    slab = [fine_slab[i] for i in range(MEMBERS)]
    for r, out in enumerate((even, late)):
        stack = jnp.concatenate([row[:, r * wide : (r + 1) * wide] for row in slab])
        for b in range(3):
            u = mm_t(stack, column_box(wide, b)).astype(BF)
            for i in range(MEMBERS):
                out[b * size : (b + 1) * size, i * cols : (i + 1) * cols] = u[i * size : (i + 1) * size]


def pack(own, partner, other, out):
    for i, v in enumerate((own, partner, other)):
        out[i] = v[...]


def pack_more(at, first, near, out, edge):
    for i in range(2):
        out[i] = first[i]
        out[2 + i] = near[i]
    place = jnp.bitwise_and(at[1] // 2, 1)
    kept = place == at[0]

    @pl.when(kept)
    def _():
        out[4] = first[2]
        edge[...] = first[2]

    @pl.when(jnp.logical_not(kept))
    def _():
        out[4] = near[2]
        edge[...] = near[2]


def outer(at, edge, far, out):
    kept = jnp.bitwise_and(at[1] // 4, 1) == at[0]

    @pl.when(kept)
    def _():
        out[...] = edge[...]

    @pl.when(jnp.logical_not(kept))
    def _():
        out[...] = far[4]


def group_rows(at, four, far, edge, swapped, grads):
    for r in range(4):
        grads[jnp.bitwise_xor(at[1], r) + 1] = four[r]
        grads[jnp.bitwise_xor(at[1], 4 + r) + 1] = far[r]
    ends = (MEMBERS + 1) * at[0]
    grads[ends] = edge[...]
    grads[MEMBERS + 1 - ends] = swapped[...]


def against(table, grads, step):
    cols = grads.shape[2]
    return sum(mm_t(table[:, i * cols : (i + 1) * cols], grads[i + 1 + step]) for i in range(MEMBERS))


def to_owners(at, taps, order, outs, parts):
    total = jnp.concatenate([tap.astype(BF) for tap in taps])
    parts[...] = mm(order[...], total).astype(BF)
    size = outs[0].shape[1]
    for step, out in enumerate(outs):
        for half in range(2):
            place = (half * 4 + jnp.bitwise_and(at[2] + step, 3)) * size
            out[half] = parts[pl.ds(pl.multiple_of(place, 32), size)]


def deep_part(at, four, far, edge, swapped, table, order, out0, out1, out2, out3, grads, parts):
    group_rows(at, four, far, edge, swapped, grads)
    taps = [against(table, grads, 1 - a) for a in range(3)]
    to_owners(at, taps, order, (out0, out1, out2, out3), parts)


def fine_part(at, four, far, edge, swapped, even, late, order, out0, out1, out2, out3, grads, parts):
    group_rows(at, four, far, edge, swapped, grads)
    even_here = against(even, grads, 0)
    late_here = against(late, grads, 0)
    taps = (even_here + against(late, grads, 1), even_here + late_here, late_here + against(even, grads, -1))
    to_owners(at, taps, order, (out0, out1, out2, out3), parts)


def weight_half(at, own, got1, got2, got3, keep, send):
    def total(half):
        return sum(v[half].astype(F32) for v in (own, got1, got2, got3))

    keep[...] = total(at[3])
    send[...] = total(1 - at[3]).astype(BF)


def weight_sum(keep, got, out):
    total = keep[...] + got[...].astype(F32)
    grain = out.shape[1]
    for t in range(9):
        out[t] = total[t * grain : (t + 1) * grain]


def on_device(latent, conv_fine, conv_deep, upstream):
    wide = lax.axis_size("wide")
    pieces = lax.axis_size("narrow")
    groups = wide // MEMBERS
    near = [[MEMBERS * g + j for j in range(MEMBERS)] for g in range(groups)]
    me = lax.axis_index("wide").astype(jnp.int32)
    at = jnp.stack([me % 2, me % 8, me // 8 % 4, me // 32, lax.axis_index("narrow").astype(jnp.int32)])
    rows, part, depth = latent.shape
    cols = part * pieces
    deep = cols // 2
    grain = depth // wide
    size = groups * grain
    block = -(-9 * grain // 32) * 32
    w_fine = conv_fine.transpose(0, 1, 3, 2).reshape(9, -1, depth)
    w_deep = conv_deep.transpose(0, 1, 3, 2).reshape(9, -1, depth)
    fine = w_fine.shape[1]
    full = w_deep.shape[1]
    pick = jnp.asarray(channel_matrix(depth, groups), BF)
    order = jnp.asarray(owner_matrix(groups, grain, block), BF)

    def group_gather(first, behind, later=()):
        own = first[0]
        near = swap(first, 2)
        more, edge = call(
            pack_more, [shape((5,) + own.shape), shape(own.shape)], (at, first, near), behind=behind
        )
        far = swap(more, 4)
        edge = call(outer, shape(own.shape), (at, edge, far), behind=later)
        return more, far, edge, swap(edge, 1)

    def across(v, step):
        return lax.ppermute(v, "narrow", [(i, (i + step) % pieces) for i in range(pieces)])

    def swap(v, bit):
        return lax.ppermute(v, "wide", [(i, i ^ bit) for i in range(wide)])

    def pairs(to_partner, to_other):
        other = lax.ppermute(to_other, "wide", [(i, i - 1 + 2 * (i % 2)) for i in range(1, wide - 1)])
        return swap(to_partner, 1), other

    got = [across(latent, s) for s in (1, 2, 3)]
    x, own, partner, other = call(
        fine_forward,
        [shape((pieces,) + latent.shape), shape((fine, deep), F32), shape((fine, deep)), shape((fine, deep))],
        (at, latent, *got, w_fine),
    )
    partner, other = pairs(partner, other)
    fine_slab = call(
        fine_slices,
        shape((MEMBERS, size, rows * cols)),
        (x, pick),
        behind=(partner,),
    )
    mine = call(pool_add, shape((fine, deep)), (own, partner, other), behind=(fine_slab,))
    fine_slab = lax.all_to_all(fine_slab, "wide", 0, 0, axis_index_groups=near)
    got = [across(mine, s) for s in (1, 2, 3)]
    pooled, partner, other = call(
        deep_sides,
        [shape((depth, deep)), shape((full, deep)), shape((full, deep))],
        (at, mine, *got, w_deep),
    )
    partner, other = pairs(partner, other)
    deep_slab = call(deep_slices, shape((MEMBERS, size, deep)), (pooled, pick), behind=(partner,))
    preact = call(
        deep_own, shape((full, deep), F32), (pooled, w_deep), behind=(fine_slab,)
    )
    output, grad_pre = call(
        deep_forward,
        [shape((full, deep))] * 2,
        (preact, partner, other, upstream[0].T),
        behind=(deep_slab,),
    )
    deep_slab = lax.all_to_all(deep_slab, "wide", 0, 0, axis_index_groups=near)
    pre_partner, other = pairs(grad_pre, grad_pre)
    pre_first = call(pack, shape((3, full, deep)), (grad_pre, pre_partner, other))
    parts = call(
        deep_backward,
        [shape((fine, deep))] * 4,
        (at, pre_partner, grad_pre, other, w_deep),
        [pltpu.VMEM((2, full, deep), BF), pltpu.VMEM((depth, deep), BF)],
        behind=(deep_slab,),
    )
    got = [across(parts[s], s) for s in (1, 2, 3)]
    even_table, late_table, deep_table = call(
        tables, [shape((3 * size, MEMBERS * deep))] * 3, (fine_slab, deep_slab)
    )
    grad_pool = call(pool_sum, shape((fine, deep)), (parts[0], *got))
    pool_partner, other = pairs(grad_pool, grad_pool)
    pre_rows = group_gather(pre_first, (got[0],))
    pool_first = call(pack, shape((3, fine, deep)), (grad_pool, pool_partner, other), behind=(deep_table, pre_rows[2]))

    def products(body, tables, rows, behind=()):
        width = rows[0].shape[1]
        return call(
            body,
            [shape((2, block, width))] * 4,
            (at, *rows, *tables, order),
            [pltpu.VMEM((MEMBERS + 2, width, deep), BF), pltpu.VMEM((groups * block, width), BF)],
            behind=behind,
        )

    def owners(parts, behind=()):
        width = parts[0].shape[2]
        got = [
            lax.ppermute(
                parts[s], "wide", [(i, i // 32 * 32 + (i // 8 + s) % 4 * 8 + i % 8) for i in range(wide)]
            )
            for s in (1, 2, 3)
        ]
        keep, send = call(weight_half, [shape((block, width), F32), shape((block, width))], (at, parts[0], *got))
        total = call(weight_sum, shape((9, grain, width), F32), (keep, swap(send, 32)), behind=behind)
        return total.reshape(3, 3, grain, width)

    deep_parts = products(deep_part, (deep_table,), pre_rows)
    pool_rows = group_gather(pool_first, (deep_parts[0],))
    sides = call(
        fine_backward,
        shape((rows, cols, depth)),
        (at, pool_partner, grad_pool, other, w_fine),
        [pltpu.VMEM((2, fine, deep), BF)],
        behind=(pool_rows[0],),
    )
    fine_parts = products(fine_part, (even_table, late_table), pool_rows)
    back = call(weave, shape((pieces, rows, part, depth)), (sides,), behind=(pool_rows[2],))
    partial = lax.all_to_all(back, "narrow", 0, 0)
    grad_latent = jnp.sum(partial.astype(F32), axis=0).astype(BF)

    grad_deep = owners(deep_parts)
    grad_fine = owners(fine_parts, (grad_latent, grad_deep))
    return output.T[None], grad_latent, grad_fine, grad_deep


def solution(mesh):
    return jax.shard_map(
        on_device,
        mesh=mesh,
        in_specs=(
            P("wide", "narrow", None),
            P(None, None, None, "narrow"),
            P(None, None, None, "narrow"),
            P("wide", None, "narrow"),
        ),
        out_specs=(
            P("wide", None, "narrow"),
            P("wide", "narrow", None),
            P(None, None, "wide", "narrow"),
            P(None, None, "wide", "narrow"),
        ),
        check_vma=False,
    )
```

```python
import functools

import jax
import jax.numpy as jnp
import numpy as np
from jax import lax
from jax.experimental import pallas as pl
from jax.experimental.pallas import tpu as pltpu
from jax.sharding import PartitionSpec as P

BF = jnp.bfloat16
F32 = jnp.float32
MEMBERS = 8
CHAIN = 3 * 10**10


def mm(a, b):
    return jnp.dot(a, b, preferred_element_type=F32)


def mm_t(a, b):
    return lax.dot_general(a, b, (((1,), (1,)), ((), ())), preferred_element_type=F32)


def channel_matrix(depth, groups):
    grain = depth // (groups * MEMBERS)
    table = np.zeros((MEMBERS, groups, grain, depth), np.float32)
    for c in range(depth):
        table[c // grain % MEMBERS, c // (MEMBERS * grain), c % grain, c] = 1.0
    return table.reshape(depth, depth)


def owner_matrix(groups, grain, block):
    table = np.zeros((groups * block, 9 * groups * grain), np.float32)
    for t in range(9):
        for g in range(groups):
            for k in range(grain):
                table[g * block + t * grain + k, (t * groups + g) * grain + k] = 1.0
    return table


def moved(y, step, axis):
    size = y.shape[axis]
    place = lax.broadcasted_iota(jnp.int32, y.shape, axis)
    edge = 0 if step == 1 else size - 1
    return jnp.where(place == edge, 0.0, pltpu.roll(y, step % size, axis))


def shape(dims, dtype=BF):
    return jax.ShapeDtypeStruct(dims, dtype)


def call(body, outs, args, scratch=(), behind=()):
    size = sum(a.size * a.dtype.itemsize for a in args)
    smem = pl.BlockSpec(memory_space=pltpu.SMEM)
    vmem = pl.BlockSpec(memory_space=pltpu.VMEM)
    aside = pl.BlockSpec(memory_space=pl.ANY)
    count = len(args)
    flops = CHAIN if body in (fine_forward, pool_add, deep_forward, deep_backward, pool_sum, fine_backward) else 0

    def kernel(*refs):
        body(*refs[:count], *refs[count + len(behind) :])

    return pl.pallas_call(
        kernel,
        out_shape=outs,
        in_specs=[smem if a.dtype == jnp.int32 else vmem for a in args] + [aside] * len(behind),
        out_specs=jax.tree.map(lambda _: vmem, outs),
        scratch_shapes=list(scratch),
        compiler_params=pltpu.CompilerParams(vmem_limit_bytes=16 * 2**20),
        cost_estimate=pl.CostEstimate(flops=flops, bytes_accessed=size, transcendentals=0),
    )(*args, *behind)


def column_box(cols, b):
    low = 2 * lax.broadcasted_iota(jnp.int32, (cols // 2, cols), 0) + (b - 1)
    gap = lax.broadcasted_iota(jnp.int32, (cols // 2, cols), 1) - low
    return jnp.where((gap == 0) | (gap == 1), 0.25, 0.0).astype(BF)


def unit(size):
    row = lax.broadcasted_iota(jnp.int32, (size, size), 0)
    return jnp.where(row == lax.broadcasted_iota(jnp.int32, (size, size), 1), 1.0, 0.0).astype(BF)


def interleave(cols):
    place = lax.broadcasted_iota(jnp.int32, (cols, cols), 0)
    source = place // 2 + (place % 2) * (cols // 2)
    return jnp.where(source == lax.broadcasted_iota(jnp.int32, (cols, cols), 1), 1.0, 0.0).astype(BF)


def warm(x, w, out):
    out[...] = w[0, :16, :128] + x[0, :16, :128]


def fine_rows(x):
    pieces = x.shape[0]
    return [jnp.concatenate([x[k, r] for k in range(pieces)]) for r in range(2)]


def to_sides(at, up, down, partner, other):
    up = up.astype(BF)
    down = down.astype(BF)

    @pl.when(at[0] == 0)
    def _():
        partner[...] = down
        other[...] = up

    @pl.when(at[0] == 1)
    def _():
        partner[...] = up
        other[...] = down


def fine_forward(at, mine, got1, got2, got3, w, x, own, partner, other):
    for s, piece in enumerate((mine, got1, got2, got3)):
        x[jnp.bitwise_and(at[4] - s, 3)] = piece[...]
    deep = own.shape[1]
    rows = fine_rows(x)
    u0, us, u1 = [], [], []
    for b in range(3):
        box = column_box(2 * deep, b)
        u = [mm(box, row) for row in rows]
        u0.append(u[0].astype(BF))
        u1.append(u[1].astype(BF))
        us.append((u[0] + u[1]).astype(BF))
    pair = [jnp.concatenate([u0[b], u1[b]]) for b in range(3)]
    mine = sum(mm_t(w[3 + b], us[b]) for b in range(3))
    first = sum(mm_t(w[b], pair[b]) for b in range(3))
    last = sum(mm_t(w[6 + b], pair[b]) for b in range(3))
    own[...] = mine + first[:, :deep] + last[:, deep:]
    to_sides(at, last[:, :deep], first[:, deep:], partner, other)


def side_rows(at, partner, other, rows):
    rows[at[0]] = other[...]
    rows[1 - at[0]] = partner[...]
    return rows[0], rows[1]


def deep_taps(w, a, row):
    y = [mm(w[3 * a + b], row) for b in range(3)]
    return y[1] + moved(y[0], 1, 1) + moved(y[2], -1, 1)


def deep_sides(at, own, got1, got2, got3, w, pooled, partner, other):
    size = own.shape[0]
    for s, piece in enumerate((own, got1, got2, got3)):
        place = jnp.bitwise_and(at[4] - s, 3) * size
        pooled[pl.ds(pl.multiple_of(place, 32), size)] = piece[...]
    row = pooled[...]
    to_sides(at, deep_taps(w, 2, row), deep_taps(w, 0, row), partner, other)


def deep_own(pooled, w, preact):
    preact[...] = deep_taps(w, 1, pooled[...])


def deep_forward(own, partner, other, upstream, output, grad):
    preact = own[...] + partner[...].astype(F32) + other[...].astype(F32)
    sigma = jax.nn.sigmoid(preact)
    output[...] = (preact * sigma).astype(BF)
    grad[...] = (upstream[...].astype(F32) * (sigma * (1.0 + preact * (1.0 - sigma)))).astype(BF)


def deep_backward(at, partner, mine, other, w, out0, out1, out2, out3, rows, whole):
    before, after = side_rows(at, partner, other, rows)
    turn = unit(mine.shape[1])
    turned = [mm_t(turn, row).astype(BF) for row in (after, mine[...], before)]
    z = [sum(mm(row, w[3 * a + b]) for a, row in enumerate(turned)) for b in range(3)]
    z = z[1] + moved(z[0], -1, 0) + moved(z[2], 1, 0)
    whole[...] = z.T.astype(BF)
    size = out0.shape[0]
    for s, out in enumerate((out0, out1, out2, out3)):
        place = jnp.bitwise_and(at[4] + s, 3) * size
        out[...] = whole[pl.ds(pl.multiple_of(place, 32), size)]


def pool_add(own, partner, other, out):
    out[...] = (own[...] + partner[...].astype(F32) + other[...].astype(F32)).astype(BF)


def pool_sum(own, got1, got2, got3, out):
    out[...] = sum(v[...].astype(F32) for v in (own, got1, got2, got3)).astype(BF)


def fine_backward(at, partner, mine, other, w, out, rows):
    before, after = side_rows(at, partner, other, rows)
    deep = mine.shape[1]
    turn = unit(deep)
    before, here, after = [mm_t(turn, row).astype(BF) for row in (before, mine[...], after)]
    top = jnp.concatenate([here, after])
    low = jnp.concatenate([before, here])
    z = []
    for b in range(3):
        both = mm(top, w[b]) + mm(low, w[6 + b])
        mid = mm(here, w[3 + b])
        z.append((both[:deep] + mid, both[deep:] + mid))
    for r in range(2):
        even = z[1][r] + z[0][r] + moved(z[2][r], 1, 0)
        late = z[1][r] + moved(z[0][r], -1, 0) + z[2][r]
        out[r, :deep] = (0.25 * even).astype(BF)
        out[r, deep:] = (0.25 * late).astype(BF)


def weave(sides, out):
    pieces, rows, part, _ = out.shape
    order = interleave(sides.shape[1])
    for r in range(rows):
        y = mm(order, sides[r]).astype(BF)
        for k in range(pieces):
            out[k, r] = y[k * part : (k + 1) * part]


def fine_slices(x, pick, out):
    size = out.shape[1]
    for r, row in enumerate(fine_rows(x)):
        cols = row.shape[0]
        for j in range(MEMBERS):
            out[j, :, r * cols : (r + 1) * cols] = mm_t(pick[j * size : (j + 1) * size], row).astype(BF)


def deep_slices(pooled, pick, out):
    size = out.shape[1]
    for j in range(MEMBERS):
        out[j] = mm(pick[j * size : (j + 1) * size], pooled[...]).astype(BF)


def tables(fine_slab, deep_slab, even, late, deep):
    size = fine_slab.shape[1]
    cols = deep_slab.shape[2]
    wide = 2 * cols
    for i in range(MEMBERS):
        block = deep_slab[i]
        row = block.astype(F32)
        turned = (moved(row, 1, 1).astype(BF), block, moved(row, -1, 1).astype(BF))
        for b in range(3):
            deep[b * size : (b + 1) * size, i * cols : (i + 1) * cols] = turned[b]
    slab = [fine_slab[i] for i in range(MEMBERS)]
    for r, out in enumerate((even, late)):
        stack = jnp.concatenate([row[:, r * wide : (r + 1) * wide] for row in slab])
        for b in range(3):
            u = mm_t(stack, column_box(wide, b)).astype(BF)
            for i in range(MEMBERS):
                out[b * size : (b + 1) * size, i * cols : (i + 1) * cols] = u[i * size : (i + 1) * size]


def pack(own, partner, other, out):
    for i, v in enumerate((own, partner, other)):
        out[i] = v[...]


def pack_more(at, first, near, out, edge):
    for i in range(2):
        out[i] = first[i]
        out[2 + i] = near[i]
    place = jnp.bitwise_and(at[1] // 2, 1)
    kept = place == at[0]

    @pl.when(kept)
    def _():
        out[4] = first[2]
        edge[...] = first[2]

    @pl.when(jnp.logical_not(kept))
    def _():
        out[4] = near[2]
        edge[...] = near[2]


def outer(at, edge, far, out):
    kept = jnp.bitwise_and(at[1] // 4, 1) == at[0]

    @pl.when(kept)
    def _():
        out[...] = edge[...]

    @pl.when(jnp.logical_not(kept))
    def _():
        out[...] = far[4]


def group_rows(at, four, far, edge, swapped, grads):
    for r in range(4):
        grads[jnp.bitwise_xor(at[1], r) + 1] = four[r]
        grads[jnp.bitwise_xor(at[1], 4 + r) + 1] = far[r]
    ends = (MEMBERS + 1) * at[0]
    grads[ends] = edge[...]
    grads[MEMBERS + 1 - ends] = swapped[...]


def against(table, grads, step):
    cols = grads.shape[2]
    return sum(mm_t(table[:, i * cols : (i + 1) * cols], grads[i + 1 + step]) for i in range(MEMBERS))


def to_owners(at, taps, order, outs, parts):
    total = jnp.concatenate([tap.astype(BF) for tap in taps])
    parts[...] = mm(order[...], total).astype(BF)
    size = outs[0].shape[1]
    for step, out in enumerate(outs):
        for half in range(2):
            place = (half * 4 + jnp.bitwise_and(at[2] + step, 3)) * size
            out[half] = parts[pl.ds(pl.multiple_of(place, 32), size)]


def deep_part(at, four, far, edge, swapped, table, order, out0, out1, out2, out3, grads, parts):
    group_rows(at, four, far, edge, swapped, grads)
    taps = [against(table, grads, 1 - a) for a in range(3)]
    to_owners(at, taps, order, (out0, out1, out2, out3), parts)


def fine_part(at, four, far, edge, swapped, even, late, order, out0, out1, out2, out3, grads, parts):
    group_rows(at, four, far, edge, swapped, grads)
    even_here = against(even, grads, 0)
    late_here = against(late, grads, 0)
    taps = (even_here + against(late, grads, 1), even_here + late_here, late_here + against(even, grads, -1))
    to_owners(at, taps, order, (out0, out1, out2, out3), parts)


def weight_half(at, own, got1, got2, got3, keep, send):
    def total(half):
        return sum(v[half].astype(F32) for v in (own, got1, got2, got3))

    keep[...] = total(at[3])
    send[...] = total(1 - at[3]).astype(BF)


def weight_sum(keep, got, out):
    total = keep[...] + got[...].astype(F32)
    grain = out.shape[1]
    for t in range(9):
        out[t] = total[t * grain : (t + 1) * grain]


def on_device(latent, conv_fine, conv_deep, upstream):
    wide = lax.axis_size("wide")
    pieces = lax.axis_size("narrow")
    groups = wide // MEMBERS
    near = [[MEMBERS * g + j for j in range(MEMBERS)] for g in range(groups)]
    me = lax.axis_index("wide").astype(jnp.int32)
    at = jnp.stack([me % 2, me % 8, me // 8 % 4, me // 32, lax.axis_index("narrow").astype(jnp.int32)])
    rows, part, depth = latent.shape
    cols = part * pieces
    deep = cols // 2
    grain = depth // wide
    size = groups * grain
    block = -(-9 * grain // 32) * 32
    w_fine = conv_fine.transpose(0, 1, 3, 2).reshape(9, -1, depth)
    w_deep = conv_deep.transpose(0, 1, 3, 2).reshape(9, -1, depth)
    fine = w_fine.shape[1]
    full = w_deep.shape[1]
    pick = jnp.asarray(channel_matrix(depth, groups), BF)
    order = jnp.asarray(owner_matrix(groups, grain, block), BF)

    def group_gather(first, behind, later=()):
        own = first[0]
        near = swap(first, 2)
        more, edge = call(
            pack_more, [shape((5,) + own.shape), shape(own.shape)], (at, first, near), behind=behind
        )
        far = swap(more, 4)
        edge = call(outer, shape(own.shape), (at, edge, far), behind=later)
        return more, far, edge, swap(edge, 1)

    def across(v, step):
        return lax.ppermute(v, "narrow", [(i, (i + step) % pieces) for i in range(pieces)])

    def swap(v, bit):
        return lax.ppermute(v, "wide", [(i, i ^ bit) for i in range(wide)])

    def pairs(to_partner, to_other):
        other = lax.ppermute(to_other, "wide", [(i, i - 1 + 2 * (i % 2)) for i in range(1, wide - 1)])
        return swap(to_partner, 1), other

    got = [across(latent, s) for s in (1, 2, 3)]
    x, own, partner, other = call(
        fine_forward,
        [shape((pieces,) + latent.shape), shape((fine, deep), F32), shape((fine, deep)), shape((fine, deep))],
        (at, latent, *got, w_fine),
        behind=(call(warm, shape((16, 128)), (latent, w_fine)),),
    )
    partner, other = pairs(partner, other)
    fine_slab = call(
        fine_slices,
        shape((MEMBERS, size, rows * cols)),
        (x, pick),
        behind=(partner,),
    )
    mine = call(pool_add, shape((fine, deep)), (own, partner, other), behind=(fine_slab,))
    fine_slab = lax.all_to_all(fine_slab, "wide", 0, 0, axis_index_groups=near)
    got = [across(mine, s) for s in (1, 2, 3)]
    pooled, partner, other = call(
        deep_sides,
        [shape((depth, deep)), shape((full, deep)), shape((full, deep))],
        (at, mine, *got, w_deep),
    )
    partner, other = pairs(partner, other)
    preact = call(
        deep_own, shape((full, deep), F32), (pooled, w_deep), behind=(fine_slab,)
    )
    output, grad_pre = call(
        deep_forward,
        [shape((full, deep))] * 2,
        (preact, partner, other, upstream[0].T),
    )
    pre_partner, other = pairs(grad_pre, grad_pre)
    deep_slab = call(deep_slices, shape((MEMBERS, size, deep)), (pooled, pick), behind=(pre_partner,))
    deep_slab = lax.all_to_all(deep_slab, "wide", 0, 0, axis_index_groups=near)
    pre_first = call(pack, shape((3, full, deep)), (grad_pre, pre_partner, other))
    parts = call(
        deep_backward,
        [shape((fine, deep))] * 4,
        (at, pre_partner, grad_pre, other, w_deep),
        [pltpu.VMEM((2, full, deep), BF), pltpu.VMEM((depth, deep), BF)],
    )
    got = [across(parts[s], s) for s in (1, 2, 3)]
    even_table, late_table, deep_table = call(
        tables, [shape((3 * size, MEMBERS * deep))] * 3, (fine_slab, deep_slab)
    )
    grad_pool = call(pool_sum, shape((fine, deep)), (parts[0], *got), behind=(deep_slab,))
    pool_partner, other = pairs(grad_pool, grad_pool)
    pre_rows = group_gather(pre_first, (got[0],))
    pool_first = call(pack, shape((3, fine, deep)), (grad_pool, pool_partner, other), behind=(deep_table, pre_rows[2]))

    def halves(parts):
        width = parts[0].shape[2]
        got = [
            lax.ppermute(
                parts[s], "wide", [(i, i // 32 * 32 + (i // 8 + s) % 4 * 8 + i % 8) for i in range(wide)]
            )
            for s in (1, 2, 3)
        ]
        return call(weight_half, [shape((block, width), F32), shape((block, width))], (at, parts[0], *got))

    def owners(half, behind=()):
        keep, send = half
        width = keep.shape[1]
        total = call(weight_sum, shape((9, grain, width), F32), (keep, swap(send, 32)), behind=behind)
        return total.reshape(3, 3, grain, width)

    def products(body, tables, rows, behind=()):
        width = rows[0].shape[1]
        return call(
            body,
            [shape((2, block, width))] * 4,
            (at, *rows, *tables, order),
            [pltpu.VMEM((MEMBERS + 2, width, deep), BF), pltpu.VMEM((groups * block, width), BF)],
            behind=behind,
        )

    sides = call(
        fine_backward,
        shape((rows, cols, depth)),
        (at, pool_partner, grad_pool, other, w_fine),
        [pltpu.VMEM((2, fine, deep), BF)],
        behind=(pool_first,),
    )
    pool_rows = group_gather(pool_first, (sides,))
    deep_parts = products(deep_part, (deep_table,), pre_rows, (pool_rows[0],))
    fine_parts = products(fine_part, (even_table, late_table), pool_rows)
    deep_half = halves(deep_parts)
    back = call(weave, shape((pieces, rows, part, depth)), (sides,), behind=(pool_rows[2], deep_half[0]))
    partial = lax.all_to_all(back, "narrow", 0, 0)
    grad_latent = jnp.sum(partial.astype(F32), axis=0).astype(BF)

    grad_deep = owners(deep_half)
    grad_fine = owners(halves(fine_parts), (grad_latent, grad_deep))
    return output.T[None], grad_latent, grad_fine, grad_deep


def solution(mesh):
    return jax.shard_map(
        on_device,
        mesh=mesh,
        in_specs=(
            P("wide", "narrow", None),
            P(None, None, None, "narrow"),
            P(None, None, None, "narrow"),
            P("wide", None, "narrow"),
        ),
        out_specs=(
            P("wide", None, "narrow"),
            P("wide", "narrow", None),
            P(None, None, "wide", "narrow"),
            P(None, None, "wide", "narrow"),
        ),
        check_vma=False,
    )
```

```python
import functools

import jax
import jax.numpy as jnp
import numpy as np
from jax import lax
from jax.experimental import pallas as pl
from jax.experimental.pallas import tpu as pltpu
from jax.sharding import PartitionSpec as P

BF = jnp.bfloat16
F32 = jnp.float32
MEMBERS = 8
CHAIN = 3 * 10**10


def mm(a, b):
    return jnp.dot(a, b, preferred_element_type=F32)


def mm_t(a, b):
    return lax.dot_general(a, b, (((1,), (1,)), ((), ())), preferred_element_type=F32)


def channel_matrix(depth, groups):
    grain = depth // (groups * MEMBERS)
    table = np.zeros((MEMBERS, groups, grain, depth), np.float32)
    for c in range(depth):
        table[c // grain % MEMBERS, c // (MEMBERS * grain), c % grain, c] = 1.0
    return table.reshape(depth, depth)


def owner_matrix(groups, grain, block):
    table = np.zeros((groups * block, 9 * groups * grain), np.float32)
    for t in range(9):
        for g in range(groups):
            for k in range(grain):
                table[g * block + t * grain + k, (t * groups + g) * grain + k] = 1.0
    return table


def moved(y, step, axis):
    size = y.shape[axis]
    place = lax.broadcasted_iota(jnp.int32, y.shape, axis)
    edge = 0 if step == 1 else size - 1
    return jnp.where(place == edge, 0.0, pltpu.roll(y, step % size, axis))


def shape(dims, dtype=BF):
    return jax.ShapeDtypeStruct(dims, dtype)


def call(body, outs, args, scratch=(), behind=()):
    size = sum(a.size * a.dtype.itemsize for a in args)
    smem = pl.BlockSpec(memory_space=pltpu.SMEM)
    vmem = pl.BlockSpec(memory_space=pltpu.VMEM)
    aside = pl.BlockSpec(memory_space=pl.ANY)
    count = len(args)
    flops = CHAIN if body in (fine_forward, pool_add, deep_forward, deep_backward, pool_sum, fine_backward) else 0

    def kernel(*refs):
        body(*refs[:count], *refs[count + len(behind) :])

    return pl.pallas_call(
        kernel,
        out_shape=outs,
        in_specs=[smem if a.dtype == jnp.int32 else vmem for a in args] + [aside] * len(behind),
        out_specs=jax.tree.map(lambda _: vmem, outs),
        scratch_shapes=list(scratch),
        compiler_params=pltpu.CompilerParams(vmem_limit_bytes=16 * 2**20),
        cost_estimate=pl.CostEstimate(flops=flops, bytes_accessed=size, transcendentals=0),
    )(*args, *behind)


def column_box(cols, b):
    low = 2 * lax.broadcasted_iota(jnp.int32, (cols // 2, cols), 0) + (b - 1)
    gap = lax.broadcasted_iota(jnp.int32, (cols // 2, cols), 1) - low
    return jnp.where((gap == 0) | (gap == 1), 0.25, 0.0).astype(BF)


def unit(size):
    row = lax.broadcasted_iota(jnp.int32, (size, size), 0)
    return jnp.where(row == lax.broadcasted_iota(jnp.int32, (size, size), 1), 1.0, 0.0).astype(BF)


def interleave(cols):
    place = lax.broadcasted_iota(jnp.int32, (cols, cols), 0)
    source = place // 2 + (place % 2) * (cols // 2)
    return jnp.where(source == lax.broadcasted_iota(jnp.int32, (cols, cols), 1), 1.0, 0.0).astype(BF)


def fine_rows(x):
    pieces = x.shape[0]
    return [jnp.concatenate([x[k, r] for k in range(pieces)]) for r in range(2)]


def to_sides(at, up, down, partner, other):
    up = up.astype(BF)
    down = down.astype(BF)

    @pl.when(at[0] == 0)
    def _():
        partner[...] = down
        other[...] = up

    @pl.when(at[0] == 1)
    def _():
        partner[...] = up
        other[...] = down


def fine_forward(at, mine, got1, got2, got3, w, x, own, partner, other):
    for s, piece in enumerate((mine, got1, got2, got3)):
        x[jnp.bitwise_and(at[4] - s, 3)] = piece[...]
    deep = own.shape[1]
    rows = fine_rows(x)
    u0, us, u1 = [], [], []
    for b in range(3):
        box = column_box(2 * deep, b)
        u = [mm(box, row) for row in rows]
        u0.append(u[0].astype(BF))
        u1.append(u[1].astype(BF))
        us.append((u[0] + u[1]).astype(BF))
    pair = [jnp.concatenate([u0[b], u1[b]]) for b in range(3)]
    mine = sum(mm_t(w[3 + b], us[b]) for b in range(3))
    first = sum(mm_t(w[b], pair[b]) for b in range(3))
    last = sum(mm_t(w[6 + b], pair[b]) for b in range(3))
    own[...] = mine + first[:, :deep] + last[:, deep:]
    to_sides(at, last[:, :deep], first[:, deep:], partner, other)


def side_rows(at, partner, other, rows):
    rows[at[0]] = other[...]
    rows[1 - at[0]] = partner[...]
    return rows[0], rows[1]


def deep_taps(w, a, row):
    y = [mm(w[3 * a + b], row) for b in range(3)]
    return y[1] + moved(y[0], 1, 1) + moved(y[2], -1, 1)


def deep_sides(at, own, got1, got2, got3, w, pooled, partner, other):
    size = own.shape[0]
    for s, piece in enumerate((own, got1, got2, got3)):
        place = jnp.bitwise_and(at[4] - s, 3) * size
        pooled[pl.ds(pl.multiple_of(place, 32), size)] = piece[...]
    row = pooled[...]
    to_sides(at, deep_taps(w, 2, row), deep_taps(w, 0, row), partner, other)


def deep_own(pooled, w, preact):
    preact[...] = deep_taps(w, 1, pooled[...])


def deep_forward(own, partner, other, upstream, output, grad):
    preact = own[...] + partner[...].astype(F32) + other[...].astype(F32)
    sigma = jax.nn.sigmoid(preact)
    output[...] = (preact * sigma).astype(BF)
    grad[...] = (upstream[...].astype(F32) * (sigma * (1.0 + preact * (1.0 - sigma)))).astype(BF)


def deep_backward(at, partner, mine, other, w, out0, out1, out2, out3, rows, whole):
    before, after = side_rows(at, partner, other, rows)
    turn = unit(mine.shape[1])
    turned = [mm_t(turn, row).astype(BF) for row in (after, mine[...], before)]
    z = [sum(mm(row, w[3 * a + b]) for a, row in enumerate(turned)) for b in range(3)]
    z = z[1] + moved(z[0], -1, 0) + moved(z[2], 1, 0)
    whole[...] = z.T.astype(BF)
    size = out0.shape[0]
    for s, out in enumerate((out0, out1, out2, out3)):
        place = jnp.bitwise_and(at[4] + s, 3) * size
        out[...] = whole[pl.ds(pl.multiple_of(place, 32), size)]


def pool_add(own, partner, other, out):
    out[...] = (own[...] + partner[...].astype(F32) + other[...].astype(F32)).astype(BF)


def pool_sum(own, got1, got2, got3, out):
    out[...] = sum(v[...].astype(F32) for v in (own, got1, got2, got3)).astype(BF)


def fine_backward(at, partner, mine, other, w, out, rows):
    before, after = side_rows(at, partner, other, rows)
    deep = mine.shape[1]
    turn = unit(deep)
    before, here, after = [mm_t(turn, row).astype(BF) for row in (before, mine[...], after)]
    top = jnp.concatenate([here, after])
    low = jnp.concatenate([before, here])
    z = []
    for b in range(3):
        both = mm(top, w[b]) + mm(low, w[6 + b])
        mid = mm(here, w[3 + b])
        z.append((both[:deep] + mid, both[deep:] + mid))
    for r in range(2):
        even = z[1][r] + z[0][r] + moved(z[2][r], 1, 0)
        late = z[1][r] + moved(z[0][r], -1, 0) + z[2][r]
        out[r, :deep] = (0.25 * even).astype(BF)
        out[r, deep:] = (0.25 * late).astype(BF)


def weave(sides, out):
    pieces, rows, part, _ = out.shape
    order = interleave(sides.shape[1])
    for r in range(rows):
        y = mm(order, sides[r]).astype(BF)
        for k in range(pieces):
            out[k, r] = y[k * part : (k + 1) * part]


def fine_slices(x, pick, out):
    size = out.shape[1]
    for r, row in enumerate(fine_rows(x)):
        cols = row.shape[0]
        for j in range(MEMBERS):
            out[j, :, r * cols : (r + 1) * cols] = mm_t(pick[j * size : (j + 1) * size], row).astype(BF)


def deep_slices(pooled, pick, out):
    size = out.shape[1]
    for j in range(MEMBERS):
        out[j] = mm(pick[j * size : (j + 1) * size], pooled[...]).astype(BF)


def tables(fine_slab, deep_slab, even, late, deep):
    size = fine_slab.shape[1]
    cols = deep_slab.shape[2]
    wide = 2 * cols
    for i in range(MEMBERS):
        block = deep_slab[i]
        row = block.astype(F32)
        turned = (moved(row, 1, 1).astype(BF), block, moved(row, -1, 1).astype(BF))
        for b in range(3):
            deep[b * size : (b + 1) * size, i * cols : (i + 1) * cols] = turned[b]
    slab = [fine_slab[i] for i in range(MEMBERS)]
    for r, out in enumerate((even, late)):
        stack = jnp.concatenate([row[:, r * wide : (r + 1) * wide] for row in slab])
        for b in range(3):
            u = mm_t(stack, column_box(wide, b)).astype(BF)
            for i in range(MEMBERS):
                out[b * size : (b + 1) * size, i * cols : (i + 1) * cols] = u[i * size : (i + 1) * size]


def pack(own, partner, other, out):
    for i, v in enumerate((own, partner, other)):
        out[i] = v[...]


def pack_more(at, first, near, out, edge):
    for i in range(2):
        out[i] = first[i]
        out[2 + i] = near[i]
    place = jnp.bitwise_and(at[1] // 2, 1)
    kept = place == at[0]

    @pl.when(kept)
    def _():
        out[4] = first[2]
        edge[...] = first[2]

    @pl.when(jnp.logical_not(kept))
    def _():
        out[4] = near[2]
        edge[...] = near[2]


def outer(at, edge, far, out):
    kept = jnp.bitwise_and(at[1] // 4, 1) == at[0]

    @pl.when(kept)
    def _():
        out[...] = edge[...]

    @pl.when(jnp.logical_not(kept))
    def _():
        out[...] = far[4]


def group_rows(at, four, far, edge, swapped, grads):
    for r in range(4):
        grads[jnp.bitwise_xor(at[1], r) + 1] = four[r]
        grads[jnp.bitwise_xor(at[1], 4 + r) + 1] = far[r]
    ends = (MEMBERS + 1) * at[0]
    grads[ends] = edge[...]
    grads[MEMBERS + 1 - ends] = swapped[...]


def against(table, grads, step):
    cols = grads.shape[2]
    return sum(mm_t(table[:, i * cols : (i + 1) * cols], grads[i + 1 + step]) for i in range(MEMBERS))


def to_owners(at, taps, order, outs, parts):
    total = jnp.concatenate([tap.astype(BF) for tap in taps])
    parts[...] = mm(order[...], total).astype(BF)
    size = outs[0].shape[1]
    for step, out in enumerate(outs):
        for half in range(2):
            place = (half * 4 + jnp.bitwise_and(at[2] + step, 3)) * size
            out[half] = parts[pl.ds(pl.multiple_of(place, 32), size)]


def deep_part(at, four, far, edge, swapped, table, order, out0, out1, out2, out3, grads, parts):
    group_rows(at, four, far, edge, swapped, grads)
    taps = [against(table, grads, 1 - a) for a in range(3)]
    to_owners(at, taps, order, (out0, out1, out2, out3), parts)


def fine_part(at, four, far, edge, swapped, even, late, order, out0, out1, out2, out3, grads, parts):
    group_rows(at, four, far, edge, swapped, grads)
    even_here = against(even, grads, 0)
    late_here = against(late, grads, 0)
    taps = (even_here + against(late, grads, 1), even_here + late_here, late_here + against(even, grads, -1))
    to_owners(at, taps, order, (out0, out1, out2, out3), parts)


def weight_half(at, own, got1, got2, got3, keep, send):
    def total(half):
        return sum(v[half].astype(F32) for v in (own, got1, got2, got3))

    keep[...] = total(at[3])
    send[...] = total(1 - at[3]).astype(BF)


def weight_sum(keep, got, out):
    total = keep[...] + got[...].astype(F32)
    grain = out.shape[1]
    for t in range(9):
        out[t] = total[t * grain : (t + 1) * grain]


def on_device(latent, conv_fine, conv_deep, upstream):
    wide = lax.axis_size("wide")
    pieces = lax.axis_size("narrow")
    groups = wide // MEMBERS
    near = [[MEMBERS * g + j for j in range(MEMBERS)] for g in range(groups)]
    me = lax.axis_index("wide").astype(jnp.int32)
    at = jnp.stack([me % 2, me % 8, me // 8 % 4, me // 32, lax.axis_index("narrow").astype(jnp.int32)])
    rows, part, depth = latent.shape
    cols = part * pieces
    deep = cols // 2
    grain = depth // wide
    size = groups * grain
    block = -(-9 * grain // 32) * 32
    w_fine = conv_fine.transpose(0, 1, 3, 2).reshape(9, -1, depth)
    w_deep = conv_deep.transpose(0, 1, 3, 2).reshape(9, -1, depth)
    fine = w_fine.shape[1]
    full = w_deep.shape[1]
    pick = jnp.asarray(channel_matrix(depth, groups), BF)
    order = jnp.asarray(owner_matrix(groups, grain, block), BF)

    def group_gather(first, behind, later=()):
        own = first[0]
        near = swap(first, 2)
        more, edge = call(
            pack_more, [shape((5,) + own.shape), shape(own.shape)], (at, first, near), behind=behind
        )
        far = swap(more, 4)
        edge = call(outer, shape(own.shape), (at, edge, far), behind=later)
        return more, far, edge, swap(edge, 1)

    def across(v, step):
        return lax.ppermute(v, "narrow", [(i, (i + step) % pieces) for i in range(pieces)])

    def swap(v, bit):
        return lax.ppermute(v, "wide", [(i, i ^ bit) for i in range(wide)])

    def pairs(to_partner, to_other):
        other = lax.ppermute(to_other, "wide", [(i, i - 1 + 2 * (i % 2)) for i in range(1, wide - 1)])
        return swap(to_partner, 1), other

    got = [across(latent, s) for s in (1, 2, 3)]
    x, own, partner, other = call(
        fine_forward,
        [shape((pieces,) + latent.shape), shape((fine, deep), F32), shape((fine, deep)), shape((fine, deep))],
        (at, latent, *got, w_fine),
    )
    partner, other = pairs(partner, other)
    fine_slab = call(
        fine_slices,
        shape((MEMBERS, size, rows * cols)),
        (x, pick),
        behind=(partner,),
    )
    mine = call(pool_add, shape((fine, deep)), (own, partner, other), behind=(fine_slab,))
    fine_slab = lax.all_to_all(fine_slab, "wide", 0, 0, axis_index_groups=near)
    got = [across(mine, s) for s in (1, 2, 3)]
    pooled, partner, other = call(
        deep_sides,
        [shape((depth, deep)), shape((full, deep)), shape((full, deep))],
        (at, mine, *got, w_deep),
    )
    partner, other = pairs(partner, other)
    preact = call(
        deep_own, shape((full, deep), F32), (pooled, w_deep), behind=(fine_slab,)
    )
    output, grad_pre = call(
        deep_forward,
        [shape((full, deep))] * 2,
        (preact, partner, other, upstream[0].T),
    )
    pre_partner, other = pairs(grad_pre, grad_pre)
    deep_slab = call(deep_slices, shape((MEMBERS, size, deep)), (pooled, pick), behind=(pre_partner,))
    deep_slab = lax.all_to_all(deep_slab, "wide", 0, 0, axis_index_groups=near)
    pre_first = call(pack, shape((3, full, deep)), (grad_pre, pre_partner, other))
    parts = call(
        deep_backward,
        [shape((fine, deep))] * 4,
        (at, pre_partner, grad_pre, other, w_deep),
        [pltpu.VMEM((2, full, deep), BF), pltpu.VMEM((depth, deep), BF)],
    )
    got = [across(parts[s], s) for s in (1, 2, 3)]
    even_table, late_table, deep_table = call(
        tables, [shape((3 * size, MEMBERS * deep))] * 3, (fine_slab, deep_slab)
    )
    grad_pool = call(pool_sum, shape((fine, deep)), (parts[0], *got), behind=(deep_slab,))
    pool_partner, other = pairs(grad_pool, grad_pool)
    pre_rows = group_gather(pre_first, (got[0],))
    pool_first = call(pack, shape((3, fine, deep)), (grad_pool, pool_partner, other), behind=(deep_table, pre_rows[2]))

    def halves(parts):
        width = parts[0].shape[2]
        got = [
            lax.ppermute(
                parts[s], "wide", [(i, i // 32 * 32 + (i // 8 + s) % 4 * 8 + i % 8) for i in range(wide)]
            )
            for s in (1, 2, 3)
        ]
        return call(weight_half, [shape((block, width), F32), shape((block, width))], (at, parts[0], *got))

    def owners(half, behind=()):
        keep, send = half
        width = keep.shape[1]
        total = call(weight_sum, shape((9, grain, width), F32), (keep, swap(send, 32)), behind=behind)
        return total.reshape(3, 3, grain, width)

    def products(body, tables, rows, behind=()):
        width = rows[0].shape[1]
        return call(
            body,
            [shape((2, block, width))] * 4,
            (at, *rows, *tables, order),
            [pltpu.VMEM((MEMBERS + 2, width, deep), BF), pltpu.VMEM((groups * block, width), BF)],
            behind=behind,
        )

    sides = call(
        fine_backward,
        shape((rows, cols, depth)),
        (at, pool_partner, grad_pool, other, w_fine),
        [pltpu.VMEM((2, fine, deep), BF)],
        behind=(pool_first,),
    )
    pool_rows = group_gather(pool_first, (sides,))
    deep_parts = products(deep_part, (deep_table,), pre_rows, (pool_rows[0],))
    fine_parts = products(fine_part, (even_table, late_table), pool_rows)
    deep_half = halves(deep_parts)
    back = call(weave, shape((pieces, rows, part, depth)), (sides,), behind=(pool_rows[2], deep_half[0]))
    partial = lax.all_to_all(back, "narrow", 0, 0)
    grad_latent = jnp.sum(partial.astype(F32), axis=0).astype(BF)

    grad_deep = owners(deep_half)
    grad_fine = owners(halves(fine_parts), (grad_latent, grad_deep))
    return output.T[None], grad_latent, grad_fine, grad_deep


def solution(mesh):
    return jax.shard_map(
        on_device,
        mesh=mesh,
        in_specs=(
            P("wide", "narrow", None),
            P(None, None, None, "narrow"),
            P(None, None, None, "narrow"),
            P("wide", None, "narrow"),
        ),
        out_specs=(
            P("wide", None, "narrow"),
            P("wide", "narrow", None),
            P(None, None, "wide", "narrow"),
            P(None, None, "wide", "narrow"),
        ),
        check_vma=False,
    )
```

```python
import functools

import jax
import jax.numpy as jnp
import numpy as np
from jax import lax
from jax.experimental import pallas as pl
from jax.experimental.pallas import tpu as pltpu
from jax.sharding import PartitionSpec as P

BF = jnp.bfloat16
F32 = jnp.float32
MEMBERS = 8
CHAIN = 3 * 10**10


def mm(a, b):
    return jnp.dot(a, b, preferred_element_type=F32)


def mm_t(a, b):
    return lax.dot_general(a, b, (((1,), (1,)), ((), ())), preferred_element_type=F32)


def channel_matrix(depth, groups):
    grain = depth // (groups * MEMBERS)
    table = np.zeros((MEMBERS, groups, grain, depth), np.float32)
    for c in range(depth):
        table[c // grain % MEMBERS, c // (MEMBERS * grain), c % grain, c] = 1.0
    return table.reshape(depth, depth)


def owner_matrix(groups, grain, block):
    table = np.zeros((groups * block, 9 * groups * grain), np.float32)
    for t in range(9):
        for g in range(groups):
            for k in range(grain):
                table[g * block + t * grain + k, (t * groups + g) * grain + k] = 1.0
    return table


def moved(y, step, axis):
    size = y.shape[axis]
    place = lax.broadcasted_iota(jnp.int32, y.shape, axis)
    edge = 0 if step == 1 else size - 1
    return jnp.where(place == edge, 0.0, pltpu.roll(y, step % size, axis))


def shape(dims, dtype=BF):
    return jax.ShapeDtypeStruct(dims, dtype)


def call(body, outs, args, scratch=(), behind=()):
    size = sum(a.size * a.dtype.itemsize for a in args)
    smem = pl.BlockSpec(memory_space=pltpu.SMEM)
    vmem = pl.BlockSpec(memory_space=pltpu.VMEM)
    aside = pl.BlockSpec(memory_space=pl.ANY)
    count = len(args)
    flops = CHAIN if body in (fine_forward, pool_add, deep_forward, deep_backward, pool_sum, fine_backward) else 0

    def kernel(*refs):
        body(*refs[:count], *refs[count + len(behind) :])

    return pl.pallas_call(
        kernel,
        out_shape=outs,
        in_specs=[smem if a.dtype == jnp.int32 else vmem for a in args] + [aside] * len(behind),
        out_specs=jax.tree.map(lambda _: vmem, outs),
        scratch_shapes=list(scratch),
        compiler_params=pltpu.CompilerParams(vmem_limit_bytes=16 * 2**20),
        cost_estimate=pl.CostEstimate(flops=flops, bytes_accessed=size, transcendentals=0),
    )(*args, *behind)


def column_box(cols, b):
    low = 2 * lax.broadcasted_iota(jnp.int32, (cols // 2, cols), 0) + (b - 1)
    gap = lax.broadcasted_iota(jnp.int32, (cols // 2, cols), 1) - low
    return jnp.where((gap == 0) | (gap == 1), 0.25, 0.0).astype(BF)


def unit(size):
    row = lax.broadcasted_iota(jnp.int32, (size, size), 0)
    return jnp.where(row == lax.broadcasted_iota(jnp.int32, (size, size), 1), 1.0, 0.0).astype(BF)


def interleave(cols):
    place = lax.broadcasted_iota(jnp.int32, (cols, cols), 0)
    source = place // 2 + (place % 2) * (cols // 2)
    return jnp.where(source == lax.broadcasted_iota(jnp.int32, (cols, cols), 1), 1.0, 0.0).astype(BF)


def fine_rows(x):
    pieces = x.shape[0]
    return [jnp.concatenate([x[k, r] for k in range(pieces)]) for r in range(2)]


def to_sides(at, up, down, partner, other):
    up = up.astype(BF)
    down = down.astype(BF)

    @pl.when(at[0] == 0)
    def _():
        partner[...] = down
        other[...] = up

    @pl.when(at[0] == 1)
    def _():
        partner[...] = up
        other[...] = down


def fine_forward(at, mine, got1, got2, got3, w, x, own, partner, other):
    for s, piece in enumerate((mine, got1, got2, got3)):
        x[jnp.bitwise_and(at[4] - s, 3)] = piece[...]
    deep = own.shape[1]
    rows = fine_rows(x)
    u0, us, u1 = [], [], []
    for b in range(3):
        box = column_box(2 * deep, b)
        u = [mm(box, row) for row in rows]
        u0.append(u[0].astype(BF))
        u1.append(u[1].astype(BF))
        us.append((u[0] + u[1]).astype(BF))
    pair = [jnp.concatenate([u0[b], u1[b]]) for b in range(3)]
    mine = sum(mm_t(w[3 + b], us[b]) for b in range(3))
    first = sum(mm_t(w[b], pair[b]) for b in range(3))
    last = sum(mm_t(w[6 + b], pair[b]) for b in range(3))
    own[...] = mine + first[:, :deep] + last[:, deep:]
    to_sides(at, last[:, :deep], first[:, deep:], partner, other)


def side_rows(at, partner, other, rows):
    rows[at[0]] = other[...]
    rows[1 - at[0]] = partner[...]
    return rows[0], rows[1]


def deep_taps(w, a, row):
    y = [mm(w[3 * a + b], row) for b in range(3)]
    return y[1] + moved(y[0], 1, 1) + moved(y[2], -1, 1)


def deep_sides(at, own, got1, got2, got3, w, pooled, partner, other):
    size = own.shape[0]
    for s, piece in enumerate((own, got1, got2, got3)):
        place = jnp.bitwise_and(at[4] - s, 3) * size
        pooled[pl.ds(pl.multiple_of(place, 32), size)] = piece[...]
    row = pooled[...]
    to_sides(at, deep_taps(w, 2, row), deep_taps(w, 0, row), partner, other)


def deep_own(pooled, w, preact):
    preact[...] = deep_taps(w, 1, pooled[...])


def deep_forward(own, partner, other, upstream, output, grad):
    preact = own[...] + partner[...].astype(F32) + other[...].astype(F32)
    sigma = jax.nn.sigmoid(preact)
    output[...] = (preact * sigma).astype(BF)
    grad[...] = (upstream[...].astype(F32) * (sigma * (1.0 + preact * (1.0 - sigma)))).astype(BF)


def deep_backward(at, partner, mine, other, w, out0, out1, out2, out3, rows, whole):
    before, after = side_rows(at, partner, other, rows)
    turn = unit(mine.shape[1])
    turned = [mm_t(turn, row).astype(BF) for row in (after, mine[...], before)]
    z = [sum(mm(row, w[3 * a + b]) for a, row in enumerate(turned)) for b in range(3)]
    z = z[1] + moved(z[0], -1, 0) + moved(z[2], 1, 0)
    whole[...] = z.T.astype(BF)
    size = out0.shape[0]
    for s, out in enumerate((out0, out1, out2, out3)):
        place = jnp.bitwise_and(at[4] + s, 3) * size
        out[...] = whole[pl.ds(pl.multiple_of(place, 32), size)]


def pool_add(own, partner, other, out):
    out[...] = (own[...] + partner[...].astype(F32) + other[...].astype(F32)).astype(BF)


def pool_sum(own, got1, got2, got3, out):
    out[...] = sum(v[...].astype(F32) for v in (own, got1, got2, got3)).astype(BF)


def fine_backward(at, partner, mine, other, w, out, rows):
    before, after = side_rows(at, partner, other, rows)
    deep = mine.shape[1]
    turn = unit(deep)
    before, here, after = [mm_t(turn, row).astype(BF) for row in (before, mine[...], after)]
    top = jnp.concatenate([here, after])
    low = jnp.concatenate([before, here])
    z = []
    for b in range(3):
        both = mm(top, w[b]) + mm(low, w[6 + b])
        mid = mm(here, w[3 + b])
        z.append((both[:deep] + mid, both[deep:] + mid))
    for r in range(2):
        even = z[1][r] + z[0][r] + moved(z[2][r], 1, 0)
        late = z[1][r] + moved(z[0][r], -1, 0) + z[2][r]
        out[r, :deep] = (0.25 * even).astype(BF)
        out[r, deep:] = (0.25 * late).astype(BF)


def weave(sides, out):
    pieces, rows, part, _ = out.shape
    order = interleave(sides.shape[1])
    for r in range(rows):
        y = mm(order, sides[r]).astype(BF)
        for k in range(pieces):
            out[k, r] = y[k * part : (k + 1) * part]


def fine_slices(x, pick, out):
    size = out.shape[1]
    for r, row in enumerate(fine_rows(x)):
        cols = row.shape[0]
        for j in range(MEMBERS):
            out[j, :, r * cols : (r + 1) * cols] = mm_t(pick[j * size : (j + 1) * size], row).astype(BF)


def deep_slices(pooled, pick, out):
    size = out.shape[1]
    for j in range(MEMBERS):
        out[j] = mm(pick[j * size : (j + 1) * size], pooled[...]).astype(BF)


def tables(fine_slab, deep_slab, even, late, deep):
    size = fine_slab.shape[1]
    cols = deep_slab.shape[2]
    wide = 2 * cols
    for i in range(MEMBERS):
        block = deep_slab[i]
        row = block.astype(F32)
        turned = (moved(row, 1, 1).astype(BF), block, moved(row, -1, 1).astype(BF))
        for b in range(3):
            deep[b * size : (b + 1) * size, i * cols : (i + 1) * cols] = turned[b]
    slab = [fine_slab[i] for i in range(MEMBERS)]
    for r, out in enumerate((even, late)):
        stack = jnp.concatenate([row[:, r * wide : (r + 1) * wide] for row in slab])
        for b in range(3):
            u = mm_t(stack, column_box(wide, b)).astype(BF)
            for i in range(MEMBERS):
                out[b * size : (b + 1) * size, i * cols : (i + 1) * cols] = u[i * size : (i + 1) * size]


def pack(own, partner, other, out):
    for i, v in enumerate((own, partner, other)):
        out[i] = v[...]


def pack_more(at, first, near, out, edge):
    for i in range(2):
        out[i] = first[i]
        out[2 + i] = near[i]
    place = jnp.bitwise_and(at[1] // 2, 1)
    kept = place == at[0]

    @pl.when(kept)
    def _():
        out[4] = first[2]
        edge[...] = first[2]

    @pl.when(jnp.logical_not(kept))
    def _():
        out[4] = near[2]
        edge[...] = near[2]


def outer(at, edge, far, out):
    kept = jnp.bitwise_and(at[1] // 4, 1) == at[0]

    @pl.when(kept)
    def _():
        out[...] = edge[...]

    @pl.when(jnp.logical_not(kept))
    def _():
        out[...] = far[4]


def outer_direct(at, own, near, far, both, out):
    source = jnp.bitwise_xor(at[1] // 2, 3 * at[0])
    for i, rows in enumerate((own, near, far, both)):

        @pl.when(source == i)
        def _(rows=rows):
            out[...] = rows[2]


def group_rows(at, rows, edge, swapped, grads):
    for r, row in enumerate(rows):
        grads[jnp.bitwise_xor(at[1], r) + 1] = row[...]
    ends = (MEMBERS + 1) * at[0]
    grads[ends] = edge[...]
    grads[MEMBERS + 1 - ends] = swapped[...]


def against(table, grads, step):
    cols = grads.shape[2]
    return sum(mm_t(table[:, i * cols : (i + 1) * cols], grads[i + 1 + step]) for i in range(MEMBERS))


def to_owners(at, taps, order, outs, parts):
    total = jnp.concatenate([tap.astype(BF) for tap in taps])
    parts[...] = mm(order[...], total).astype(BF)
    size = outs[0].shape[1]
    for step, out in enumerate(outs):
        for half in range(2):
            place = (half * 4 + jnp.bitwise_and(at[2] + step, 3)) * size
            out[half] = parts[pl.ds(pl.multiple_of(place, 32), size)]


def deep_part(at, four, far, edge, swapped, table, order, out0, out1, out2, out3, grads, parts):
    rows = [four.at[r] for r in range(4)] + [far.at[r] for r in range(4)]
    group_rows(at, rows, edge, swapped, grads)
    taps = [against(table, grads, 1 - a) for a in range(3)]
    to_owners(at, taps, order, (out0, out1, out2, out3), parts)


def fine_part(at, own, near, far, both, edge, swapped, even, late, order, out0, out1, out2, out3, grads, parts):
    rows = [rows.at[r] for rows in (own, near, far, both) for r in range(2)]
    group_rows(at, rows, edge, swapped, grads)
    even_here = against(even, grads, 0)
    late_here = against(late, grads, 0)
    taps = (even_here + against(late, grads, 1), even_here + late_here, late_here + against(even, grads, -1))
    to_owners(at, taps, order, (out0, out1, out2, out3), parts)


def weight_half(at, own, got1, got2, got3, keep, send):
    def total(half):
        return sum(v[half].astype(F32) for v in (own, got1, got2, got3))

    keep[...] = total(at[3])
    send[...] = total(1 - at[3]).astype(BF)


def weight_sum(keep, got, out):
    total = keep[...] + got[...].astype(F32)
    grain = out.shape[1]
    for t in range(9):
        out[t] = total[t * grain : (t + 1) * grain]


def on_device(latent, conv_fine, conv_deep, upstream):
    wide = lax.axis_size("wide")
    pieces = lax.axis_size("narrow")
    groups = wide // MEMBERS
    near = [[MEMBERS * g + j for j in range(MEMBERS)] for g in range(groups)]
    me = lax.axis_index("wide").astype(jnp.int32)
    at = jnp.stack([me % 2, me % 8, me // 8 % 4, me // 32, lax.axis_index("narrow").astype(jnp.int32)])
    rows, part, depth = latent.shape
    cols = part * pieces
    deep = cols // 2
    grain = depth // wide
    size = groups * grain
    block = -(-9 * grain // 32) * 32
    w_fine = conv_fine.transpose(0, 1, 3, 2).reshape(9, -1, depth)
    w_deep = conv_deep.transpose(0, 1, 3, 2).reshape(9, -1, depth)
    fine = w_fine.shape[1]
    full = w_deep.shape[1]
    pick = jnp.asarray(channel_matrix(depth, groups), BF)
    order = jnp.asarray(owner_matrix(groups, grain, block), BF)

    def group_gather(first, behind, later=()):
        own = first[0]
        near = swap(first, 2)
        more, edge = call(
            pack_more, [shape((5,) + own.shape), shape(own.shape)], (at, first, near), behind=behind
        )
        far = swap(more, 4)
        edge = call(outer, shape(own.shape), (at, edge, far), behind=later)
        return more, far, edge, swap(edge, 1)

    def across(v, step):
        return lax.ppermute(v, "narrow", [(i, (i + step) % pieces) for i in range(pieces)])

    def swap(v, bit):
        return lax.ppermute(v, "wide", [(i, i ^ bit) for i in range(wide)])

    def pairs(to_partner, to_other):
        other = lax.ppermute(to_other, "wide", [(i, i - 1 + 2 * (i % 2)) for i in range(1, wide - 1)])
        return swap(to_partner, 1), other

    got = [across(latent, s) for s in (1, 2, 3)]
    x, own, partner, other = call(
        fine_forward,
        [shape((pieces,) + latent.shape), shape((fine, deep), F32), shape((fine, deep)), shape((fine, deep))],
        (at, latent, *got, w_fine),
    )
    partner, other = pairs(partner, other)
    fine_slab = call(
        fine_slices,
        shape((MEMBERS, size, rows * cols)),
        (x, pick),
        behind=(partner,),
    )
    mine = call(pool_add, shape((fine, deep)), (own, partner, other), behind=(fine_slab,))
    fine_slab = lax.all_to_all(fine_slab, "wide", 0, 0, axis_index_groups=near)
    got = [across(mine, s) for s in (1, 2, 3)]
    pooled, partner, other = call(
        deep_sides,
        [shape((depth, deep)), shape((full, deep)), shape((full, deep))],
        (at, mine, *got, w_deep),
    )
    partner, other = pairs(partner, other)
    preact = call(
        deep_own, shape((full, deep), F32), (pooled, w_deep), behind=(fine_slab,)
    )
    output, grad_pre = call(
        deep_forward,
        [shape((full, deep))] * 2,
        (preact, partner, other, upstream[0].T),
    )
    pre_partner, other = pairs(grad_pre, grad_pre)
    deep_slab = call(deep_slices, shape((MEMBERS, size, deep)), (pooled, pick), behind=(pre_partner,))
    deep_slab = lax.all_to_all(deep_slab, "wide", 0, 0, axis_index_groups=near)
    pre_first = call(pack, shape((3, full, deep)), (grad_pre, pre_partner, other))
    parts = call(
        deep_backward,
        [shape((fine, deep))] * 4,
        (at, pre_partner, grad_pre, other, w_deep),
        [pltpu.VMEM((2, full, deep), BF), pltpu.VMEM((depth, deep), BF)],
    )
    got = [across(parts[s], s) for s in (1, 2, 3)]
    even_table, late_table, deep_table = call(
        tables, [shape((3 * size, MEMBERS * deep))] * 3, (fine_slab, deep_slab)
    )
    grad_pool = call(pool_sum, shape((fine, deep)), (parts[0], *got), behind=(deep_slab,))
    pool_partner, other = pairs(grad_pool, grad_pool)
    pre_rows = group_gather(pre_first, (got[0],))
    pool_first = call(pack, shape((3, fine, deep)), (grad_pool, pool_partner, other), behind=(deep_table, pre_rows[2]))

    def halves(parts):
        width = parts[0].shape[2]
        got = [
            lax.ppermute(
                parts[s], "wide", [(i, i // 32 * 32 + (i // 8 + s) % 4 * 8 + i % 8) for i in range(wide)]
            )
            for s in (1, 2, 3)
        ]
        return call(weight_half, [shape((block, width), F32), shape((block, width))], (at, parts[0], *got))

    def owners(half, behind=()):
        keep, send = half
        width = keep.shape[1]
        total = call(weight_sum, shape((9, grain, width), F32), (keep, swap(send, 32)), behind=behind)
        return total.reshape(3, 3, grain, width)

    def products(body, tables, rows, behind=()):
        width = rows[-1].shape[0]
        return call(
            body,
            [shape((2, block, width))] * 4,
            (at, *rows, *tables, order),
            [pltpu.VMEM((MEMBERS + 2, width, deep), BF), pltpu.VMEM((groups * block, width), BF)],
            behind=behind,
        )

    sides = call(
        fine_backward,
        shape((rows, cols, depth)),
        (at, pool_partner, grad_pool, other, w_fine),
        [pltpu.VMEM((2, fine, deep), BF)],
        behind=(pool_first,),
    )
    deep_parts = products(deep_part, (deep_table,), pre_rows, (pool_first,))
    pool_rows = [pool_first] + [swap(pool_first, bit) for bit in (2, 4, 6)]
    pool_edge = call(outer_direct, shape((fine, deep)), (at, *pool_rows), behind=(sides, deep_parts[0]))
    pool_rows += [pool_edge, swap(pool_edge, 1)]
    fine_parts = products(fine_part, (even_table, late_table), pool_rows)
    deep_half = halves(deep_parts)
    back = call(weave, shape((pieces, rows, part, depth)), (sides,), behind=(pool_edge,))
    partial = lax.all_to_all(back, "narrow", 0, 0)
    grad_latent = jnp.sum(partial.astype(F32), axis=0).astype(BF)

    grad_deep = owners(deep_half)
    grad_fine = owners(halves(fine_parts), (grad_latent, grad_deep))
    return output.T[None], grad_latent, grad_fine, grad_deep


def solution(mesh):
    return jax.shard_map(
        on_device,
        mesh=mesh,
        in_specs=(
            P("wide", "narrow", None),
            P(None, None, None, "narrow"),
            P(None, None, None, "narrow"),
            P("wide", None, "narrow"),
        ),
        out_specs=(
            P("wide", None, "narrow"),
            P("wide", "narrow", None),
            P(None, None, "wide", "narrow"),
            P(None, None, "wide", "narrow"),
        ),
        check_vma=False,
    )
```

```python
import functools

import jax
import jax.numpy as jnp
import numpy as np
from jax import lax
from jax.experimental import pallas as pl
from jax.experimental.pallas import tpu as pltpu
from jax.sharding import PartitionSpec as P

BF = jnp.bfloat16
F32 = jnp.float32
MEMBERS = 8
CHAIN = 3 * 10**10


def mm(a, b):
    return jnp.dot(a, b, preferred_element_type=F32)


def mm_t(a, b):
    return lax.dot_general(a, b, (((1,), (1,)), ((), ())), preferred_element_type=F32)


def channel_matrix(depth, groups):
    grain = depth // (groups * MEMBERS)
    table = np.zeros((MEMBERS, groups, grain, depth), np.float32)
    for c in range(depth):
        table[c // grain % MEMBERS, c // (MEMBERS * grain), c % grain, c] = 1.0
    return table.reshape(depth, depth)


def owner_matrix(groups, grain, block):
    table = np.zeros((groups * block, 9 * groups * grain), np.float32)
    for t in range(9):
        for g in range(groups):
            for k in range(grain):
                table[g * block + t * grain + k, (t * groups + g) * grain + k] = 1.0
    return table


def moved(y, step, axis):
    size = y.shape[axis]
    place = lax.broadcasted_iota(jnp.int32, y.shape, axis)
    edge = 0 if step == 1 else size - 1
    return jnp.where(place == edge, 0.0, pltpu.roll(y, step % size, axis))


def shape(dims, dtype=BF):
    return jax.ShapeDtypeStruct(dims, dtype)


def call(body, outs, args, scratch=(), behind=()):
    size = sum(a.size * a.dtype.itemsize for a in args)
    smem = pl.BlockSpec(memory_space=pltpu.SMEM)
    vmem = pl.BlockSpec(memory_space=pltpu.VMEM)
    aside = pl.BlockSpec(memory_space=pl.ANY)
    count = len(args)
    flops = CHAIN if body in (fine_forward, pool_add, deep_forward, deep_backward, pool_sum, fine_backward) else 0

    def kernel(*refs):
        body(*refs[:count], *refs[count + len(behind) :])

    return pl.pallas_call(
        kernel,
        out_shape=outs,
        in_specs=[smem if a.dtype == jnp.int32 else vmem for a in args] + [aside] * len(behind),
        out_specs=jax.tree.map(lambda _: vmem, outs),
        scratch_shapes=list(scratch),
        compiler_params=pltpu.CompilerParams(vmem_limit_bytes=16 * 2**20),
        cost_estimate=pl.CostEstimate(flops=flops, bytes_accessed=size, transcendentals=0),
    )(*args, *behind)


def column_box(cols, b):
    low = 2 * lax.broadcasted_iota(jnp.int32, (cols // 2, cols), 0) + (b - 1)
    gap = lax.broadcasted_iota(jnp.int32, (cols // 2, cols), 1) - low
    return jnp.where((gap == 0) | (gap == 1), 0.25, 0.0).astype(BF)


def unit(size):
    row = lax.broadcasted_iota(jnp.int32, (size, size), 0)
    return jnp.where(row == lax.broadcasted_iota(jnp.int32, (size, size), 1), 1.0, 0.0).astype(BF)


def interleave(cols):
    place = lax.broadcasted_iota(jnp.int32, (cols, cols), 0)
    source = place // 2 + (place % 2) * (cols // 2)
    return jnp.where(source == lax.broadcasted_iota(jnp.int32, (cols, cols), 1), 1.0, 0.0).astype(BF)


def fine_rows(x):
    pieces = x.shape[0]
    return [jnp.concatenate([x[k, r] for k in range(pieces)]) for r in range(2)]


def to_sides(at, up, down, partner, other):
    up = up.astype(BF)
    down = down.astype(BF)

    @pl.when(at[0] == 0)
    def _():
        partner[...] = down
        other[...] = up

    @pl.when(at[0] == 1)
    def _():
        partner[...] = up
        other[...] = down


def fine_forward(at, mine, got1, got2, got3, w, x, own, partner, other):
    for s, piece in enumerate((mine, got1, got2, got3)):
        x[jnp.bitwise_and(at[4] - s, 3)] = piece[...]
    deep = own.shape[1]
    rows = fine_rows(x)
    u0, us, u1 = [], [], []
    for b in range(3):
        box = column_box(2 * deep, b)
        u = [mm(box, row) for row in rows]
        u0.append(u[0].astype(BF))
        u1.append(u[1].astype(BF))
        us.append((u[0] + u[1]).astype(BF))
    pair = [jnp.concatenate([u0[b], u1[b]]) for b in range(3)]
    mine = sum(mm_t(w[3 + b], us[b]) for b in range(3))
    first = sum(mm_t(w[b], pair[b]) for b in range(3))
    last = sum(mm_t(w[6 + b], pair[b]) for b in range(3))
    own[...] = mine + first[:, :deep] + last[:, deep:]
    to_sides(at, last[:, :deep], first[:, deep:], partner, other)


def side_rows(at, partner, other, rows):
    rows[at[0]] = other[...]
    rows[1 - at[0]] = partner[...]
    return rows[0], rows[1]


def deep_taps(w, a, row):
    y = [mm(w[3 * a + b], row) for b in range(3)]
    return y[1] + moved(y[0], 1, 1) + moved(y[2], -1, 1)


def deep_sides(at, own, got1, got2, got3, w, pooled, partner, other):
    size = own.shape[0]
    for s, piece in enumerate((own, got1, got2, got3)):
        place = jnp.bitwise_and(at[4] - s, 3) * size
        pooled[pl.ds(pl.multiple_of(place, 32), size)] = piece[...]
    row = pooled[...]
    to_sides(at, deep_taps(w, 2, row), deep_taps(w, 0, row), partner, other)


def deep_own(pooled, w, preact):
    preact[...] = deep_taps(w, 1, pooled[...])


def deep_forward(own, partner, other, upstream, output, grad):
    preact = own[...] + partner[...].astype(F32) + other[...].astype(F32)
    sigma = jax.nn.sigmoid(preact)
    output[...] = (preact * sigma).astype(BF)
    grad[...] = (upstream[...].astype(F32) * (sigma * (1.0 + preact * (1.0 - sigma)))).astype(BF)


def deep_backward(at, partner, mine, other, w, out0, out1, out2, out3, rows, whole):
    before, after = side_rows(at, partner, other, rows)
    turn = unit(mine.shape[1])
    turned = [mm_t(turn, row).astype(BF) for row in (after, mine[...], before)]
    z = [sum(mm(row, w[3 * a + b]) for a, row in enumerate(turned)) for b in range(3)]
    z = z[1] + moved(z[0], -1, 0) + moved(z[2], 1, 0)
    whole[...] = z.T.astype(BF)
    size = out0.shape[0]
    for s, out in enumerate((out0, out1, out2, out3)):
        place = jnp.bitwise_and(at[4] + s, 3) * size
        out[...] = whole[pl.ds(pl.multiple_of(place, 32), size)]


def pool_add(own, partner, other, out):
    out[...] = (own[...] + partner[...].astype(F32) + other[...].astype(F32)).astype(BF)


def pool_sum(own, got1, got2, got3, out):
    out[...] = sum(v[...].astype(F32) for v in (own, got1, got2, got3)).astype(BF)


def fine_backward(at, partner, mine, other, w, out, rows):
    before, after = side_rows(at, partner, other, rows)
    deep = mine.shape[1]
    turn = unit(deep)
    before, here, after = [mm_t(turn, row).astype(BF) for row in (before, mine[...], after)]
    top = jnp.concatenate([here, after])
    low = jnp.concatenate([before, here])
    z = []
    for b in range(3):
        both = mm(top, w[b]) + mm(low, w[6 + b])
        mid = mm(here, w[3 + b])
        z.append((both[:deep] + mid, both[deep:] + mid))
    for r in range(2):
        even = z[1][r] + z[0][r] + moved(z[2][r], 1, 0)
        late = z[1][r] + moved(z[0][r], -1, 0) + z[2][r]
        out[r, :deep] = (0.25 * even).astype(BF)
        out[r, deep:] = (0.25 * late).astype(BF)


def weave(sides, out):
    pieces, rows, part, _ = out.shape
    order = interleave(sides.shape[1])
    for r in range(rows):
        y = mm(order, sides[r]).astype(BF)
        for k in range(pieces):
            out[k, r] = y[k * part : (k + 1) * part]


def fine_slices(x, pick, out):
    size = out.shape[1]
    for r, row in enumerate(fine_rows(x)):
        cols = row.shape[0]
        for j in range(MEMBERS):
            out[j, :, r * cols : (r + 1) * cols] = mm_t(pick[j * size : (j + 1) * size], row).astype(BF)


def deep_slices(pooled, pick, out):
    size = out.shape[1]
    for j in range(MEMBERS):
        out[j] = mm(pick[j * size : (j + 1) * size], pooled[...]).astype(BF)


def tables(fine_slab, deep_slab, even, late, deep):
    size = fine_slab.shape[1]
    cols = deep_slab.shape[2]
    wide = 2 * cols
    for i in range(MEMBERS):
        block = deep_slab[i]
        row = block.astype(F32)
        turned = (moved(row, 1, 1).astype(BF), block, moved(row, -1, 1).astype(BF))
        for b in range(3):
            deep[b * size : (b + 1) * size, i * cols : (i + 1) * cols] = turned[b]
    slab = [fine_slab[i] for i in range(MEMBERS)]
    for r, out in enumerate((even, late)):
        stack = jnp.concatenate([row[:, r * wide : (r + 1) * wide] for row in slab])
        for b in range(3):
            u = mm_t(stack, column_box(wide, b)).astype(BF)
            for i in range(MEMBERS):
                out[b * size : (b + 1) * size, i * cols : (i + 1) * cols] = u[i * size : (i + 1) * size]


def pack(own, partner, other, out):
    for i, v in enumerate((own, partner, other)):
        out[i] = v[...]


def pack_more(at, first, near, out, edge):
    for i in range(2):
        out[i] = first[i]
        out[2 + i] = near[i]
    place = jnp.bitwise_and(at[1] // 2, 1)
    kept = place == at[0]

    @pl.when(kept)
    def _():
        out[4] = first[2]
        edge[...] = first[2]

    @pl.when(jnp.logical_not(kept))
    def _():
        out[4] = near[2]
        edge[...] = near[2]


def outer(at, edge, far, out):
    kept = jnp.bitwise_and(at[1] // 4, 1) == at[0]

    @pl.when(kept)
    def _():
        out[...] = edge[...]

    @pl.when(jnp.logical_not(kept))
    def _():
        out[...] = far[4]


def outer_direct(at, own, near, far, both, out):
    source = jnp.bitwise_xor(at[1] // 2, 3 * at[0])
    for i, rows in enumerate((own, near, far, both)):

        @pl.when(source == i)
        def _(rows=rows):
            out[...] = rows[2]


def group_rows(at, rows, edge, swapped, grads):
    for r, row in enumerate(rows):
        grads[jnp.bitwise_xor(at[1], r) + 1] = row[...]
    ends = (MEMBERS + 1) * at[0]
    grads[ends] = edge[...]
    grads[MEMBERS + 1 - ends] = swapped[...]


def against(table, grads, step):
    cols = grads.shape[2]
    return sum(mm_t(table[:, i * cols : (i + 1) * cols], grads[i + 1 + step]) for i in range(MEMBERS))


def to_owners(at, taps, order, outs, parts):
    total = jnp.concatenate([tap.astype(BF) for tap in taps])
    parts[...] = mm(order[...], total).astype(BF)
    size = outs[0].shape[1]
    for step, out in enumerate(outs):
        for half in range(2):
            place = (half * 4 + jnp.bitwise_and(at[2] + step, 3)) * size
            out[half] = parts[pl.ds(pl.multiple_of(place, 32), size)]


def deep_part(at, four, far, edge, swapped, table, order, out0, out1, out2, out3, grads, parts):
    rows = [four.at[r] for r in range(4)] + [far.at[r] for r in range(4)]
    group_rows(at, rows, edge, swapped, grads)
    taps = [against(table, grads, 1 - a) for a in range(3)]
    to_owners(at, taps, order, (out0, out1, out2, out3), parts)


def fine_part(at, own, near, far, both, edge, swapped, even, late, order, out0, out1, out2, out3, grads, parts):
    rows = [rows.at[r] for rows in (own, near, far, both) for r in range(2)]
    group_rows(at, rows, edge, swapped, grads)
    even_here = against(even, grads, 0)
    late_here = against(late, grads, 0)
    taps = (even_here + against(late, grads, 1), even_here + late_here, late_here + against(even, grads, -1))
    to_owners(at, taps, order, (out0, out1, out2, out3), parts)


def weight_half(at, own, got1, got2, got3, keep, send):
    def total(half):
        return sum(v[half].astype(F32) for v in (own, got1, got2, got3))

    keep[...] = total(at[3])
    send[...] = total(1 - at[3]).astype(BF)


def weight_sum(keep, got, out):
    total = keep[...] + got[...].astype(F32)
    grain = out.shape[1]
    for t in range(9):
        out[t] = total[t * grain : (t + 1) * grain]


def on_device(latent, conv_fine, conv_deep, upstream):
    wide = lax.axis_size("wide")
    pieces = lax.axis_size("narrow")
    groups = wide // MEMBERS
    near = [[MEMBERS * g + j for j in range(MEMBERS)] for g in range(groups)]
    me = lax.axis_index("wide").astype(jnp.int32)
    at = jnp.stack([me % 2, me % 8, me // 8 % 4, me // 32, lax.axis_index("narrow").astype(jnp.int32)])
    rows, part, depth = latent.shape
    cols = part * pieces
    deep = cols // 2
    grain = depth // wide
    size = groups * grain
    block = -(-9 * grain // 32) * 32
    w_fine = conv_fine.transpose(0, 1, 3, 2).reshape(9, -1, depth)
    w_deep = conv_deep.transpose(0, 1, 3, 2).reshape(9, -1, depth)
    fine = w_fine.shape[1]
    full = w_deep.shape[1]
    pick = jnp.asarray(channel_matrix(depth, groups), BF)
    order = jnp.asarray(owner_matrix(groups, grain, block), BF)

    def group_gather(first, behind, later=()):
        own = first[0]
        near = swap(first, 2)
        more, edge = call(
            pack_more, [shape((5,) + own.shape), shape(own.shape)], (at, first, near), behind=behind
        )
        far = swap(more, 4)
        edge = call(outer, shape(own.shape), (at, edge, far), behind=later)
        return more, far, edge, swap(edge, 1)

    def across(v, step):
        return lax.ppermute(v, "narrow", [(i, (i + step) % pieces) for i in range(pieces)])

    def swap(v, bit):
        return lax.ppermute(v, "wide", [(i, i ^ bit) for i in range(wide)])

    def pairs(to_partner, to_other):
        other = lax.ppermute(to_other, "wide", [(i, i - 1 + 2 * (i % 2)) for i in range(1, wide - 1)])
        return swap(to_partner, 1), other

    got = [across(latent, s) for s in (1, 2, 3)]
    x, own, partner, other = call(
        fine_forward,
        [shape((pieces,) + latent.shape), shape((fine, deep), F32), shape((fine, deep)), shape((fine, deep))],
        (at, latent, *got, w_fine),
    )
    partner, other = pairs(partner, other)
    fine_slab = call(
        fine_slices,
        shape((MEMBERS, size, rows * cols)),
        (x, pick),
        behind=(partner,),
    )
    mine = call(pool_add, shape((fine, deep)), (own, partner, other), behind=(fine_slab,))
    fine_slab = lax.all_to_all(fine_slab, "wide", 0, 0, axis_index_groups=near)
    got = [across(mine, s) for s in (1, 2, 3)]
    pooled, partner, other = call(
        deep_sides,
        [shape((depth, deep)), shape((full, deep)), shape((full, deep))],
        (at, mine, *got, w_deep),
    )
    partner, other = pairs(partner, other)
    preact = call(
        deep_own, shape((full, deep), F32), (pooled, w_deep), behind=(fine_slab,)
    )
    output, grad_pre = call(
        deep_forward,
        [shape((full, deep))] * 2,
        (preact, partner, other, upstream[0].T),
    )
    pre_partner, other = pairs(grad_pre, grad_pre)
    deep_pre = call(deep_slices, shape((MEMBERS, size, deep)), (pooled, pick), behind=(pre_partner,))
    deep_slab = lax.all_to_all(deep_pre, "wide", 0, 0, axis_index_groups=near)
    pre_first = call(pack, shape((3, full, deep)), (grad_pre, pre_partner, other), behind=(deep_pre,))
    parts = call(
        deep_backward,
        [shape((fine, deep))] * 4,
        (at, pre_partner, grad_pre, other, w_deep),
        [pltpu.VMEM((2, full, deep), BF), pltpu.VMEM((depth, deep), BF)],
    )
    got = [across(parts[s], s) for s in (1, 2, 3)]
    even_table, late_table, deep_table = call(
        tables, [shape((3 * size, MEMBERS * deep))] * 3, (fine_slab, deep_slab)
    )
    grad_pool = call(pool_sum, shape((fine, deep)), (parts[0], *got), behind=(deep_slab,))
    pool_partner, other = pairs(grad_pool, grad_pool)
    pre_rows = group_gather(pre_first, (got[0],))
    pool_first = call(pack, shape((3, fine, deep)), (grad_pool, pool_partner, other), behind=(deep_table, pre_rows[2]))

    def halves(parts):
        width = parts[0].shape[2]
        got = [
            lax.ppermute(
                parts[s], "wide", [(i, i // 32 * 32 + (i // 8 + s) % 4 * 8 + i % 8) for i in range(wide)]
            )
            for s in (1, 2, 3)
        ]
        return call(weight_half, [shape((block, width), F32), shape((block, width))], (at, parts[0], *got))

    def owners(half, behind=()):
        keep, send = half
        width = keep.shape[1]
        total = call(weight_sum, shape((9, grain, width), F32), (keep, swap(send, 32)), behind=behind)
        return total.reshape(3, 3, grain, width)

    def products(body, tables, rows, behind=()):
        width = rows[-1].shape[0]
        return call(
            body,
            [shape((2, block, width))] * 4,
            (at, *rows, *tables, order),
            [pltpu.VMEM((MEMBERS + 2, width, deep), BF), pltpu.VMEM((groups * block, width), BF)],
            behind=behind,
        )

    sides = call(
        fine_backward,
        shape((rows, cols, depth)),
        (at, pool_partner, grad_pool, other, w_fine),
        [pltpu.VMEM((2, fine, deep), BF)],
        behind=(pool_first,),
    )
    deep_parts = products(deep_part, (deep_table,), pre_rows, (pool_first,))
    pool_rows = [pool_first] + [swap(pool_first, bit) for bit in (2, 4, 6)]
    pool_edge = call(outer_direct, shape((fine, deep)), (at, *pool_rows), behind=(sides, deep_parts[0]))
    pool_rows += [pool_edge, swap(pool_edge, 1)]
    fine_parts = products(fine_part, (even_table, late_table), pool_rows)
    deep_half = halves(deep_parts)
    back = call(weave, shape((pieces, rows, part, depth)), (sides,), behind=(pool_edge,))
    partial = lax.all_to_all(back, "narrow", 0, 0)
    grad_latent = jnp.sum(partial.astype(F32), axis=0).astype(BF)

    grad_deep = owners(deep_half)
    grad_fine = owners(halves(fine_parts), (grad_latent, grad_deep))
    return output.T[None], grad_latent, grad_fine, grad_deep


def solution(mesh):
    return jax.shard_map(
        on_device,
        mesh=mesh,
        in_specs=(
            P("wide", "narrow", None),
            P(None, None, None, "narrow"),
            P(None, None, None, "narrow"),
            P("wide", None, "narrow"),
        ),
        out_specs=(
            P("wide", None, "narrow"),
            P("wide", "narrow", None),
            P(None, None, "wide", "narrow"),
            P(None, None, "wide", "narrow"),
        ),
        check_vma=False,
    )
```

```python
import functools

import jax
import jax.numpy as jnp
import numpy as np
from jax import lax
from jax.experimental import pallas as pl
from jax.experimental.pallas import tpu as pltpu
from jax.sharding import PartitionSpec as P

BF = jnp.bfloat16
F32 = jnp.float32
MEMBERS = 8
CHAIN = 3 * 10**10


def mm(a, b):
    return jnp.dot(a, b, preferred_element_type=F32)


def mm_t(a, b):
    return lax.dot_general(a, b, (((1,), (1,)), ((), ())), preferred_element_type=F32)


def channel_matrix(depth, groups):
    grain = depth // (groups * MEMBERS)
    table = np.zeros((MEMBERS, groups, grain, depth), np.float32)
    for c in range(depth):
        table[c // grain % MEMBERS, c // (MEMBERS * grain), c % grain, c] = 1.0
    return table.reshape(depth, depth)


def owner_matrix(groups, grain, block):
    table = np.zeros((groups * block, 9 * groups * grain), np.float32)
    for t in range(9):
        for g in range(groups):
            for k in range(grain):
                table[g * block + t * grain + k, (t * groups + g) * grain + k] = 1.0
    return table


def moved(y, step, axis):
    size = y.shape[axis]
    place = lax.broadcasted_iota(jnp.int32, y.shape, axis)
    edge = 0 if step == 1 else size - 1
    return jnp.where(place == edge, 0.0, pltpu.roll(y, step % size, axis))


def shape(dims, dtype=BF):
    return jax.ShapeDtypeStruct(dims, dtype)


def call(body, outs, args, scratch=(), behind=()):
    size = sum(a.size * a.dtype.itemsize for a in args)
    smem = pl.BlockSpec(memory_space=pltpu.SMEM)
    vmem = pl.BlockSpec(memory_space=pltpu.VMEM)
    aside = pl.BlockSpec(memory_space=pl.ANY)
    count = len(args)
    flops = CHAIN if body in (fine_forward, pool_add, deep_forward, deep_backward, pool_sum, fine_backward) else CHAIN // 3 if body is tables else 0

    def kernel(*refs):
        body(*refs[:count], *refs[count + len(behind) :])

    return pl.pallas_call(
        kernel,
        out_shape=outs,
        in_specs=[smem if a.dtype == jnp.int32 else vmem for a in args] + [aside] * len(behind),
        out_specs=jax.tree.map(lambda _: vmem, outs),
        scratch_shapes=list(scratch),
        compiler_params=pltpu.CompilerParams(vmem_limit_bytes=16 * 2**20),
        cost_estimate=pl.CostEstimate(flops=flops, bytes_accessed=size, transcendentals=0),
    )(*args, *behind)


def column_box(cols, b):
    low = 2 * lax.broadcasted_iota(jnp.int32, (cols // 2, cols), 0) + (b - 1)
    gap = lax.broadcasted_iota(jnp.int32, (cols // 2, cols), 1) - low
    return jnp.where((gap == 0) | (gap == 1), 0.25, 0.0).astype(BF)


def unit(size):
    row = lax.broadcasted_iota(jnp.int32, (size, size), 0)
    return jnp.where(row == lax.broadcasted_iota(jnp.int32, (size, size), 1), 1.0, 0.0).astype(BF)


def interleave(cols):
    place = lax.broadcasted_iota(jnp.int32, (cols, cols), 0)
    source = place // 2 + (place % 2) * (cols // 2)
    return jnp.where(source == lax.broadcasted_iota(jnp.int32, (cols, cols), 1), 1.0, 0.0).astype(BF)


def fine_rows(x):
    pieces = x.shape[0]
    return [jnp.concatenate([x[k, r] for k in range(pieces)]) for r in range(2)]


def to_sides(at, up, down, partner, other):
    up = up.astype(BF)
    down = down.astype(BF)

    @pl.when(at[0] == 0)
    def _():
        partner[...] = down
        other[...] = up

    @pl.when(at[0] == 1)
    def _():
        partner[...] = up
        other[...] = down


def fine_forward(at, mine, got1, got2, got3, w, x, own, partner, other):
    for s, piece in enumerate((mine, got1, got2, got3)):
        x[jnp.bitwise_and(at[4] - s, 3)] = piece[...]
    deep = own.shape[1]
    rows = fine_rows(x)
    u0, us, u1 = [], [], []
    for b in range(3):
        box = column_box(2 * deep, b)
        u = [mm(box, row) for row in rows]
        u0.append(u[0].astype(BF))
        u1.append(u[1].astype(BF))
        us.append((u[0] + u[1]).astype(BF))
    pair = [jnp.concatenate([u0[b], u1[b]]) for b in range(3)]
    mine = sum(mm_t(w[3 + b], us[b]) for b in range(3))
    first = sum(mm_t(w[b], pair[b]) for b in range(3))
    last = sum(mm_t(w[6 + b], pair[b]) for b in range(3))
    own[...] = mine + first[:, :deep] + last[:, deep:]
    to_sides(at, last[:, :deep], first[:, deep:], partner, other)


def side_rows(at, partner, other, rows):
    rows[at[0]] = other[...]
    rows[1 - at[0]] = partner[...]
    return rows[0], rows[1]


def deep_taps(w, a, row):
    y = [mm(w[3 * a + b], row) for b in range(3)]
    return y[1] + moved(y[0], 1, 1) + moved(y[2], -1, 1)


def deep_sides(at, own, got1, got2, got3, w, pooled, partner, other):
    size = own.shape[0]
    for s, piece in enumerate((own, got1, got2, got3)):
        place = jnp.bitwise_and(at[4] - s, 3) * size
        pooled[pl.ds(pl.multiple_of(place, 32), size)] = piece[...]
    row = pooled[...]
    to_sides(at, deep_taps(w, 2, row), deep_taps(w, 0, row), partner, other)


def deep_own(pooled, w, preact):
    preact[...] = deep_taps(w, 1, pooled[...])


def deep_forward(own, partner, other, upstream, output, grad):
    preact = own[...] + partner[...].astype(F32) + other[...].astype(F32)
    sigma = jax.nn.sigmoid(preact)
    output[...] = (preact * sigma).astype(BF)
    grad[...] = (upstream[...].astype(F32) * (sigma * (1.0 + preact * (1.0 - sigma)))).astype(BF)


def deep_backward(at, partner, mine, other, w, out0, out1, out2, out3, rows, whole):
    before, after = side_rows(at, partner, other, rows)
    turn = unit(mine.shape[1])
    turned = [mm_t(turn, row).astype(BF) for row in (after, mine[...], before)]
    z = [sum(mm(row, w[3 * a + b]) for a, row in enumerate(turned)) for b in range(3)]
    z = z[1] + moved(z[0], -1, 0) + moved(z[2], 1, 0)
    whole[...] = z.T.astype(BF)
    size = out0.shape[0]
    for s, out in enumerate((out0, out1, out2, out3)):
        place = jnp.bitwise_and(at[4] + s, 3) * size
        out[...] = whole[pl.ds(pl.multiple_of(place, 32), size)]


def pool_add(own, partner, other, out):
    out[...] = (own[...] + partner[...].astype(F32) + other[...].astype(F32)).astype(BF)


def pool_sum(own, got1, got2, got3, out):
    out[...] = sum(v[...].astype(F32) for v in (own, got1, got2, got3)).astype(BF)


def fine_backward(at, partner, mine, other, w, out, rows):
    before, after = side_rows(at, partner, other, rows)
    deep = mine.shape[1]
    turn = unit(deep)
    before, here, after = [mm_t(turn, row).astype(BF) for row in (before, mine[...], after)]
    top = jnp.concatenate([here, after])
    low = jnp.concatenate([before, here])
    z = []
    for b in range(3):
        both = mm(top, w[b]) + mm(low, w[6 + b])
        mid = mm(here, w[3 + b])
        z.append((both[:deep] + mid, both[deep:] + mid))
    for r in range(2):
        even = z[1][r] + z[0][r] + moved(z[2][r], 1, 0)
        late = z[1][r] + moved(z[0][r], -1, 0) + z[2][r]
        out[r, :deep] = (0.25 * even).astype(BF)
        out[r, deep:] = (0.25 * late).astype(BF)


def weave(sides, out):
    pieces, rows, part, _ = out.shape
    order = interleave(sides.shape[1])
    for r in range(rows):
        y = mm(order, sides[r]).astype(BF)
        for k in range(pieces):
            out[k, r] = y[k * part : (k + 1) * part]


def fine_slices(x, pick, out):
    size = out.shape[1]
    for r, row in enumerate(fine_rows(x)):
        cols = row.shape[0]
        for j in range(MEMBERS):
            out[j, :, r * cols : (r + 1) * cols] = mm_t(pick[j * size : (j + 1) * size], row).astype(BF)


def deep_slices(pooled, pick, out):
    size = out.shape[1]
    for j in range(MEMBERS):
        out[j] = mm(pick[j * size : (j + 1) * size], pooled[...]).astype(BF)


def tables(fine_slab, deep_slab, even, late, deep):
    size = fine_slab.shape[1]
    cols = deep_slab.shape[2]
    wide = 2 * cols
    for i in range(MEMBERS):
        block = deep_slab[i]
        row = block.astype(F32)
        turned = (moved(row, 1, 1).astype(BF), block, moved(row, -1, 1).astype(BF))
        for b in range(3):
            deep[b * size : (b + 1) * size, i * cols : (i + 1) * cols] = turned[b]
    slab = [fine_slab[i] for i in range(MEMBERS)]
    for r, out in enumerate((even, late)):
        stack = jnp.concatenate([row[:, r * wide : (r + 1) * wide] for row in slab])
        for b in range(3):
            u = mm_t(stack, column_box(wide, b)).astype(BF)
            for i in range(MEMBERS):
                out[b * size : (b + 1) * size, i * cols : (i + 1) * cols] = u[i * size : (i + 1) * size]


def pack(own, partner, other, out):
    for i, v in enumerate((own, partner, other)):
        out[i] = v[...]


def pack_more(at, first, near, out, edge):
    for i in range(2):
        out[i] = first[i]
        out[2 + i] = near[i]
    place = jnp.bitwise_and(at[1] // 2, 1)
    kept = place == at[0]

    @pl.when(kept)
    def _():
        out[4] = first[2]
        edge[...] = first[2]

    @pl.when(jnp.logical_not(kept))
    def _():
        out[4] = near[2]
        edge[...] = near[2]


def outer(at, edge, far, out):
    kept = jnp.bitwise_and(at[1] // 4, 1) == at[0]

    @pl.when(kept)
    def _():
        out[...] = edge[...]

    @pl.when(jnp.logical_not(kept))
    def _():
        out[...] = far[4]


def outer_direct(at, own, near, far, both, out):
    source = jnp.bitwise_xor(at[1] // 2, 3 * at[0])
    for i, rows in enumerate((own, near, far, both)):

        @pl.when(source == i)
        def _(rows=rows):
            out[...] = rows[2]


def group_rows(at, rows, edge, swapped, grads):
    for r, row in enumerate(rows):
        grads[jnp.bitwise_xor(at[1], r) + 1] = row[...]
    ends = (MEMBERS + 1) * at[0]
    grads[ends] = edge[...]
    grads[MEMBERS + 1 - ends] = swapped[...]


def against(table, grads, step):
    cols = grads.shape[2]
    return sum(mm_t(table[:, i * cols : (i + 1) * cols], grads[i + 1 + step]) for i in range(MEMBERS))


def to_owners(at, taps, order, outs, parts):
    total = jnp.concatenate([tap.astype(BF) for tap in taps])
    parts[...] = mm(order[...], total).astype(BF)
    size = outs[0].shape[1]
    for step, out in enumerate(outs):
        for half in range(2):
            place = (half * 4 + jnp.bitwise_and(at[2] + step, 3)) * size
            out[half] = parts[pl.ds(pl.multiple_of(place, 32), size)]


def deep_part(at, four, far, edge, swapped, table, order, out0, out1, out2, out3, grads, parts):
    rows = [four.at[r] for r in range(4)] + [far.at[r] for r in range(4)]
    group_rows(at, rows, edge, swapped, grads)
    taps = [against(table, grads, 1 - a) for a in range(3)]
    to_owners(at, taps, order, (out0, out1, out2, out3), parts)


def fine_part(at, own, near, far, both, edge, swapped, even, late, order, out0, out1, out2, out3, grads, parts):
    rows = [rows.at[r] for rows in (own, near, far, both) for r in range(2)]
    group_rows(at, rows, edge, swapped, grads)
    even_here = against(even, grads, 0)
    late_here = against(late, grads, 0)
    taps = (even_here + against(late, grads, 1), even_here + late_here, late_here + against(even, grads, -1))
    to_owners(at, taps, order, (out0, out1, out2, out3), parts)


def weight_half(at, own, got1, got2, got3, keep, send):
    def total(half):
        return sum(v[half].astype(F32) for v in (own, got1, got2, got3))

    keep[...] = total(at[3])
    send[...] = total(1 - at[3]).astype(BF)


def weight_sum(keep, got, out):
    total = keep[...] + got[...].astype(F32)
    grain = out.shape[1]
    for t in range(9):
        out[t] = total[t * grain : (t + 1) * grain]


def on_device(latent, conv_fine, conv_deep, upstream):
    wide = lax.axis_size("wide")
    pieces = lax.axis_size("narrow")
    groups = wide // MEMBERS
    near = [[MEMBERS * g + j for j in range(MEMBERS)] for g in range(groups)]
    me = lax.axis_index("wide").astype(jnp.int32)
    at = jnp.stack([me % 2, me % 8, me // 8 % 4, me // 32, lax.axis_index("narrow").astype(jnp.int32)])
    rows, part, depth = latent.shape
    cols = part * pieces
    deep = cols // 2
    grain = depth // wide
    size = groups * grain
    block = -(-9 * grain // 32) * 32
    w_fine = conv_fine.transpose(0, 1, 3, 2).reshape(9, -1, depth)
    w_deep = conv_deep.transpose(0, 1, 3, 2).reshape(9, -1, depth)
    fine = w_fine.shape[1]
    full = w_deep.shape[1]
    pick = jnp.asarray(channel_matrix(depth, groups), BF)
    order = jnp.asarray(owner_matrix(groups, grain, block), BF)

    def group_gather(first, behind, later=()):
        own = first[0]
        near = swap(first, 2)
        more, edge = call(
            pack_more, [shape((5,) + own.shape), shape(own.shape)], (at, first, near), behind=behind
        )
        far = swap(more, 4)
        edge = call(outer, shape(own.shape), (at, edge, far), behind=later)
        return more, far, edge, swap(edge, 1)

    def across(v, step):
        return lax.ppermute(v, "narrow", [(i, (i + step) % pieces) for i in range(pieces)])

    def swap(v, bit):
        return lax.ppermute(v, "wide", [(i, i ^ bit) for i in range(wide)])

    def pairs(to_partner, to_other):
        other = lax.ppermute(to_other, "wide", [(i, i - 1 + 2 * (i % 2)) for i in range(1, wide - 1)])
        return swap(to_partner, 1), other

    got = [across(latent, s) for s in (1, 2, 3)]
    x, own, partner, other = call(
        fine_forward,
        [shape((pieces,) + latent.shape), shape((fine, deep), F32), shape((fine, deep)), shape((fine, deep))],
        (at, latent, *got, w_fine),
    )
    partner, other = pairs(partner, other)
    fine_slab = call(
        fine_slices,
        shape((MEMBERS, size, rows * cols)),
        (x, pick),
        behind=(partner,),
    )
    mine = call(pool_add, shape((fine, deep)), (own, partner, other), behind=(fine_slab,))
    fine_slab = lax.all_to_all(fine_slab, "wide", 0, 0, axis_index_groups=near)
    got = [across(mine, s) for s in (1, 2, 3)]
    pooled, partner, other = call(
        deep_sides,
        [shape((depth, deep)), shape((full, deep)), shape((full, deep))],
        (at, mine, *got, w_deep),
    )
    partner, other = pairs(partner, other)
    preact = call(
        deep_own, shape((full, deep), F32), (pooled, w_deep), behind=(fine_slab,)
    )
    output, grad_pre = call(
        deep_forward,
        [shape((full, deep))] * 2,
        (preact, partner, other, upstream[0].T),
    )
    pre_partner, other = pairs(grad_pre, grad_pre)
    deep_pre = call(deep_slices, shape((MEMBERS, size, deep)), (pooled, pick), behind=(pre_partner,))
    deep_slab = lax.all_to_all(deep_pre, "wide", 0, 0, axis_index_groups=near)
    pre_first = call(pack, shape((3, full, deep)), (grad_pre, pre_partner, other), behind=(deep_pre,))
    parts = call(
        deep_backward,
        [shape((fine, deep))] * 4,
        (at, pre_partner, grad_pre, other, w_deep),
        [pltpu.VMEM((2, full, deep), BF), pltpu.VMEM((depth, deep), BF)],
    )
    got = [across(parts[s], s) for s in (1, 2, 3)]
    even_table, late_table, deep_table = call(
        tables, [shape((3 * size, MEMBERS * deep))] * 3, (fine_slab, deep_slab)
    )
    grad_pool = call(pool_sum, shape((fine, deep)), (parts[0], *got), behind=(deep_slab,))
    pool_partner, other = pairs(grad_pool, grad_pool)
    pre_rows = group_gather(pre_first, (got[0],))

    def halves(parts):
        width = parts[0].shape[2]
        got = [
            lax.ppermute(
                parts[s], "wide", [(i, i // 32 * 32 + (i // 8 + s) % 4 * 8 + i % 8) for i in range(wide)]
            )
            for s in (1, 2, 3)
        ]
        return call(weight_half, [shape((block, width), F32), shape((block, width))], (at, parts[0], *got))

    def owners(half, behind=()):
        keep, send = half
        width = keep.shape[1]
        total = call(weight_sum, shape((9, grain, width), F32), (keep, swap(send, 32)), behind=behind)
        return total.reshape(3, 3, grain, width)

    def products(body, tables, rows, behind=()):
        width = rows[-1].shape[0]
        return call(
            body,
            [shape((2, block, width))] * 4,
            (at, *rows, *tables, order),
            [pltpu.VMEM((MEMBERS + 2, width, deep), BF), pltpu.VMEM((groups * block, width), BF)],
            behind=behind,
        )

    deep_parts = products(deep_part, (deep_table,), pre_rows)
    pool_first = call(pack, shape((3, fine, deep)), (grad_pool, pool_partner, other), behind=(deep_parts[0],))
    sides = call(
        fine_backward,
        shape((rows, cols, depth)),
        (at, pool_partner, grad_pool, other, w_fine),
        [pltpu.VMEM((2, fine, deep), BF)],
        behind=(pool_first,),
    )
    pool_rows = [pool_first] + [swap(pool_first, bit) for bit in (2, 4, 6)]
    pool_edge = call(outer_direct, shape((fine, deep)), (at, *pool_rows), behind=(sides, deep_parts[0]))
    pool_rows += [pool_edge, swap(pool_edge, 1)]
    fine_parts = products(fine_part, (even_table, late_table), pool_rows)
    deep_half = halves(deep_parts)
    back = call(weave, shape((pieces, rows, part, depth)), (sides,), behind=(pool_edge,))
    partial = lax.all_to_all(back, "narrow", 0, 0)
    grad_latent = jnp.sum(partial.astype(F32), axis=0).astype(BF)

    grad_deep = owners(deep_half)
    grad_fine = owners(halves(fine_parts), (grad_latent, grad_deep))
    return output.T[None], grad_latent, grad_fine, grad_deep


def solution(mesh):
    return jax.shard_map(
        on_device,
        mesh=mesh,
        in_specs=(
            P("wide", "narrow", None),
            P(None, None, None, "narrow"),
            P(None, None, None, "narrow"),
            P("wide", None, "narrow"),
        ),
        out_specs=(
            P("wide", None, "narrow"),
            P("wide", "narrow", None),
            P(None, None, "wide", "narrow"),
            P(None, None, "wide", "narrow"),
        ),
        check_vma=False,
    )
```

```python
import functools

import jax
import jax.numpy as jnp
import numpy as np
from jax import lax
from jax.experimental import pallas as pl
from jax.experimental.pallas import tpu as pltpu
from jax.sharding import PartitionSpec as P

BF = jnp.bfloat16
F32 = jnp.float32
MEMBERS = 8
CHAIN = 3 * 10**10


def mm(a, b):
    return jnp.dot(a, b, preferred_element_type=F32)


def mm_t(a, b):
    return lax.dot_general(a, b, (((1,), (1,)), ((), ())), preferred_element_type=F32)


def channel_matrix(depth, groups):
    grain = depth // (groups * MEMBERS)
    table = np.zeros((MEMBERS, groups, grain, depth), np.float32)
    for c in range(depth):
        table[c // grain % MEMBERS, c // (MEMBERS * grain), c % grain, c] = 1.0
    return table.reshape(depth, depth)


def owner_matrix(groups, grain, block):
    table = np.zeros((groups * block, 9 * groups * grain), np.float32)
    for t in range(9):
        for g in range(groups):
            for k in range(grain):
                table[g * block + t * grain + k, (t * groups + g) * grain + k] = 1.0
    return table


def moved(y, step, axis):
    size = y.shape[axis]
    place = lax.broadcasted_iota(jnp.int32, y.shape, axis)
    edge = 0 if step == 1 else size - 1
    return jnp.where(place == edge, 0.0, pltpu.roll(y, step % size, axis))


def shape(dims, dtype=BF):
    return jax.ShapeDtypeStruct(dims, dtype)


def call(body, outs, args, scratch=(), behind=()):
    size = sum(a.size * a.dtype.itemsize for a in args)
    smem = pl.BlockSpec(memory_space=pltpu.SMEM)
    vmem = pl.BlockSpec(memory_space=pltpu.VMEM)
    aside = pl.BlockSpec(memory_space=pl.ANY)
    count = len(args)
    flops = CHAIN if body in (fine_forward, pool_add, deep_forward, deep_backward, pool_sum, fine_backward) else 0

    def kernel(*refs):
        body(*refs[:count], *refs[count + len(behind) :])

    return pl.pallas_call(
        kernel,
        out_shape=outs,
        in_specs=[smem if a.dtype == jnp.int32 else vmem for a in args] + [aside] * len(behind),
        out_specs=jax.tree.map(lambda _: vmem, outs),
        scratch_shapes=list(scratch),
        compiler_params=pltpu.CompilerParams(vmem_limit_bytes=16 * 2**20),
        cost_estimate=pl.CostEstimate(flops=flops, bytes_accessed=size, transcendentals=0),
    )(*args, *behind)


def column_box(cols, b):
    low = 2 * lax.broadcasted_iota(jnp.int32, (cols // 2, cols), 0) + (b - 1)
    gap = lax.broadcasted_iota(jnp.int32, (cols // 2, cols), 1) - low
    return jnp.where((gap == 0) | (gap == 1), 0.25, 0.0).astype(BF)


def unit(size):
    row = lax.broadcasted_iota(jnp.int32, (size, size), 0)
    return jnp.where(row == lax.broadcasted_iota(jnp.int32, (size, size), 1), 1.0, 0.0).astype(BF)


def interleave(cols):
    place = lax.broadcasted_iota(jnp.int32, (cols, cols), 0)
    source = place // 2 + (place % 2) * (cols // 2)
    return jnp.where(source == lax.broadcasted_iota(jnp.int32, (cols, cols), 1), 1.0, 0.0).astype(BF)


def fine_rows(x):
    pieces = x.shape[0]
    return [jnp.concatenate([x[k, r] for k in range(pieces)]) for r in range(2)]


def to_sides(at, up, down, partner, other):
    up = up.astype(BF)
    down = down.astype(BF)

    @pl.when(at[0] == 0)
    def _():
        partner[...] = down
        other[...] = up

    @pl.when(at[0] == 1)
    def _():
        partner[...] = up
        other[...] = down


def fine_forward(at, mine, got2, got1, got3, w, x, own, partner, other):
    for s, piece in ((0, mine), (2, got2), (1, got1), (3, got3)):
        x[jnp.bitwise_and(at[4] - s, 3)] = piece[...]
    deep = own.shape[1]
    rows = fine_rows(x)
    u0, us, u1 = [], [], []
    for b in range(3):
        box = column_box(2 * deep, b)
        u = [mm(box, row) for row in rows]
        u0.append(u[0].astype(BF))
        u1.append(u[1].astype(BF))
        us.append((u[0] + u[1]).astype(BF))
    pair = [jnp.concatenate([u0[b], u1[b]]) for b in range(3)]
    mine = sum(mm_t(w[3 + b], us[b]) for b in range(3))
    first = sum(mm_t(w[b], pair[b]) for b in range(3))
    last = sum(mm_t(w[6 + b], pair[b]) for b in range(3))
    own[...] = mine + first[:, :deep] + last[:, deep:]
    to_sides(at, last[:, :deep], first[:, deep:], partner, other)


def side_rows(at, partner, other, rows):
    rows[at[0]] = other[...]
    rows[1 - at[0]] = partner[...]
    return rows[0], rows[1]


def deep_taps(w, a, row):
    y = [mm(w[3 * a + b], row) for b in range(3)]
    return y[1] + moved(y[0], 1, 1) + moved(y[2], -1, 1)


def deep_sides(at, own, got1, got2, got3, w, pooled, partner, other):
    size = own.shape[0]
    for s, piece in enumerate((own, got1, got2, got3)):
        place = jnp.bitwise_and(at[4] - s, 3) * size
        pooled[pl.ds(pl.multiple_of(place, 32), size)] = piece[...]
    row = pooled[...]
    to_sides(at, deep_taps(w, 2, row), deep_taps(w, 0, row), partner, other)


def deep_own(pooled, w, preact):
    preact[...] = deep_taps(w, 1, pooled[...])


def deep_forward(own, partner, other, upstream, output, grad):
    preact = own[...] + partner[...].astype(F32) + other[...].astype(F32)
    sigma = jax.nn.sigmoid(preact)
    output[...] = (preact * sigma).astype(BF)
    grad[...] = (upstream[...].astype(F32) * (sigma * (1.0 + preact * (1.0 - sigma)))).astype(BF)


def deep_backward(at, partner, mine, other, w, out0, out1, out2, out3, rows, whole):
    before, after = side_rows(at, partner, other, rows)
    turn = unit(mine.shape[1])
    turned = [mm_t(turn, row).astype(BF) for row in (after, mine[...], before)]
    z = [sum(mm(row, w[3 * a + b]) for a, row in enumerate(turned)) for b in range(3)]
    z = z[1] + moved(z[0], -1, 0) + moved(z[2], 1, 0)
    whole[...] = z.T.astype(BF)
    size = out0.shape[0]
    for s, out in enumerate((out0, out1, out2, out3)):
        place = jnp.bitwise_and(at[4] + s, 3) * size
        out[...] = whole[pl.ds(pl.multiple_of(place, 32), size)]


def pool_add(own, partner, other, out):
    out[...] = (own[...] + partner[...].astype(F32) + other[...].astype(F32)).astype(BF)


def pool_sum(own, got1, got2, got3, out):
    out[...] = sum(v[...].astype(F32) for v in (own, got1, got2, got3)).astype(BF)


def fine_backward(at, partner, mine, other, w, out, rows):
    before, after = side_rows(at, partner, other, rows)
    deep = mine.shape[1]
    turn = unit(deep)
    before, here, after = [mm_t(turn, row).astype(BF) for row in (before, mine[...], after)]
    top = jnp.concatenate([here, after])
    low = jnp.concatenate([before, here])
    z = []
    for b in range(3):
        both = mm(top, w[b]) + mm(low, w[6 + b])
        mid = mm(here, w[3 + b])
        z.append((both[:deep] + mid, both[deep:] + mid))
    for r in range(2):
        even = z[1][r] + z[0][r] + moved(z[2][r], 1, 0)
        late = z[1][r] + moved(z[0][r], -1, 0) + z[2][r]
        out[r, :deep] = (0.25 * even).astype(BF)
        out[r, deep:] = (0.25 * late).astype(BF)


def weave(sides, out):
    pieces, rows, part, _ = out.shape
    order = interleave(sides.shape[1])
    for r in range(rows):
        y = mm(order, sides[r]).astype(BF)
        for k in range(pieces):
            out[k, r] = y[k * part : (k + 1) * part]


def fine_slices(x, pick, out):
    size = out.shape[1]
    for r, row in enumerate(fine_rows(x)):
        cols = row.shape[0]
        for j in range(MEMBERS):
            out[j, :, r * cols : (r + 1) * cols] = mm_t(pick[j * size : (j + 1) * size], row).astype(BF)


def deep_slices(pooled, pick, out):
    size = out.shape[1]
    for j in range(MEMBERS):
        out[j] = mm(pick[j * size : (j + 1) * size], pooled[...]).astype(BF)


def tables(fine_slab, deep_slab, even, late, deep):
    size = fine_slab.shape[1]
    cols = deep_slab.shape[2]
    wide = 2 * cols
    for i in range(MEMBERS):
        block = deep_slab[i]
        row = block.astype(F32)
        turned = (moved(row, 1, 1).astype(BF), block, moved(row, -1, 1).astype(BF))
        for b in range(3):
            deep[b * size : (b + 1) * size, i * cols : (i + 1) * cols] = turned[b]
    slab = [fine_slab[i] for i in range(MEMBERS)]
    for r, out in enumerate((even, late)):
        stack = jnp.concatenate([row[:, r * wide : (r + 1) * wide] for row in slab])
        for b in range(3):
            u = mm_t(stack, column_box(wide, b)).astype(BF)
            for i in range(MEMBERS):
                out[b * size : (b + 1) * size, i * cols : (i + 1) * cols] = u[i * size : (i + 1) * size]


def pack(own, partner, other, out):
    for i, v in enumerate((own, partner, other)):
        out[i] = v[...]


def pack_more(at, first, near, out, edge):
    for i in range(2):
        out[i] = first[i]
        out[2 + i] = near[i]
    place = jnp.bitwise_and(at[1] // 2, 1)
    kept = place == at[0]

    @pl.when(kept)
    def _():
        out[4] = first[2]
        edge[...] = first[2]

    @pl.when(jnp.logical_not(kept))
    def _():
        out[4] = near[2]
        edge[...] = near[2]


def outer(at, edge, far, out):
    kept = jnp.bitwise_and(at[1] // 4, 1) == at[0]

    @pl.when(kept)
    def _():
        out[...] = edge[...]

    @pl.when(jnp.logical_not(kept))
    def _():
        out[...] = far[4]


def outer_direct(at, own, near, far, both, out):
    source = jnp.bitwise_xor(at[1] // 2, 3 * at[0])
    for i, rows in enumerate((own, near, far, both)):

        @pl.when(source == i)
        def _(rows=rows):
            out[...] = rows[2]


def group_rows(at, rows, edge, swapped, grads):
    for r, row in enumerate(rows):
        grads[jnp.bitwise_xor(at[1], r) + 1] = row[...]
    ends = (MEMBERS + 1) * at[0]
    grads[ends] = edge[...]
    grads[MEMBERS + 1 - ends] = swapped[...]


def against(table, grads, step):
    cols = grads.shape[2]
    return sum(mm_t(table[:, i * cols : (i + 1) * cols], grads[i + 1 + step]) for i in range(MEMBERS))


def to_owners(at, taps, order, outs, parts):
    total = jnp.concatenate([tap.astype(BF) for tap in taps])
    parts[...] = mm(order[...], total).astype(BF)
    size = outs[0].shape[1]
    for step, out in enumerate(outs):
        for half in range(2):
            place = (half * 4 + jnp.bitwise_and(at[2] + step, 3)) * size
            out[half] = parts[pl.ds(pl.multiple_of(place, 32), size)]


def deep_part(at, four, far, edge, swapped, table, order, out0, out1, out2, out3, grads, parts):
    rows = [four.at[r] for r in range(4)] + [far.at[r] for r in range(4)]
    group_rows(at, rows, edge, swapped, grads)
    taps = [against(table, grads, 1 - a) for a in range(3)]
    to_owners(at, taps, order, (out0, out1, out2, out3), parts)


def fine_part(at, own, near, far, both, edge, swapped, even, late, order, out0, out1, out2, out3, grads, parts):
    rows = [rows.at[r] for rows in (own, near, far, both) for r in range(2)]
    group_rows(at, rows, edge, swapped, grads)
    even_here = against(even, grads, 0)
    late_here = against(late, grads, 0)
    taps = (even_here + against(late, grads, 1), even_here + late_here, late_here + against(even, grads, -1))
    to_owners(at, taps, order, (out0, out1, out2, out3), parts)


def weight_half(at, own, got1, got2, got3, keep, send):
    def total(half):
        return sum(v[half].astype(F32) for v in (own, got1, got2, got3))

    keep[...] = total(at[3])
    send[...] = total(1 - at[3]).astype(BF)


def weight_sum(keep, got, out):
    total = keep[...] + got[...].astype(F32)
    grain = out.shape[1]
    for t in range(9):
        out[t] = total[t * grain : (t + 1) * grain]


def on_device(latent, conv_fine, conv_deep, upstream):
    wide = lax.axis_size("wide")
    pieces = lax.axis_size("narrow")
    groups = wide // MEMBERS
    near = [[MEMBERS * g + j for j in range(MEMBERS)] for g in range(groups)]
    me = lax.axis_index("wide").astype(jnp.int32)
    at = jnp.stack([me % 2, me % 8, me // 8 % 4, me // 32, lax.axis_index("narrow").astype(jnp.int32)])
    rows, part, depth = latent.shape
    cols = part * pieces
    deep = cols // 2
    grain = depth // wide
    size = groups * grain
    block = -(-9 * grain // 32) * 32
    w_fine = conv_fine.transpose(0, 1, 3, 2).reshape(9, -1, depth)
    w_deep = conv_deep.transpose(0, 1, 3, 2).reshape(9, -1, depth)
    fine = w_fine.shape[1]
    full = w_deep.shape[1]
    pick = jnp.asarray(channel_matrix(depth, groups), BF)
    order = jnp.asarray(owner_matrix(groups, grain, block), BF)

    def group_gather(first, behind, later=()):
        own = first[0]
        near = swap(first, 2)
        more, edge = call(
            pack_more, [shape((5,) + own.shape), shape(own.shape)], (at, first, near), behind=behind
        )
        far = swap(more, 4)
        edge = call(outer, shape(own.shape), (at, edge, far), behind=later)
        return more, far, edge, swap(edge, 1)

    def across(v, step):
        return lax.ppermute(v, "narrow", [(i, (i + step) % pieces) for i in range(pieces)])

    def swap(v, bit):
        return lax.ppermute(v, "wide", [(i, i ^ bit) for i in range(wide)])

    def pairs(to_partner, to_other):
        other = lax.ppermute(to_other, "wide", [(i, i - 1 + 2 * (i % 2)) for i in range(1, wide - 1)])
        return swap(to_partner, 1), other

    two = across(latent, 2)
    got = [two, across(latent, 1), across(latent, 3)]
    x, own, partner, other = call(
        fine_forward,
        [shape((pieces,) + latent.shape), shape((fine, deep), F32), shape((fine, deep)), shape((fine, deep))],
        (at, latent, *got, w_fine),
    )
    partner, other = pairs(partner, other)
    fine_slab = call(
        fine_slices,
        shape((MEMBERS, size, rows * cols)),
        (x, pick),
        behind=(partner,),
    )
    mine = call(pool_add, shape((fine, deep)), (own, partner, other), behind=(fine_slab,))
    fine_slab = lax.all_to_all(fine_slab, "wide", 0, 0, axis_index_groups=near)
    got = [across(mine, s) for s in (1, 2, 3)]
    pooled, partner, other = call(
        deep_sides,
        [shape((depth, deep)), shape((full, deep)), shape((full, deep))],
        (at, mine, *got, w_deep),
    )
    partner, other = pairs(partner, other)
    preact = call(
        deep_own, shape((full, deep), F32), (pooled, w_deep), behind=(fine_slab,)
    )
    output, grad_pre = call(
        deep_forward,
        [shape((full, deep))] * 2,
        (preact, partner, other, upstream[0].T),
    )
    pre_partner, other = pairs(grad_pre, grad_pre)
    deep_pre = call(deep_slices, shape((MEMBERS, size, deep)), (pooled, pick), behind=(pre_partner,))
    deep_slab = lax.all_to_all(deep_pre, "wide", 0, 0, axis_index_groups=near)
    pre_first = call(pack, shape((3, full, deep)), (grad_pre, pre_partner, other), behind=(deep_pre,))
    parts = call(
        deep_backward,
        [shape((fine, deep))] * 4,
        (at, pre_partner, grad_pre, other, w_deep),
        [pltpu.VMEM((2, full, deep), BF), pltpu.VMEM((depth, deep), BF)],
    )
    got = [across(parts[s], s) for s in (1, 2, 3)]
    even_table, late_table, deep_table = call(
        tables, [shape((3 * size, MEMBERS * deep))] * 3, (fine_slab, deep_slab)
    )
    grad_pool = call(pool_sum, shape((fine, deep)), (parts[0], *got), behind=(deep_slab,))
    pool_partner, other = pairs(grad_pool, grad_pool)
    pre_rows = group_gather(pre_first, (got[0],))
    pool_first = call(pack, shape((3, fine, deep)), (grad_pool, pool_partner, other), behind=(deep_table, pre_rows[2]))

    def halves(parts):
        width = parts[0].shape[2]
        got = [
            lax.ppermute(
                parts[s], "wide", [(i, i // 32 * 32 + (i // 8 + s) % 4 * 8 + i % 8) for i in range(wide)]
            )
            for s in (1, 2, 3)
        ]
        return call(weight_half, [shape((block, width), F32), shape((block, width))], (at, parts[0], *got))

    def owners(half, behind=()):
        keep, send = half
        width = keep.shape[1]
        total = call(weight_sum, shape((9, grain, width), F32), (keep, swap(send, 32)), behind=behind)
        return total.reshape(3, 3, grain, width)

    def products(body, tables, rows, behind=()):
        width = rows[-1].shape[0]
        return call(
            body,
            [shape((2, block, width))] * 4,
            (at, *rows, *tables, order),
            [pltpu.VMEM((MEMBERS + 2, width, deep), BF), pltpu.VMEM((groups * block, width), BF)],
            behind=behind,
        )

    sides = call(
        fine_backward,
        shape((rows, cols, depth)),
        (at, pool_partner, grad_pool, other, w_fine),
        [pltpu.VMEM((2, fine, deep), BF)],
        behind=(pool_first,),
    )
    deep_parts = products(deep_part, (deep_table,), pre_rows, (pool_first,))
    pool_rows = [pool_first] + [swap(pool_first, bit) for bit in (2, 4, 6)]
    pool_edge = call(outer_direct, shape((fine, deep)), (at, *pool_rows), behind=(sides, deep_parts[0]))
    pool_rows += [pool_edge, swap(pool_edge, 1)]
    fine_parts = products(fine_part, (even_table, late_table), pool_rows)
    deep_half = halves(deep_parts)
    back = call(weave, shape((pieces, rows, part, depth)), (sides,), behind=(pool_edge,))
    partial = lax.all_to_all(back, "narrow", 0, 0)
    grad_latent = jnp.sum(partial.astype(F32), axis=0).astype(BF)

    grad_deep = owners(deep_half)
    grad_fine = owners(halves(fine_parts), (grad_latent, grad_deep))
    return output.T[None], grad_latent, grad_fine, grad_deep


def solution(mesh):
    return jax.shard_map(
        on_device,
        mesh=mesh,
        in_specs=(
            P("wide", "narrow", None),
            P(None, None, None, "narrow"),
            P(None, None, None, "narrow"),
            P("wide", None, "narrow"),
        ),
        out_specs=(
            P("wide", None, "narrow"),
            P("wide", "narrow", None),
            P(None, None, "wide", "narrow"),
            P(None, None, "wide", "narrow"),
        ),
        check_vma=False,
    )
```
